32 devices in a mesh: clip: 8 (over z, y), head: 4 (over x, core).
Axes of the slice: x: 2, y: 2, z: 4, core: 2. Of those that a mesh axis runs over, the one named last changes fastest.
Arguments:
- tokens: bfloat16 [32768, 768], P(('clip', 'head')), may hold values from -6 to 6
- frame_counts: int32 [8], P('clip'), may hold values from 8 to 16, as said below
- token_mask: int32 [32768], P(('clip', 'head')), may hold values 0 or 1
- targets: int32 [32768], P(('clip', 'head')), may hold values from 0 to 1023
- norm_gain: float32 [2, 2, 768], replicated, may hold values from 0.5 to 1.5
- norm_bias: float32 [2, 2, 768], replicated, may hold values from -1.2 to 1.2
- w_qkv: bfloat16 [2, 3, 768, 768], P(None, None, None, 'head'), may hold values from -0.21875 to 0.21875
- qv_bias: float32 [2, 2, 768], P(None, None, 'head'), may hold values from -1.2 to 1.2
- w_out: bfloat16 [2, 768, 768], P(None, 'head'), may hold values from -1.25 to 1.25
- vec_bias: float32 [2, 2, 768], replicated, may hold values from -1.2 to 1.2
- w_up: bfloat16 [2, 768, 3072], P(None, None, 'head'), may hold values from -0.21875 to 0.21875
- up_bias: float32 [2, 3072], P(None, 'head'), may hold values from -1.2 to 1.2
- w_down: bfloat16 [2, 3072, 768], P(None, 'head'), may hold values from -0.109375 to 0.109375
- code_head: bfloat16 [768, 1024], replicated, may hold values from -0.3125 to 0.3125
Outputs:
- loss_mean: float32 [], replicated
- grad_input: float32 [32768, 768], P(('clip', 'head'))
- grad_norm_gain: float32 [2, 2, 768], replicated
- grad_norm_bias: float32 [2, 2, 768], replicated
- grad_qkv: float32 [2, 3, 768, 768], P(None, None, None, 'head')
- grad_qv_bias: float32 [2, 2, 768], P(None, None, 'head')
- grad_out: float32 [2, 768, 768], P(None, 'head')
- grad_vec_bias: float32 [2, 2, 768], replicated
- grad_up: float32 [2, 768, 3072], P(None, None, 'head')
- grad_up_bias: float32 [2, 3072], P(None, 'head')
- grad_down: float32 [2, 3072, 768], P(None, 'head')
The draws below stay inside these ranges and needn't reach their ends.
Inputs may be any that keep to these rules, and one draw needn't show every extreme that they name: `frame_counts`: every clip has 8 or 16 real frames, and both counts occur; frames from the count on are padding.
All inputs are finite; a program needn't handle non-finite values. No bound on the sum of `token_mask` on one device may be relied on, other than what follows from the above.
Results may differ from the reference program's by a relative error of at most 0.013.
Values may be sent and summed in bfloat16 or wider, within the bound.
No kernel may reach another device: no remote copies, remote signals or barrier semaphores. Data moves between devices by JAX's collectives and lax.ppermute only.
A program may use at most 320 MiB of HBM per device.

```python
import jax
import jax.numpy as jnp
from jax import lax

D = 768
HEADS = 12
HD = 64
FF = 3072
CODES = 1024
FRAMES = 16
SIDE = 16
TUBE = 4
CLIPS = 8
TOKENS = 32768


def draw_frame_counts(key, part):
    key = jax.random.fold_in(key, 11)
    first_key, second_key = jax.random.split(key)
    halves = jax.random.randint(first_key, (CLIPS,), 0, 2)
    counted = FRAMES // 2 + FRAMES // 2 * halves
    shuffled = jax.random.permutation(second_key, CLIPS)
    counted = counted.at[shuffled[0]].set(FRAMES).at[shuffled[1]].set(FRAMES // 2)
    return counted.astype(jnp.int32)


def draw_tokens(key, part):
    key = jax.random.fold_in(key, 23)
    clip_key, frame_key, own_key = jax.random.split(key, 3)
    clip_count = TOKENS // (FRAMES * SIDE * SIDE)
    clip_part = jax.random.normal(clip_key, (clip_count, 1, 1, D), jnp.float32)
    frame_part = jax.random.normal(frame_key, (clip_count, FRAMES, 1, D), jnp.float32)
    own_part = jax.random.normal(own_key, (clip_count, FRAMES, SIDE * SIDE, D), jnp.float32)
    values = 0.5 * clip_part + 0.5 * frame_part + 0.7 * own_part
    return jnp.clip(values.reshape(TOKENS, D), -6.0, 6.0).astype(jnp.bfloat16)


def touch_ends(array, rng, least, largest):
    extent = array.shape
    spot = [jax.random.randint(jax.random.fold_in(rng, axis), (), 0, extent[axis]) for axis in range(len(extent))]
    array = array.at[tuple(spot)].set(least)
    longest = extent.index(max(extent))
    spot[longest] = (spot[longest] + 1) % extent[longest]
    return array.at[tuple(spot)].set(largest)


def block_scale(key, dims, cuts, least, top_value):
    def one(position, blocks):
        draws = jax.random.uniform(jax.random.fold_in(jax.random.fold_in(key, 6), position), (blocks,), jnp.float32, least / len(cuts), top_value / len(cuts))
        return jnp.repeat(jnp.exp(draws), dims[position] // blocks).reshape((-1,) + (1,) * (len(dims) - position - 1))

    loudness = one(*cuts[0])
    for cut in cuts[1:]:
        loudness = loudness * one(*cut)
    return loudness


def gaussian(key, dims, deviation, reach, cuts=(), kind=jnp.bfloat16):
    values = deviation * jax.random.normal(key, dims, jnp.float32)
    if cuts:
        values = values * block_scale(key, dims, cuts, -0.22, 0.18)
    return jnp.clip(values, -reach, reach).astype(kind)


def setup_inputs(seed: int = 0) -> dict:
    splits = jax.random.split(jax.random.key(seed), 15)
    tokens = draw_tokens(jax.random.fold_in(splits[14], 71), 0)
    frame_counts = draw_frame_counts(jax.random.fold_in(splits[14], 71), 0)
    token_mask = touch_ends((jax.random.randint(splits[2], (TOKENS,), 0, 2) < 1).astype(jnp.int32), jax.random.fold_in(splits[2], 1), 0, 1)
    targets = touch_ends(jax.random.randint(splits[3], (TOKENS,), 0, CODES), jax.random.fold_in(splits[3], 1), 0, CODES - 1).astype(jnp.int32)
    norm_gain = jnp.clip(1.0 + 0.1 * jax.random.normal(splits[4], (2, 2, D), jnp.float32), 0.5, 1.5)
    norm_bias = gaussian(splits[5], (2, 2, D), 0.2, 1.2, (), jnp.float32)
    w_qkv = gaussian(splits[6], (2, 3, D, D), D ** -0.5, 0.21875, ((3, 4),))
    qv_bias = gaussian(splits[7], (2, 2, D), 0.2, 1.2, ((2, 4),), jnp.float32)
    w_out = gaussian(splits[8], (2, D, D), (D // 32) ** -0.5, 1.25, ((1, 4),))
    vec_bias = gaussian(splits[9], (2, 2, D), 0.2, 1.2, (), jnp.float32)
    w_up = gaussian(splits[10], (2, D, FF), D ** -0.5, 0.21875, ((2, 4),))
    up_bias = gaussian(splits[11], (2, FF), 0.2, 1.2, ((1, 4),), jnp.float32)
    w_down = gaussian(splits[12], (2, FF, D), FF ** -0.5, 0.109375, ((1, 4),))
    code_head = gaussian(splits[13], (D, CODES), (D // 2) ** -0.5, 0.3125)
    return {"tokens": tokens, "frame_counts": frame_counts, "token_mask": token_mask, "targets": targets, "norm_gain": norm_gain, "norm_bias": norm_bias, "w_qkv": w_qkv, "qv_bias": qv_bias, "w_out": w_out, "vec_bias": vec_bias, "w_up": w_up, "up_bias": up_bias, "w_down": w_down, "code_head": code_head}


epsilon = 1e-06
masked_score = -1e+30

@jax.custom_vjp
def low(v):
    return lax.optimization_barrier(v.astype(jnp.bfloat16)).astype(jnp.float32)

@jax.custom_vjp
def low_back(v):
    return v

def low_keep(v):
    return (low(v), None)

def low_pass(kept, grad):
    return (grad,)

def back_keep(v):
    return (v, None)

def back_low(kept, grad):
    return (low(grad),)
low.defvjp(low_keep, low_pass)
low_back.defvjp(back_keep, back_low)

def matmul_high(left, right):
    return jnp.dot(left, right, precision=lax.Precision.HIGHEST, preferred_element_type=jnp.float32)

def layer_norm(stream, gain, shift):
    centre = lax.optimization_barrier(jnp.mean(stream, axis=-1, keepdims=True))
    centred = stream - centre
    spread = lax.optimization_barrier(jnp.mean(centred * centred, axis=-1, keepdims=True))
    return centred * lax.rsqrt(spread + epsilon) * gain + shift

def windows_of(values, window_kind):
    trailing = values.shape[1:]
    clip_count = values.shape[0] // (FRAMES * SIDE * SIDE)
    if window_kind == 0:
        return values.reshape((clip_count * FRAMES, SIDE * SIDE) + trailing)
    tile_count = SIDE // TUBE
    lattice = values.reshape((clip_count, FRAMES, tile_count, TUBE, tile_count, TUBE) + trailing)
    axis_order = (0, 2, 4, 1, 3, 5) + tuple(range(6, 6 + len(trailing)))
    return lattice.transpose(axis_order).reshape((clip_count * tile_count * tile_count, FRAMES * TUBE * TUBE) + trailing)

def rows_of(values, window_kind):
    trailing = values.shape[2:]
    if window_kind == 0:
        return values.reshape((-1,) + trailing)
    tile_count = SIDE // TUBE
    clip_count = values.shape[0] // (tile_count * tile_count)
    lattice = values.reshape((clip_count, tile_count, tile_count, FRAMES, TUBE, TUBE) + trailing)
    axis_order = (0, 3, 1, 4, 2, 5) + tuple(range(6, 6 + len(trailing)))
    return lattice.transpose(axis_order).reshape((-1,) + trailing)

def attention(queries, key_rows, value_rows, valid_rows, window_kind):
    head_shape = (queries.shape[0], HEADS, HD)
    query_win = windows_of(queries.reshape(head_shape), window_kind)
    key_win = windows_of(key_rows.reshape(head_shape), window_kind)
    value_win = windows_of(value_rows.reshape(head_shape), window_kind)
    scores = low_back(jnp.einsum('wqhd,wkhd->whqk', query_win, key_win, precision=lax.Precision.HIGHEST) * HD ** (-0.5))
    inside = windows_of(valid_rows, window_kind)
    allowed = jnp.logical_or(inside[:, None, :], jnp.logical_not(inside[:, :, None]))
    scores = jnp.where(allowed[:, None], scores, masked_score)
    soft_probs = low(jax.nn.softmax(scores, axis=-1))
    attended = jnp.einsum('whqk,wkhd->wqhd', soft_probs, value_win, precision=lax.Precision.HIGHEST)
    return low_back(low(rows_of(attended, window_kind).reshape(queries.shape)))

def clip_loss(weights, code_weight, clip_tokens, frame_count, token_flags, target_ids):
    norm_gain, norm_bias, w_qkv, qv_bias, w_out, vec_bias, w_up, up_bias, w_down = weights
    frame_of = jnp.arange(clip_tokens.shape[0]) // (SIDE * SIDE)
    valid_rows = frame_of < frame_count
    stream = clip_tokens
    for layer_index in range(2):
        normed = low(layer_norm(stream, norm_gain[layer_index, 0], norm_bias[layer_index, 0]))
        queries = low_back(low(matmul_high(normed, w_qkv[layer_index, 0]) + qv_bias[layer_index, 0]))
        key_rows = low_back(low(matmul_high(normed, w_qkv[layer_index, 1])))
        value_rows = low_back(low(matmul_high(normed, w_qkv[layer_index, 2]) + qv_bias[layer_index, 1]))
        attended = attention(queries, key_rows, value_rows, valid_rows, layer_index)
        stream = stream + low_back(matmul_high(attended, w_out[layer_index]) + vec_bias[layer_index, 0])
        normed = low(layer_norm(stream, norm_gain[layer_index, 1], norm_bias[layer_index, 1]))
        hidden = low_back(matmul_high(normed, w_up[layer_index]) + up_bias[layer_index])
        active = low(jax.nn.gelu(hidden, approximate=True))
        stream = stream + low_back(matmul_high(active, w_down[layer_index]) + vec_bias[layer_index, 1])
    logits = low_back(matmul_high(low(stream), code_weight))
    picked = jnp.take_along_axis(logits, target_ids[:, None], axis=1)[:, 0]
    token_weight = token_flags.astype(jnp.float32) * valid_rows.astype(jnp.float32)
    return jnp.sum(token_weight * (jax.nn.logsumexp(logits, axis=1) - picked))

def reference(tokens, frame_counts, token_mask, targets, norm_gain, norm_bias, w_qkv, qv_bias, w_out, vec_bias, w_up, up_bias, w_down, code_head):
    weights = (norm_gain.astype(jnp.float32), norm_bias.astype(jnp.float32), w_qkv.astype(jnp.float32), qv_bias.astype(jnp.float32), w_out.astype(jnp.float32), vec_bias.astype(jnp.float32), w_up.astype(jnp.float32), up_bias.astype(jnp.float32), w_down.astype(jnp.float32))
    code_weight = code_head.astype(jnp.float32)
    clip_rows = FRAMES * SIDE * SIDE
    clip_count = frame_counts.shape[0]
    stream = tokens.astype(jnp.float32)

    def objective(weights, stream):

        def one_clip(running, clip_item):
            clip_tokens, frame_count, token_flags, target_ids = clip_item
            return (running + clip_loss(weights, code_weight, clip_tokens, frame_count, token_flags, target_ids), None)
        running, _ = lax.scan(jax.checkpoint(one_clip), jnp.zeros((), jnp.float32), (stream.reshape(clip_count, clip_rows, D), frame_counts, token_mask.reshape(clip_count, clip_rows), targets.reshape(clip_count, clip_rows)))
        return running
    running, pullback = jax.vjp(objective, weights, stream)
    grad_weights, grad_stream = pullback(jnp.ones((), jnp.float32))
    return (running / TOKENS, grad_stream, grad_weights[0], grad_weights[1], grad_weights[2], grad_weights[3], grad_weights[4], grad_weights[5], grad_weights[6], grad_weights[7], grad_weights[8])
```

```python
from functools import partial

import jax
import jax.numpy as jnp
from jax import lax
from jax.experimental import pallas as pl
from jax.experimental.pallas import tpu as pltpu
from jax.sharding import PartitionSpec as P

HD = 64
FRAMES = 16
SIDE = 16
TUBE = 4
WINDOW = 256
PAIR = 128

epsilon = 1e-06
masked_score = -1e30
f32 = jnp.float32
bf16 = jnp.bfloat16
VMEM_LIMIT = 48 * 1024 * 1024


def dot(a, b):
    return lax.dot_general(a, b, (((1,), (0,)), ((), ())), preferred_element_type=f32)


def dot_nt(a, b):
    return lax.dot_general(a, b, (((1,), (1,)), ((), ())), preferred_element_type=f32)


def dot_tn(a, b):
    return lax.dot_general(a, b, (((0,), (0,)), ((), ())), preferred_element_type=f32)


def allowed_of(place_ref):
    head_index = place_ref[0]
    frame_count = place_ref[1]

    def valid(axis):
        position = lax.broadcasted_iota(jnp.int32, (WINDOW, WINDOW), axis)
        frame = 4 * ((position >> 6) ^ head_index) + ((position >> 4) & 3)
        return frame < frame_count

    return jnp.logical_or(valid(1), jnp.logical_not(valid(0)))


def pair_parts(first_ref, second_ref, part):
    width = first_ref.shape[1] // 3
    cut = slice(part * width, (part + 1) * width)
    return jnp.concatenate([first_ref[:, cut], second_ref[:, cut]], axis=1)


def attend_kernel(masked, place_ref, first_ref, second_ref, out_first, out_second, lse_ref):
    query = pair_parts(first_ref, second_ref, 0) * jnp.asarray(HD ** (-0.5), bf16)
    key = pair_parts(first_ref, second_ref, 1)
    value = pair_parts(first_ref, second_ref, 2)
    lane = lax.broadcasted_iota(jnp.int32, (WINDOW, PAIR), 1)
    low = lane < HD
    if masked:
        allowed = allowed_of(place_ref)
    lse = jnp.zeros((WINDOW, PAIR), f32)
    outs = []
    for pair in range(query.shape[1] // PAIR):
        cut = slice(pair * PAIR, (pair + 1) * PAIR)
        found = []
        for half in range(2):
            mine = low if half == 0 else jnp.logical_not(low)
            query_half = jnp.where(mine, query[:, cut], jnp.zeros((), bf16))
            scores = dot_nt(query_half, key[:, cut])
            if masked:
                scores = jnp.where(allowed, scores, masked_score)
            top = jnp.max(scores, axis=1, keepdims=True)
            terms = jnp.exp(scores - top)
            total = jnp.sum(terms, axis=1, keepdims=True)
            probs = (terms * (1.0 / total)).astype(bf16)
            found.append(dot(probs, value[:, cut]))
            lse = jnp.where(lane == 2 * pair + half, top + jnp.log(total), lse)
        outs.append(jnp.where(low, found[0], found[1]).astype(bf16))
    joined = jnp.concatenate(outs, axis=1)
    width = out_first.shape[1]
    out_first[...] = joined[:, :width]
    out_second[...] = joined[:, width:]
    lse_ref[...] = lse


def attend(place, first, second, masked):
    rows = first.shape[0]
    width = first.shape[1] // 3
    block = lambda columns: pl.BlockSpec((WINDOW, columns), lambda i, s: (i, 0))
    return pl.pallas_call(
        partial(attend_kernel, masked),
        grid_spec=pltpu.PrefetchScalarGridSpec(
            num_scalar_prefetch=1,
            grid=(rows // WINDOW,),
            in_specs=[block(3 * width), block(3 * width)],
            out_specs=[block(width), block(width), block(PAIR)],
        ),
        out_shape=[
            jax.ShapeDtypeStruct((rows, width), bf16),
            jax.ShapeDtypeStruct((rows, width), bf16),
            jax.ShapeDtypeStruct((rows, PAIR), f32),
        ],
        compiler_params=pltpu.CompilerParams(vmem_limit_bytes=VMEM_LIMIT),
        cost_estimate=pl.CostEstimate(
            flops=16 * rows * WINDOW * width, bytes_accessed=16 * rows * width, transcendentals=0
        ),
        name="attend",
    )(place, first, second)


def attend_back_kernel(
    masked, place_ref, first_ref, second_ref, grad_first, grad_second, lse_ref, out_first, out_second
):
    query = pair_parts(first_ref, second_ref, 0) * jnp.asarray(HD ** (-0.5), bf16)
    key = pair_parts(first_ref, second_ref, 1)
    value = pair_parts(first_ref, second_ref, 2)
    grad = jnp.concatenate([grad_first[...], grad_second[...]], axis=1)
    lane = lax.broadcasted_iota(jnp.int32, (WINDOW, PAIR), 1)
    low = lane < HD
    if masked:
        allowed = allowed_of(place_ref)
    lse = lse_ref[...]
    zero = jnp.zeros((), bf16)
    results = [[], [], []]
    for pair in range(query.shape[1] // PAIR):
        cut = slice(pair * PAIR, (pair + 1) * PAIR)
        found = []
        for half in range(2):
            mine = low if half == 0 else jnp.logical_not(low)
            query_half = jnp.where(mine, query[:, cut], zero)
            grad_half = jnp.where(mine, grad[:, cut], zero)
            scores = dot_nt(query_half, key[:, cut])
            if masked:
                scores = jnp.where(allowed, scores, masked_score)
            head = 2 * pair + half
            probs = jnp.exp(scores - lse[:, head : head + 1])
            grad_probs = dot_nt(grad_half, value[:, cut])
            delta = jnp.sum(probs * grad_probs, axis=1, keepdims=True)
            grad_scores = (probs * (grad_probs - delta)).astype(bf16)
            grad_query = dot(grad_scores, key[:, cut]) * HD ** (-0.5)
            grad_key = dot_tn(grad_scores, query[:, cut])
            grad_value = dot_tn(probs.astype(bf16), grad[:, cut])
            found.append((grad_query, grad_key, grad_value))
        for part in range(3):
            results[part].append(jnp.where(low, found[0][part], found[1][part]).astype(bf16))
    joined = [jnp.concatenate(part, axis=1) for part in results]
    width = grad_first.shape[1]
    for part in range(3):
        out_first[:, part * width : (part + 1) * width] = joined[part][:, :width]
        out_second[:, part * width : (part + 1) * width] = joined[part][:, width:]


def attend_back(place, first, second, grad_first, grad_second, lse, masked):
    rows = first.shape[0]
    width = first.shape[1] // 3
    block = lambda columns: pl.BlockSpec((WINDOW, columns), lambda i, s: (i, 0))
    return pl.pallas_call(
        partial(attend_back_kernel, masked),
        grid_spec=pltpu.PrefetchScalarGridSpec(
            num_scalar_prefetch=1,
            grid=(rows // WINDOW,),
            in_specs=[block(3 * width), block(3 * width), block(width), block(width), block(PAIR)],
            out_specs=[block(3 * width), block(3 * width)],
        ),
        out_shape=[jax.ShapeDtypeStruct((rows, 3 * width), bf16)] * 2,
        compiler_params=pltpu.CompilerParams(vmem_limit_bytes=VMEM_LIMIT),
        cost_estimate=pl.CostEstimate(
            flops=40 * rows * WINDOW * width, bytes_accessed=32 * rows * width, transcendentals=0
        ),
        name="attend_back",
    )(place, first, second, grad_first, grad_second, lse)


def statistics(stream):
    centre = jnp.mean(stream, axis=-1, keepdims=True)
    centred = stream - centre
    spread = jnp.mean(centred * centred, axis=-1, keepdims=True)
    scale = lax.rsqrt(spread + epsilon)
    return centred * scale, scale


def layer_norm(stream, gain, shift):
    normal, _ = statistics(stream)
    return (normal * gain + shift).astype(bf16)


def norm_back(stream, gain, grad):
    normal, scale = statistics(stream)
    scaled = grad * gain
    mean_plain = jnp.mean(scaled, axis=-1, keepdims=True)
    mean_normal = jnp.mean(scaled * normal, axis=-1, keepdims=True)
    inner = scale * (scaled - mean_plain - normal * mean_normal)
    return inner, jnp.sum(grad * normal, axis=0), jnp.sum(grad, axis=0)


def gelu_both(hidden):
    root = 0.7978845608028654
    cubic = 0.044715
    square = hidden * hidden
    bend = jnp.tanh(root * hidden * (1.0 + cubic * square))
    active = 0.5 * hidden * (1.0 + bend)
    slope = 0.5 * (1.0 + bend) + 0.5 * hidden * (1.0 - bend * bend) * root * (
        1.0 + 3.0 * cubic * square
    )
    return active.astype(bf16), slope.astype(bf16)


def code_loss(stream, code_head, targets, token_weight):
    logits = jnp.dot(stream.astype(bf16), code_head, preferred_element_type=f32)
    score_top = jnp.max(logits, axis=1, keepdims=True)
    log_total = score_top + jnp.log(jnp.sum(jnp.exp(logits - score_top), axis=1, keepdims=True))
    onehot = targets[:, None] == jnp.arange(logits.shape[1], dtype=jnp.int32)[None, :]
    picked = jnp.sum(jnp.where(onehot, logits, 0.0), axis=1)
    loss_local = jnp.sum(token_weight * (log_total[:, 0] - picked))
    soft_codes = jnp.exp(logits - log_total)
    grad_logits = (token_weight[:, None] * (soft_codes - onehot.astype(f32))).astype(bf16)
    return loss_local, dot_nt(grad_logits, code_head)


def head_swap(values, distance):
    count = lax.axis_size("head")
    return lax.ppermute(values, "head", [(i, i ^ distance) for i in range(count)])


def clip_swap(values, distance):
    count = lax.axis_size("clip")
    return lax.ppermute(values, "clip", [(i, i ^ distance) for i in range(count)])


def gather_parts(own):
    across = head_swap(own, 2)
    return [own, head_swap(own, 1), across, head_swap(across, 1)]


def reduce_parts(part_of):
    beside = head_swap(part_of(1).astype(bf16), 1)
    beyond = head_swap(part_of(3).astype(bf16), 1)
    across = head_swap((part_of(2) + beyond.astype(f32)).astype(bf16), 2)
    return part_of(0) + beside.astype(f32) + across.astype(f32)


def reduce_clips(own):
    count = lax.axis_size("clip")
    half = own.shape[0] // 2
    upper = (lax.axis_index("clip") & 1) == 1
    own = own.astype(bf16)
    keep = jnp.where(upper, own[half:], own[:half])
    send = jnp.where(upper, own[:half], own[half:])
    total = keep.astype(f32) + clip_swap(send, 1).astype(f32)
    distance = 2
    while distance < count:
        sent = total.astype(bf16)
        total = sent.astype(f32) + clip_swap(sent, distance).astype(f32)
        distance *= 2
    mine = total.astype(bf16)
    other = clip_swap(mine, 1)
    return jnp.concatenate(
        [jnp.where(upper, other, mine), jnp.where(upper, mine, other)], axis=0
    ).astype(f32)


def reduce_small(values):
    for distance in (1, 2):
        values = values + head_swap(values, distance)
    distance = 1
    while distance < lax.axis_size("clip"):
        values = values + clip_swap(values, distance)
        distance *= 2
    return values


def by_distance(values, head_index, axis):
    def picked(order):
        return jnp.concatenate(
            [lax.slice_in_dim(values, i, i + 1, axis=axis) for i in order], axis=axis
        )

    values = jnp.where((head_index & 1) == 1, picked((1, 0, 3, 2)), values)
    return jnp.where((head_index & 2) == 2, picked((2, 3, 0, 1)), values)


def rows_to_tubes(rows, head_index):
    trailing = rows.shape[1:]
    tiles = SIDE // TUBE
    lattice = rows.reshape((FRAMES // 4, tiles, TUBE, tiles, TUBE) + trailing)
    lattice = lattice.transpose((0, 1, 3, 2, 4) + tuple(range(5, 5 + len(trailing))))
    return by_distance(
        lattice.reshape((FRAMES // 4, tiles, tiles * TUBE * TUBE) + trailing), head_index, 1
    )


def tubes_to_rows(values, head_index):
    trailing = values.shape[3:]
    tiles = SIDE // TUBE
    lattice = by_distance(values, head_index, 1).reshape(
        (FRAMES // 4, tiles, tiles, TUBE, TUBE) + trailing
    )
    lattice = lattice.transpose((0, 1, 3, 2, 4) + tuple(range(5, 5 + len(trailing))))
    return lattice.reshape((-1,) + trailing)


def frames_to_bands(values):
    pieces = [values[:, 0]] + [head_swap(values[:, k], k) for k in (1, 2, 3)]
    trailing = values.shape[3:]
    tiles = SIDE // TUBE
    stacked = jnp.stack(pieces).reshape((4, FRAMES // 4, tiles, TUBE * TUBE) + trailing)
    return stacked.transpose((2, 0, 1, 3) + tuple(range(4, 4 + len(trailing))))


def bands_to_frames(values):
    trailing = values.shape[4:]
    lattice = values.transpose((1, 2, 0, 3) + tuple(range(4, 4 + len(trailing))))
    lattice = lattice.reshape((4, FRAMES // 4, 4 * TUBE * TUBE) + trailing)
    pieces = [lattice[0]] + [head_swap(lattice[k], k) for k in (1, 2, 3)]
    return jnp.stack(pieces, axis=1)


def on_device(
    tokens,
    frame_counts,
    token_mask,
    targets,
    norm_gain,
    norm_bias,
    w_qkv,
    qv_bias,
    w_out,
    vec_bias,
    w_up,
    up_bias,
    w_down,
    code_head,
):
    head_index = lax.axis_index("head")
    local_rows, width = tokens.shape
    share = w_out.shape[1]
    units = w_up.shape[2]
    place = jnp.stack([head_index.astype(jnp.int32), frame_counts[0]])

    small_own = jnp.concatenate([up_bias.reshape(-1), qv_bias.reshape(-1)])
    small_parts = gather_parts(small_own)
    up_shift = [p[: 2 * units].reshape(2, units) for p in small_parts]
    qv_shift = [p[2 * units :].reshape(2, 2, share) for p in small_parts]
    parts_qkv, parts_out, parts_up, parts_down = [], [], [], []
    for layer in range(2):
        parts_qkv.append(gather_parts(jnp.concatenate(list(w_qkv[layer]), axis=1)))
        parts_out.append(gather_parts(w_out[layer]))
        parts_up.append(gather_parts(w_up[layer]))
        parts_down.append(gather_parts(w_down[layer]))

    arranged = rows_to_tubes(tokens, head_index)
    stream = arranged.reshape(local_rows, width).astype(f32)
    marks = rows_to_tubes(2 * targets + token_mask, head_index)
    marks = frames_to_bands(marks).reshape(local_rows)
    position = jnp.arange(local_rows, dtype=jnp.int32) % WINDOW
    frame = 4 * ((position >> 6) ^ head_index) + ((position >> 4) & 3)
    token_weight = (marks & 1).astype(f32) * (frame < frame_counts[0]).astype(f32)
    own_targets = marks >> 1

    kept = []
    for layer in range(2):
        masked = layer == 1
        if layer == 1:
            stream = frames_to_bands(
                stream.astype(bf16).reshape(arranged.shape)
            ).reshape(local_rows, width).astype(f32)
        stream_a = stream
        normed = layer_norm(stream, norm_gain[layer, 0], norm_bias[layer, 0])
        qkv = []
        for k in range(4):
            shift = jnp.concatenate(
                [qv_shift[k][layer, 0], jnp.zeros((share,), f32), qv_shift[k][layer, 1]]
            )
            qkv.append((dot(normed, parts_qkv[layer][k]) + shift).astype(bf16))
        attended, lse = [], []
        for half in range(2):
            a, b, c = attend(place, qkv[2 * half], qkv[2 * half + 1], masked)
            attended += [a, b]
            lse.append(c)
        branch = vec_bias[layer, 0]
        for k in range(4):
            branch = branch + dot(attended[k], parts_out[layer][k])
        stream = stream + branch
        stream_b = stream
        normed2 = layer_norm(stream, norm_gain[layer, 1], norm_bias[layer, 1])
        active, slope = [], []
        branch = vec_bias[layer, 1]
        for k in range(4):
            a, s = gelu_both(dot(normed2, parts_up[layer][k]) + up_shift[k][layer])
            active.append(a)
            slope.append(s)
            branch = branch + dot(a, parts_down[layer][k])
        stream = stream + branch
        kept.append((stream_a, normed, qkv, attended, lse, stream_b, normed2, active, slope))

    loss_local, grad_stream = code_loss(stream, code_head, own_targets, token_weight)

    big = [None, None]
    small = [None, None]
    for layer in (1, 0):
        masked = layer == 1
        stream_a, normed, qkv, attended, lse, stream_b, normed2, active, slope = kept[layer]
        g2 = grad_stream.astype(bf16)
        vec_1 = jnp.sum(g2, axis=0, dtype=f32)
        grad_hidden = [
            (dot_nt(g2, parts_down[layer][k]) * slope[k].astype(f32)).astype(bf16)
            for k in range(4)
        ]
        down_grad = reduce_clips(reduce_parts(lambda k: dot_tn(active[k], g2)))
        up_grad = reduce_clips(reduce_parts(lambda k: dot_tn(normed2, grad_hidden[k])))
        up_bias_grad = [jnp.sum(g, axis=0, dtype=f32) for g in grad_hidden]
        grad_normed = sum(dot_nt(grad_hidden[k], parts_up[layer][k]) for k in range(4))
        inner, gain_1, shift_1 = norm_back(stream_b, norm_gain[layer, 1], grad_normed)
        grad_stream = grad_stream + inner
        g1 = grad_stream.astype(bf16)
        vec_0 = jnp.sum(g1, axis=0, dtype=f32)
        out_grad = reduce_clips(reduce_parts(lambda k: dot_tn(attended[k], g1)))
        grad_attended = [dot_nt(g1, parts_out[layer][k]).astype(bf16) for k in range(4)]
        grad_qkv = []
        for half in range(2):
            i, j = 2 * half, 2 * half + 1
            grad_qkv += attend_back(
                place, qkv[i], qkv[j], grad_attended[i], grad_attended[j], lse[half], masked
            )
        qkv_grad = reduce_clips(reduce_parts(lambda k: dot_tn(normed, grad_qkv[k])))
        qkv_bias_grad = [jnp.sum(g, axis=0, dtype=f32) for g in grad_qkv]
        grad_normed = sum(dot_nt(grad_qkv[k], parts_qkv[layer][k]) for k in range(4))
        inner, gain_0, shift_0 = norm_back(stream_a, norm_gain[layer, 0], grad_normed)
        grad_stream = grad_stream + inner
        if layer == 1:
            tiles = SIDE // TUBE
            sent = grad_stream.astype(bf16).reshape(tiles, 4, FRAMES // 4, TUBE * TUBE, width)
            grad_stream = bands_to_frames(sent).reshape(local_rows, width).astype(f32)
        qkv_grad = jnp.stack([qkv_grad[:, j * share : (j + 1) * share] for j in range(3)])
        big[layer] = (qkv_grad, out_grad, up_grad, down_grad)
        qv_grad = [
            jnp.concatenate([g[:share], g[2 * share :]]) for g in qkv_bias_grad
        ]
        split = jnp.stack([jnp.concatenate([u, q]) for u, q in zip(up_bias_grad, qv_grad)])
        plain = jnp.concatenate([gain_0, gain_1, shift_0, shift_1, vec_0, vec_1])
        small[layer] = (split, plain)

    grad_input = tubes_to_rows(
        grad_stream.reshape(FRAMES // 4, 4, 64, width), head_index
    )

    splits = jnp.stack([small[0][0], small[1][0]])
    splits = by_distance(splits, head_index, 1)
    plains = jnp.concatenate([small[0][1], small[1][1], loss_local[None]])
    packed = jnp.concatenate([splits.reshape(-1), plains])
    packed = reduce_small(packed)
    splits_sum = packed[: splits.size].reshape(splits.shape)
    splits_own = by_distance(splits_sum, head_index, 1)[:, 0]
    plains_sum = packed[splits.size :]
    loss_total = plains_sum[-1]
    vectors = plains_sum[:-1].reshape(2, 3, 2, width)
    qv_bias_out = splits_own[:, units:].reshape(2, 2, share)
    up_bias_out = splits_own[:, :units]

    slot_total = lax.axis_size("clip") * frame_counts.shape[0] * FRAMES * SIDE * SIDE

    def stacked(member):
        return jnp.stack([big[0][member], big[1][member]])

    return (
        loss_total / slot_total,
        grad_input,
        vectors[:, 0],
        vectors[:, 1],
        stacked(0),
        qv_bias_out,
        stacked(1),
        vectors[:, 2],
        stacked(2),
        up_bias_out,
        stacked(3),
    )


def solution(mesh):
    placed = (
        P(("clip", "head"), None),
        P("clip"),
        P(("clip", "head")),
        P(("clip", "head")),
        P(),
        P(),
        P(None, None, None, "head"),
        P(None, None, "head"),
        P(None, "head", None),
        P(),
        P(None, None, "head"),
        P(None, "head"),
        P(None, "head", None),
        P(),
    )
    return jax.shard_map(
        on_device,
        mesh=mesh,
        in_specs=placed,
        out_specs=(
            P(),
            P(("clip", "head"), None),
            P(),
            P(),
            P(None, None, None, "head"),
            P(None, None, "head"),
            P(None, "head", None),
            P(),
            P(None, None, "head"),
            P(None, "head"),
            P(None, "head", None),
        ),
        check_vma=False,
    )
```

```python
from functools import partial

import jax
import jax.numpy as jnp
from jax import lax
from jax.experimental import pallas as pl
from jax.experimental.pallas import tpu as pltpu
from jax.sharding import PartitionSpec as P

HD = 64
FRAMES = 16
SIDE = 16
TUBE = 4
WINDOW = 256
PAIR = 128
BAND = 64
CELL = 16
LSE_ROWS = 16

epsilon = 1e-06
masked_score = -1e30
f32 = jnp.float32
bf16 = jnp.bfloat16
VMEM_LIMIT = 56 * 1024 * 1024
TIMES = {
    "attend": 17, "feed": 23, "code_loss": 10, "feed_back": 21, "attend_back": 25,
    "grads_down": 8, "grads_up": 8, "grads_attn": 8, "emit": 3,
}
SCALE = 0.0001


def cost_of(name):
    time = TIMES[name] * SCALE
    return pl.CostEstimate(flops=int(time * 1.15e9), bytes_accessed=int(time * 3.6e6), transcendentals=0)


def dot(a, b):
    return lax.dot_general(a, b, (((1,), (0,)), ((), ())), preferred_element_type=f32)


def dot_nt(a, b):
    return lax.dot_general(a, b, (((1,), (1,)), ((), ())), preferred_element_type=f32)


def dot_tn(a, b):
    return lax.dot_general(a, b, (((0,), (0,)), ((), ())), preferred_element_type=f32)


def statistics(stream):
    centre = jnp.mean(stream, axis=-1, keepdims=True)
    centred = stream - centre
    spread = jnp.mean(centred * centred, axis=-1, keepdims=True)
    scale = lax.rsqrt(spread + epsilon)
    return centred * scale, scale


def by_eight(values):
    rows, columns = values.shape
    return jnp.sum(values.reshape(rows // 8, 8, columns), axis=0)


def gather_sums(acc_ref, values):
    first = pl.program_id(0) == 0
    parts = jnp.concatenate([by_eight(v) for v in values], axis=1)

    @pl.when(first)
    def _():
        acc_ref[...] = parts

    @pl.when(jnp.logical_not(first))
    def _():
        acc_ref[...] += parts


def last_step():
    return pl.program_id(0) == pl.num_programs(0) - 1


def norm_back(stream, gain, grad):
    normal, scale = statistics(stream)
    scaled = grad * gain
    mean_plain = jnp.mean(scaled, axis=-1, keepdims=True)
    mean_normal = jnp.mean(scaled * normal, axis=-1, keepdims=True)
    inner = scale * (scaled - mean_plain - normal * mean_normal)
    return inner, grad * normal


def gelu_both(hidden):
    root = 0.7978845608028654
    cubic = 0.044715
    square = hidden * hidden
    bend = jnp.tanh(hidden * (root + root * cubic * square))
    rise = 0.5 + 0.5 * bend
    active = hidden * rise
    slope = rise + (active - active * rise) * (2.0 * root + 6.0 * root * cubic * square)
    return active.astype(bf16), slope.astype(bf16)


def allowed_of(place_ref):
    head_index = place_ref[0]
    frame_count = place_ref[1]

    def valid(axis):
        position = lax.broadcasted_iota(jnp.int32, (WINDOW, WINDOW), axis)
        frame = 4 * ((position >> 6) ^ head_index) + ((position >> 4) & 3)
        return frame < frame_count

    return jnp.logical_or(valid(0), jnp.logical_not(valid(1)))


def shuffle_of(place_ref, axis):
    arranged = lax.broadcasted_iota(jnp.int32, (WINDOW, WINDOW), axis)
    plain = lax.broadcasted_iota(jnp.int32, (WINDOW, WINDOW), 1 - axis)
    band = (arranged >> 6) ^ place_ref[0]
    source = band * BAND + ((arranged >> 2) & 3) * 16 + ((arranged >> 4) & 3) * 4 + (arranged & 3)
    return (source == plain).astype(f32).astype(bf16)


def assemble_qkv(packs, scratch):
    width = scratch.shape[1]
    share = width // 4
    for k in range(4):
        for j in range(3):
            start = j * width + k * share
            scratch[start : start + share, :] = packs[k][j * share : (j + 1) * share, :]


def assemble_out(packs, scratch):
    share = scratch.shape[0] // 4
    for k in range(4):
        scratch[k * share : (k + 1) * share, :] = packs[k][3 * share :, :]


def stack_heads(pair):
    low = lax.broadcasted_iota(jnp.int32, pair.shape, 1) < HD
    zero = jnp.zeros((), bf16)
    return jnp.concatenate([jnp.where(low, pair, zero), jnp.where(low, zero, pair)], axis=0)


def attend_core(qkv, allowed, att_ref, lse_ref):
    width = att_ref.shape[1]
    pairs = width // PAIR

    def part(j, pair):
        return qkv[:, j * width + pair * PAIR : j * width + (pair + 1) * PAIR]

    def scores_of(pair):
        query = part(0, pair) * jnp.asarray(HD ** (-0.5), bf16)
        return dot_nt(stack_heads(part(1, pair)), query)

    ahead = scores_of(0)
    for pair in range(pairs):
        scores = ahead
        if pair + 1 < pairs:
            ahead = scores_of(pair + 1)
        probs = []
        for half in range(2):
            mine = scores[half * WINDOW : (half + 1) * WINDOW]
            if allowed is not None:
                mine = jnp.where(allowed, mine, masked_score)
            top = jnp.max(mine, axis=0, keepdims=True)
            terms = jnp.exp(mine - top)
            total = jnp.sum(terms, axis=0, keepdims=True)
            probs.append((terms * (1.0 / total)).astype(bf16))
            head = 2 * pair + half
            lse_ref[head : head + 1, :] = top + jnp.log(total)
        out = dot_tn(jnp.concatenate(probs, axis=0), stack_heads(part(2, pair)))
        att_ref[:, pair * PAIR : (pair + 1) * PAIR] = out.astype(bf16)


def attend_kernel(layer, place_ref, *refs):
    if layer == 0:
        tokens_ref, marks_ref, *refs = refs
        shuffle = shuffle_of(place_ref, 0)
        stream = dot(shuffle, tokens_ref[...])
    else:
        pieces, refs = refs[:4], refs[4:]
        stream = jnp.concatenate(
            [p[...].reshape(BAND, p.shape[-1]) for p in pieces], axis=0
        ).astype(f32)
    gain_ref, shift_ref, s0, s1, s2, s3, p0, p1, p2, p3, x_ref, normed_ref, qkv_ref, att_ref, lse_ref, *refs = refs
    *mark_refs, scratch = refs
    share = scratch.shape[1] // 4

    @pl.when(pl.program_id(0) == 0)
    def _():
        assemble_qkv((p0, p1, p2, p3), scratch)

    if layer == 0:
        chosen = shuffle_of(place_ref, 1).astype(f32)
        marks = jnp.sum(chosen * marks_ref[...], axis=0, keepdims=True)
        for k in range(4):
            mark_refs[k][pl.ds(pl.program_id(0), 1), :] = marks[:, k * BAND : (k + 1) * BAND]
    x_ref[...] = stream.astype(bf16)
    normal, _ = statistics(stream)
    normed = (normal * gain_ref[layer, 0:1] + shift_ref[layer, 0:1]).astype(bf16)
    normed_ref[...] = normed
    start = 2 * layer * share
    smalls = (s0, s1, s2, s3)
    bias = jnp.concatenate(
        [r[2:3, start : start + share] for r in smalls]
        + [jnp.zeros((1, 4 * share), f32)]
        + [r[2:3, start + share : start + 2 * share] for r in smalls],
        axis=1,
    )
    qkv = (dot_nt(normed, scratch[...]) + bias).astype(bf16)
    qkv_ref[...] = qkv
    allowed = allowed_of(place_ref) if layer == 1 else None
    attend_core(qkv, allowed, att_ref, lse_ref)


def whole(array):
    zeros = (0,) * array.ndim
    return pl.BlockSpec(array.shape, lambda i, s: zeros)


def rows_of(columns, rows=WINDOW):
    return pl.BlockSpec((rows, columns), lambda i, s: (i, 0))


def tube_of(columns):
    return pl.BlockSpec((4, 1, CELL, columns), lambda i, s: (0, i, 0, 0))


def sums_of(columns):
    return pl.BlockSpec((8, columns), lambda i, s: (0, 0))


def call(kernel, name, place, steps, operands, outs, scratch=(), aliases={}):
    return pl.pallas_call(
        kernel,
        grid_spec=pltpu.PrefetchScalarGridSpec(
            num_scalar_prefetch=1,
            grid=(steps,),
            in_specs=[spec for _, spec in operands],
            out_specs=[spec for _, _, spec in outs],
            scratch_shapes=list(scratch),
        ),
        out_shape=[jax.ShapeDtypeStruct(shape, dtype) for shape, dtype, _ in outs],
        compiler_params=pltpu.CompilerParams(vmem_limit_bytes=VMEM_LIMIT),
        cost_estimate=cost_of(name),
        input_output_aliases=aliases,
        name=name,
    )(place, *[array for array, _ in operands])


def attend(layer, place, inputs, gain, shift, smalls, packs):
    width = gain.shape[-1]
    rows = 4 * WINDOW
    if layer == 0:
        tokens, marks = inputs
        first = [(tokens, rows_of(width)), (marks, rows_of(1))]
    else:
        first = [(p, tube_of(width)) for p in inputs]
    operands = first + [(a, whole(a)) for a in (gain, shift, *smalls, *packs)]
    outs = [
        ((rows, width), bf16, rows_of(width)),
        ((rows, width), bf16, rows_of(width)),
        ((rows, 3 * width), bf16, rows_of(3 * width)),
        ((rows, width), bf16, rows_of(width)),
        ((4 * LSE_ROWS, WINDOW), f32, rows_of(WINDOW, LSE_ROWS)),
    ]
    if layer == 0:
        outs += [((4, BAND), f32, pl.BlockSpec((4, BAND), lambda i, s: (0, 0)))] * 4
    return call(
        partial(attend_kernel, layer), "attend", place, 4, operands, outs,
        [pltpu.VMEM((3 * width, width), bf16)],
    )


def attend_back_core(qkv, grad, lse_ref, allowed):
    width = grad.shape[1]
    pairs = width // PAIR

    def part(j, pair):
        return qkv[:, j * width + pair * PAIR : j * width + (pair + 1) * PAIR]

    def first_of(pair):
        query = part(0, pair) * jnp.asarray(HD ** (-0.5), bf16)
        grad_part = grad[:, pair * PAIR : (pair + 1) * PAIR]
        keys = stack_heads(part(1, pair))
        scores = dot_nt(keys, query)
        grad_probs = dot_nt(stack_heads(part(2, pair)), grad_part)
        return query, grad_part, keys, scores, grad_probs

    low = lax.broadcasted_iota(jnp.int32, (WINDOW, PAIR), 1) < HD
    results = [[], [], []]
    ahead = first_of(0)
    for pair in range(pairs):
        query, grad_part, keys, scores, grad_probs = ahead
        if pair + 1 < pairs:
            ahead = first_of(pair + 1)
        all_probs, all_scores = [], []
        for half in range(2):
            rows = slice(half * WINDOW, (half + 1) * WINDOW)
            mine = scores[rows]
            if allowed is not None:
                mine = jnp.where(allowed, mine, masked_score)
            head = 2 * pair + half
            probs = jnp.exp(mine - lse_ref[head : head + 1, :])
            grad_mine = grad_probs[rows]
            delta = jnp.sum(probs * grad_mine, axis=0, keepdims=True)
            all_probs.append(probs.astype(bf16))
            all_scores.append((probs * (grad_mine - delta)).astype(bf16))
        probs = jnp.concatenate(all_probs, axis=0)
        grad_scores = jnp.concatenate(all_scores, axis=0)
        grad_query = dot_tn(grad_scores, keys) * HD ** (-0.5)
        grad_key = dot(grad_scores, query)
        grad_value = dot(probs, grad_part)
        results[0].append(grad_query.astype(bf16))
        results[1].append(jnp.where(low, grad_key[:WINDOW], grad_key[WINDOW:]).astype(bf16))
        results[2].append(jnp.where(low, grad_value[:WINDOW], grad_value[WINDOW:]).astype(bf16))
    return [jnp.concatenate(part, axis=1) for part in results]


def attend_back_kernel(layer, place_ref, *refs):
    (stream_ref, g1_ref, x_ref, qkv_ref, lse_ref, gain_ref, p0, p1, p2, p3, *outs) = refs
    d0, d1, d2, d3, *outs = outs
    if layer == 1:
        pieces, outs = outs[:4], outs[4:]
    else:
        (final_ref, *outs) = outs
    sums_ref, scratch, out_scratch, acc = outs
    width = stream_ref.shape[1]
    share = width // 4

    @pl.when(pl.program_id(0) == 0)
    def _():
        assemble_qkv((p0, p1, p2, p3), scratch)
        assemble_out((p0, p1, p2, p3), out_scratch)

    grad_att = dot_nt(g1_ref[...], out_scratch[...]).astype(bf16)
    allowed = allowed_of(place_ref) if layer == 1 else None
    parts = attend_back_core(qkv_ref[...], grad_att, lse_ref, allowed)
    for k, ref in enumerate((d0, d1, d2, d3)):
        for j in range(3):
            ref[:, j * share : (j + 1) * share] = parts[j][:, k * share : (k + 1) * share]
    joined = jnp.concatenate(parts, axis=1)
    grad_normed = dot(joined, scratch[...])
    inner, scaled = norm_back(x_ref[...].astype(f32), gain_ref[layer, 0:1], grad_normed)
    gather_sums(acc, [parts[0].astype(f32), parts[2].astype(f32), scaled, grad_normed])
    stream = stream_ref[...] + inner
    if layer == 1:
        for k in range(4):
            pieces[k][...] = (
                stream[k * BAND : (k + 1) * BAND].astype(bf16).reshape(4, 1, CELL, width)
            )
    else:
        shuffle = shuffle_of(place_ref, 1)
        high = stream.astype(bf16)
        low = (stream - high.astype(f32)).astype(bf16)
        final_ref[...] = dot(shuffle, high) + dot(shuffle, low)

    @pl.when(last_step())
    def _():
        total = jnp.sum(acc[...], axis=0, keepdims=True)
        sums_ref[...] = jnp.zeros(sums_ref.shape, f32)
        for k in range(4):
            query = total[:, k * share : (k + 1) * share]
            value = total[:, width + k * share : width + (k + 1) * share]
            sums_ref[pl.ds(place_ref[0] ^ k, 1), : 2 * share] = jnp.concatenate([query, value], axis=1)
        sums_ref[4:5, :] = total[:, 2 * width : 3 * width]
        sums_ref[5:6, :] = total[:, 3 * width :]


def attend_back(layer, place, stream, g1, x, qkv, lse, gain, packs):
    rows, width = stream.shape
    share = width // 4
    operands = [
        (stream, rows_of(width)),
        (g1, rows_of(width)),
        (x, rows_of(width)),
        (qkv, rows_of(3 * width)),
        (lse, rows_of(WINDOW, LSE_ROWS)),
    ] + [(a, whole(a)) for a in (gain, *packs)]
    outs = [((rows, 3 * share), bf16, rows_of(3 * share))] * 4
    if layer == 1:
        outs = outs + [((4, 4, CELL, width), bf16, tube_of(width))] * 4
    else:
        outs = outs + [((rows, width), f32, rows_of(width))]
    outs = outs + [((8, width), f32, sums_of(width))]
    return call(
        partial(attend_back_kernel, layer), "attend_back", place, 4, operands, outs,
        [pltpu.VMEM((3 * width, width), bf16), pltpu.VMEM((width, width), bf16), pltpu.VMEM((8, 4 * width), f32)],
    )


def feed_kernel(layer, place_ref, *refs):
    (
        x_ref, att_ref, a0, a1, a2, a3, vec_ref, gain_ref, shift_ref, s0, s1, s2, s3,
        u0, u1, u2, u3, d0, d1, d2, d3, stream_ref, normed_ref, active_ref, slope_ref, *outs
    ) = refs
    ups, downs = (u0, u1, u2, u3), (d0, d1, d2, d3)
    *pieces, scratch = outs
    width = x_ref.shape[1]

    @pl.when(pl.program_id(0) == 0)
    def _():
        share = width // 4
        for k, part in enumerate((a0, a1, a2, a3)):
            scratch[k * share : (k + 1) * share, :] = part[...]

    stream = x_ref[...].astype(f32) + dot(att_ref[...], scratch[...]) + vec_ref[layer, 0:1]
    stream_ref[...] = stream
    normal, _ = statistics(stream)
    normed = (normal * gain_ref[layer, 1:2] + shift_ref[layer, 1:2]).astype(bf16)
    normed_ref[...] = normed
    total = stream + vec_ref[layer, 1:2]
    units = u0.shape[1]
    ahead = dot(normed, ups[0][...])
    for k in range(4):
        hidden = ahead
        if k < 3:
            ahead = dot(normed, ups[k + 1][...])
        cut = slice(k * units, (k + 1) * units)
        active, slope = gelu_both(hidden + (s0, s1, s2, s3)[k][layer : layer + 1, :])
        active_ref[:, cut] = active
        slope_ref[:, cut] = slope
        total = total + dot(active, downs[k][...])
    total = total.astype(bf16)
    if layer == 0:
        for k in range(4):
            pieces[k][...] = total[k * BAND : (k + 1) * BAND].reshape(1, BAND, width)
    else:
        pieces[0][...] = total


def feed_specs(layer, packs):
    ups, downs, across = packs
    width = across[0].shape[1]
    block = (width, width)

    def of_layer(a):
        return (a, pl.BlockSpec((None, *block), lambda i, s: (layer, 0, 0)))

    def of_half(a, half):
        return (a, pl.BlockSpec(block, lambda i, s: (half, 0)))

    return [
        *[of_layer(a) for a in ups],
        *[of_half(a, 0) for a in across],
        *[of_layer(a) for a in downs],
        *[of_half(a, 1) for a in across],
    ]


def feed(layer, place, x, att, attn_packs, vecs, gain, shift, smalls, packs):
    rows, width = x.shape
    units = packs[0][0].shape[2]
    last = pl.BlockSpec((width // 4, width), lambda i, s: (3, 0))
    operands = (
        [(x, rows_of(width)), (att, rows_of(width))]
        + [(a, last) for a in attn_packs]
        + [(a, whole(a)) for a in (vecs, gain, shift, *smalls)]
        + feed_specs(layer, packs)
    )
    outs = [
        ((rows, width), f32, rows_of(width)),
        ((rows, width), bf16, rows_of(width)),
        ((rows, 4 * units), bf16, rows_of(4 * units)),
        ((rows, 4 * units), bf16, rows_of(4 * units)),
    ]
    if layer == 0:
        piece = pl.BlockSpec((1, BAND, width), lambda i, s: (i, 0, 0))
        outs = outs + [((4, BAND, width), bf16, piece)] * 4
    else:
        outs = outs + [((rows, width), bf16, rows_of(width))]
    return call(
        partial(feed_kernel, layer), "feed", place, 4, operands, outs,
        [pltpu.VMEM((width, width), bf16)],
    )


def loss_kernel(place_ref, final_ref, head_ref, m0, m1, m2, m3, grad_ref, g2_ref, loss_ref, acc):
    logits = dot(final_ref[...], head_ref[...])
    spread = jnp.concatenate(
        [jnp.broadcast_to(m[f : f + 1, :], (CELL, BAND)) for m in (m0, m1, m2, m3) for f in range(4)],
        axis=0,
    )
    position = lax.broadcasted_iota(jnp.int32, (WINDOW, BAND), 0)
    lane = lax.broadcasted_iota(jnp.int32, (WINDOW, BAND), 1)
    mine = lane == pl.program_id(0) * CELL + (position & (CELL - 1))
    mark = jnp.sum(jnp.where(mine, spread, 0.0), axis=1, keepdims=True).astype(jnp.int32)
    place_of = lax.broadcasted_iota(jnp.int32, (WINDOW, 1), 0)
    frame = 4 * ((place_of >> 6) ^ place_ref[0]) + ((place_of >> 4) & 3)
    weight = jnp.where(frame < place_ref[1], (mark & 1).astype(f32), 0.0)
    top = jnp.max(logits, axis=1, keepdims=True)
    terms = jnp.exp(logits - top)
    total = jnp.sum(terms, axis=1, keepdims=True)
    code = lax.broadcasted_iota(jnp.int32, logits.shape, 1)
    chosen = code == (mark >> 1)
    picked = jnp.sum(jnp.where(chosen, logits, 0.0), axis=1, keepdims=True)
    entry = weight * (top + jnp.log(total) - picked)
    soft = terms * (1.0 / total)
    grad_logits = (weight * (soft - jnp.where(chosen, 1.0, 0.0))).astype(bf16)
    grad = dot_nt(grad_logits, head_ref[...])
    grad_ref[...] = grad
    g2_ref[...] = grad.astype(bf16)
    gather_sums(acc, [jnp.broadcast_to(entry, (WINDOW, PAIR))])

    @pl.when(last_step())
    def _():
        total = jnp.sum(acc[...], axis=0, keepdims=True)
        loss_ref[...] = jnp.broadcast_to(total[:, :1], loss_ref.shape)


def code_loss(place, final, code_head, marks):
    rows, width = final.shape
    operands = [(final, rows_of(width))] + [(a, whole(a)) for a in (code_head, *marks)]
    outs = [
        ((rows, width), f32, rows_of(width)),
        ((rows, width), bf16, rows_of(width)),
        ((8, width), f32, sums_of(width)),
    ]
    return call(
        loss_kernel, "code_loss", place, 4, operands, outs, [pltpu.VMEM((8, PAIR), f32)]
    )


def feed_back_kernel(layer, place_ref, *refs):
    if layer == 1:
        grad_ref, *refs = refs
        grad = grad_ref[...]
    else:
        pieces, refs = refs[:4], refs[4:]
        grad = jnp.concatenate(
            [p[...].reshape(BAND, p.shape[-1]) for p in pieces], axis=0
        ).astype(f32)
    (
        slope_ref, stream_ref, gain_ref, u0, u1, u2, u3, d0, d1, d2, d3, hidden_ref, next_ref, g1_ref, *outs
    ) = refs
    if layer == 0:
        (g2_ref, *outs) = outs
    sums_ref, acc = outs
    g2 = grad.astype(bf16)
    if layer == 0:
        g2_ref[...] = g2
    units = u0.shape[1]
    grad_normed = jnp.zeros(grad.shape, f32)
    sums = []
    ups, downs = (u0, u1, u2, u3), (d0, d1, d2, d3)
    ahead = dot_nt(g2, downs[0][...])
    for k in range(4):
        grad_active = ahead
        if k < 3:
            ahead = dot_nt(g2, downs[k + 1][...])
        cut = slice(k * units, (k + 1) * units)
        grad_hidden = (grad_active * slope_ref[:, cut].astype(f32)).astype(bf16)
        hidden_ref[:, cut] = grad_hidden
        sums.append(grad_hidden.astype(f32))
        grad_normed = grad_normed + dot_nt(grad_hidden, ups[k][...])
    inner, scaled = norm_back(stream_ref[...], gain_ref[layer, 1:2], grad_normed)
    grad = grad + inner
    next_ref[...] = grad
    g1 = grad.astype(bf16)
    g1_ref[...] = g1
    gather_sums(acc, sums + [scaled, grad_normed, g2.astype(f32), g1.astype(f32)])

    @pl.when(last_step())
    def _():
        total = jnp.sum(acc[...], axis=0, keepdims=True)
        for k in range(4):
            sums_ref[pl.ds(place_ref[0] ^ k, 1), :] = total[:, k * units : (k + 1) * units]
            start = 4 * units + k * grad.shape[1]
            sums_ref[4 + k : 5 + k, :] = total[:, start : start + grad.shape[1]]


def feed_back(layer, place, grad, slope, stream, gain, packs):
    rows, width = stream.shape
    units = packs[0][0].shape[2]
    if layer == 1:
        first = [(grad, rows_of(width))]
    else:
        piece = pl.BlockSpec((1, BAND, width), lambda i, s: (i, 0, 0))
        first = [(p, piece) for p in grad]
    operands = (
        first
        + [(slope, rows_of(4 * units)), (stream, rows_of(width))]
        + [(gain, whole(gain))]
        + feed_specs(layer, packs)
    )
    outs = [
        ((rows, 4 * units), bf16, rows_of(4 * units)),
        ((rows, width), f32, rows_of(width)),
        ((rows, width), bf16, rows_of(width)),
    ]
    if layer == 0:
        outs = outs + [((rows, width), bf16, rows_of(width))]
    outs = outs + [((8, width), f32, sums_of(width))]
    return call(
        partial(feed_back_kernel, layer), "feed_back", place, 4, operands, outs,
        [pltpu.VMEM((8, 4 * units + 4 * width), f32)],
    )


ORDER = (1, 3, 2, 0)


def grad_kernel(kind, place_ref, *refs):
    refs = list(refs)

    def take(count):
        taken = refs[:count]
        del refs[:count]
        return taken

    sources = {"attn": 7, "up": 2, "down": 2}[kind]
    arrays = take(sources)
    outs = take(4)
    bufs = take(7 if kind == "attn" else 5)
    out_bufs = take(4)
    in_sem, out_sem = refs
    width = out_bufs[0].shape[-1]
    copies = []

    def fetch(source, buf):
        copy = pltpu.make_async_copy(source, buf, in_sem.at[len(copies)])
        copy.start()
        copies.append(copy)
        return [copy, buf]

    def ready(item):
        if item[0] is not None:
            item[0].wait()
            item[0] = None
        return item[1]

    def columns(ref, k):
        return ref.at[:, pl.ds(k * width, width)]

    if kind == "attn":
        normed = fetch(arrays[0], bufs[0])
        sides = [fetch(arrays[3], bufs[3])]
        g1 = fetch(arrays[1], bufs[1])
        att = fetch(arrays[2], bufs[2])
        sides += [fetch(arrays[3 + n], bufs[3 + n]) for n in range(1, 4)]
        plan = [(normed, side) for side in sides]
    else:
        fixed, split = (arrays[1], arrays[0]) if kind == "down" else (arrays[0], arrays[1])
        fixed = fetch(fixed, bufs[4])
        split = [fetch(columns(split, k), bufs[n]) for n, k in enumerate(ORDER)]
        plan = [(s, fixed) if kind == "down" else (fixed, s) for s in split]
    sent = []
    for n, (left, right) in enumerate(plan):
        value = dot_tn(ready(left)[...], ready(right)[...])
        if kind == "attn":
            share = width // 4
            k = ORDER[n]
            beside = dot_tn(ready(g1)[...], ready(att)[:, k * share : (k + 1) * share])
            value = jnp.concatenate([value, beside], axis=1)
        out_bufs[n][...] = value.astype(bf16)
        copy = pltpu.make_async_copy(out_bufs[n], outs[n], out_sem.at[n])
        copy.start()
        sent.append(copy)
    for copy in sent:
        copy.wait()


def grads(kind, place, arrays, width):
    rows = arrays[1].shape[0]
    if kind == "attn":
        arrays = list(arrays[:3]) + [arrays[3][k] for k in ORDER]
        loads = [a.shape for a in arrays]
    else:
        loads = [(rows, width)] * 5
    anywhere = pl.BlockSpec(memory_space=pl.ANY)
    scratch = (
        [pltpu.VMEM(shape, bf16) for shape in loads]
        + [pltpu.VMEM((width, width), bf16)] * 4
        + [pltpu.SemaphoreType.DMA((len(loads),)), pltpu.SemaphoreType.DMA((4,))]
    )
    operands = [(a, anywhere) for a in arrays]
    outs = [((width, width), bf16, anywhere)] * 4
    return call(partial(grad_kernel, kind), "grads_" + kind, place, 1, operands, outs, scratch)


def emit_kernel(attention, split, aliased, place_ref, *refs):
    if split:
        mine_ref, other_ref, *refs = refs
        mine = pl.program_id(0) == place_ref[2]
        value = jnp.where(mine, mine_ref[...].astype(f32), other_ref[...].astype(f32))
    else:
        whole_ref, *refs = refs
        value = whole_ref[...].astype(f32)
    outs = refs[aliased:]
    if attention:
        qkv_ref, out_ref = outs
        share = qkv_ref.shape[-1]
        for j in range(3):
            qkv_ref[0, j] = value[:, j * share : (j + 1) * share]
        out_ref[0] = value[:, 3 * share :].T
    else:
        outs[0][0] = value


def emit(place, layer, attention, summed, earlier):
    split = len(summed) == 2
    width = summed[0].shape[1]
    half = width // 2
    share = width // 4
    if attention:
        outs = [
            ((2, 3, width, share), f32, pl.BlockSpec((1, 3, half, share), lambda i, s: (layer, 0, i, 0))),
            ((2, share, width), f32, pl.BlockSpec((1, share, half), lambda i, s: (layer, 0, i))),
        ]
    else:
        outs = [((2, width, width), f32, pl.BlockSpec((1, half, width), lambda i, s: (layer, i, 0)))]
    if split:
        operands = [(a, whole(a)) for a in summed]
    else:
        operands = [(summed[0], pl.BlockSpec((half, width), lambda i, s: (i, 0)))]
    aliases = {}
    if earlier is not None:
        aliases = {1 + len(operands) + n: n for n in range(len(earlier))}
        operands += [(e, pl.BlockSpec(memory_space=pl.ANY)) for e in earlier]
    return call(
        partial(emit_kernel, attention, split, len(aliases)), "emit", place, 2, operands, outs,
        aliases=aliases,
    )


def head_swap(values, distance):
    count = lax.axis_size("head")
    return lax.ppermute(values, "head", [(i, i ^ distance) for i in range(count)])


def clip_swap(values, distance):
    count = lax.axis_size("clip")
    return lax.ppermute(values, "clip", [(i, i ^ distance) for i in range(count)])


class Order:
    def __init__(self):
        self.last = ()
        self.pending = []

    def run(self, step, *values):
        values, _ = lax.optimization_barrier((values, self.last))
        out = step(*values)
        self.last = (jax.tree.leaves(out)[0],)
        return out

    def send(self, swap, values, distance):
        values, _ = lax.optimization_barrier((values, self.last))
        out = swap(values, distance)
        self.pending.append(out)
        return out

    def close(self):
        self.last = self.last + tuple(self.pending)
        self.pending = []


class Pack:
    def __init__(self, order, place, kind, arrays, width):
        self.order = order
        self.upper = place[2] == 1
        self.parts = order.run(lambda *a: grads(kind, place, a, width), *arrays)
        count = lax.axis_size("clip")
        self.distances = [1 << n for n in range(count.bit_length() - 1)] + [1]
        self.stage = 0

    def prepare(self):
        run = self.order.run
        if self.stage == 1:

            def add(part, beyond):
                return (part.astype(f32) + beyond.astype(f32)).astype(bf16)

            self.leaving = run(add, self.parts[2], self.beyond)
        elif self.stage == 2:

            def add(part, beside, across):
                total = part.astype(f32) + beside.astype(f32) + across.astype(f32)
                half = total.shape[0] // 2
                low, high = total[:half], total[half:]
                return (
                    jnp.where(self.upper, low, high).astype(bf16),
                    jnp.where(self.upper, high, low).astype(bf16),
                )

            self.leaving, self.sum = run(add, self.parts[3], self.beside, self.moved)
        elif self.stage > 2:

            def add(total, moved):
                return (total.astype(f32) + moved.astype(f32)).astype(bf16)

            self.leaving = self.sum = run(add, self.sum, self.moved)

    def launch(self):
        send = self.order.send
        if self.stage == 0:
            self.beside = send(head_swap, self.parts[0], 1)
            self.beyond = send(head_swap, self.parts[1], 1)
        elif self.stage == 1:
            self.moved = send(head_swap, self.leaving, 2)
        else:
            self.moved = send(clip_swap, self.leaving, self.distances[self.stage - 2])
        self.stage += 1

    def done(self):
        return self.stage == 2 + len(self.distances)

    def whole(self):
        assert self.done()
        return self.sum, self.moved


def on_device(
    tokens,
    frame_counts,
    token_mask,
    targets,
    norm_gain,
    norm_bias,
    w_qkv,
    qv_bias,
    w_out,
    vec_bias,
    w_up,
    up_bias,
    w_down,
    code_head,
):
    head_index = lax.axis_index("head")
    width = tokens.shape[1]
    share = w_out.shape[1]
    upper = lax.axis_index("clip") & 1
    place = jnp.stack(
        [head_index.astype(jnp.int32), frame_counts[0], upper.astype(jnp.int32)]
    )
    order = Order()

    def tied(values, *after):
        return lax.optimization_barrier((values, after))[0]

    clip_count = lax.axis_size("clip")
    own_small = jnp.concatenate([up_bias, qv_bias.reshape(1, width)], axis=0)
    piece = (w_up.shape[1] + w_down.shape[1]) // clip_count
    first_row = lax.axis_index("clip") * piece

    def chunk(layer):
        halves = [w_up[layer], w_down[layer]]
        rows = halves[0].shape[0]
        start = first_row % rows
        parts = [lax.dynamic_slice_in_dim(h, start, piece, 0) for h in halves]
        return jnp.where(first_row < rows, parts[0], parts[1])

    def gather_feed(chunk_across):
        return lax.all_gather(chunk_across, "clip", axis=0, tiled=True)

    def attn_pack(layer):
        transposed = w_qkv[layer].swapaxes(1, 2).reshape(-1, width)
        return jnp.concatenate([transposed, w_out[layer]], axis=0)

    def spread(own, across):
        return [own, head_swap(own, 1), across, head_swap(across, 1)]

    chunk_0 = head_swap(chunk(0), 2)
    smalls = spread(own_small, head_swap(own_small, 2))
    own = tied(attn_pack(0), chunk_0, smalls[2])
    attn = [spread(own, head_swap(own, 2)), None]
    feed_across = [gather_feed(chunk_0), None]
    ups = [w_up, head_swap(tied(w_up, attn[0][2]), 1)]
    downs = [w_down, head_swap(tied(w_down, attn[0][2]), 1)]
    packs = [None, None]

    marks = (2 * targets + token_mask).astype(f32).reshape(-1, 1)
    kept = []
    inputs = (tokens, marks)
    for layer in range(2):
        x, normed, qkv, att, lse, *mark_pieces = order.run(
            lambda *a: attend(layer, place, a, norm_gain, norm_bias, smalls, attn[layer]), *inputs
        )
        if layer == 0:
            marks = [mark_pieces[0]] + [head_swap(mark_pieces[k], k) for k in (1, 2, 3)]
            chunk_1 = head_swap(tied(chunk(1), x), 2)
            own = tied(attn_pack(1), chunk_1)
            attn[1] = spread(own, head_swap(own, 2))
            feed_across[1] = gather_feed(chunk_1)
        across = tied(feed_across[layer], x)
        packs[layer] = (ups, downs, [across, head_swap(across, 1)])
        stream, normed2, active, slope, *outs = order.run(
            lambda a, b: feed(
                layer, place, a, b, attn[layer], vec_bias, norm_gain, norm_bias, smalls, packs[layer]
            ),
            x, att,
        )
        kept.append((x, normed, qkv, att, lse, stream, normed2, active, slope))
        if layer == 0:
            inputs = [outs[0]] + [order.send(head_swap, outs[k], k) for k in (1, 2, 3)]
            inputs = [p.reshape(4, 4, CELL, width) for p in inputs]
            order.close()
    grad, g2, loss_sum = order.run(lambda a: code_loss(place, a, code_head, marks), outs[0])

    def run_feed_back(layer, grad):
        x, normed, qkv, att, lse, stream, normed2, active, slope = kept[layer]
        return order.run(
            lambda a: feed_back(layer, place, a, slope, stream, norm_gain, packs[layer]), grad
        )

    def run_attend_back(layer, grad_next, g1):
        x, normed, qkv, att, lse, *_ = kept[layer]
        return order.run(
            lambda a, b: attend_back(
                layer, place, a, b, x, qkv, lse, norm_gain, attn[layer]
            ),
            grad_next, g1,
        )

    def pack(kind, *arrays):
        return Pack(order, place, kind, arrays, width)

    def move(*ones):
        for one in ones:
            one.prepare()
        for one in ones:
            one.launch()

    normed, att, normed2, active = kept[1][1], kept[1][3], kept[1][6], kept[1][7]
    down_1 = pack("down", active, g2)
    move(down_1)
    grad_hidden, grad_next, g1, feed_sum_1 = run_feed_back(1, grad)
    order.close()

    up_1 = pack("up", normed2, grad_hidden)
    move(down_1, up_1)
    *rest, attn_sum_1 = run_attend_back(1, grad_next, g1)
    order.close()

    sides, outs = rest[:4], rest[4:]
    grad = [outs[0]] + [order.send(head_swap, outs[k], k) for k in (1, 2, 3)]
    grad = [p.reshape(4, BAND, width) for p in grad]
    move(down_1)
    attn_1 = pack("attn", normed, g1, att, sides)
    order.close()

    normed, att, normed2, active = kept[0][1], kept[0][3], kept[0][6], kept[0][7]
    move(up_1, attn_1, down_1)
    grad_hidden, grad_next, g1, g2, feed_sum_0 = run_feed_back(0, grad)
    down_0 = pack("down", active, g2)
    order.close()

    move(attn_1, up_1, down_1, down_0)
    up_0 = pack("up", normed2, grad_hidden)
    *rest, attn_sum_0 = run_attend_back(0, grad_next, g1)
    sides, (grad_input,) = rest[:4], rest[4:]
    order.close()

    move(down_0, up_0, attn_1, up_1, down_1)
    attn_0 = pack("attn", normed, g1, att, sides)
    packed = jnp.concatenate([feed_sum_0, feed_sum_1, attn_sum_0, attn_sum_1, loss_sum], axis=0)
    order.close()

    swaps = [(head_swap, 1), (head_swap, 2)]
    swaps += [(clip_swap, 1 << n) for n in range(clip_count.bit_length() - 1)]
    moving = [attn_0, up_0, down_0, attn_1, up_1, down_1]
    while not attn_0.done() or swaps:
        move(*[one for one in moving if not one.done()])
        if swaps:
            swap, distance = swaps.pop(0)
            packed = packed + order.send(swap, packed, distance)
        order.close()

    attn_out = emit(place, 0, True, attn_0.whole(), emit(place, 1, True, attn_1.whole(), None))
    up_out = emit(place, 0, False, up_0.whole(), emit(place, 1, False, up_1.whole(), None))
    down_out = emit(place, 0, False, down_0.whole(), emit(place, 1, False, down_1.whole(), None))

    feed_sums = packed[:16].reshape(2, 8, width)
    attn_sums = packed[16:32].reshape(2, 8, width)
    loss_total = packed[32, 0]
    own_feed = lax.dynamic_index_in_dim(feed_sums, head_index, 1, keepdims=False)
    own_attn = lax.dynamic_index_in_dim(attn_sums, head_index, 1, keepdims=False)
    slot_total = clip_count * frame_counts.shape[0] * FRAMES * SIDE * SIDE

    return (
        loss_total / slot_total,
        grad_input,
        jnp.stack([attn_sums[:, 4], feed_sums[:, 4]], axis=1),
        jnp.stack([attn_sums[:, 5], feed_sums[:, 5]], axis=1),
        attn_out[0],
        own_attn[:, : 2 * share].reshape(2, 2, share),
        attn_out[1],
        jnp.stack([feed_sums[:, 7], feed_sums[:, 6]], axis=1),
        up_out[0],
        own_feed,
        down_out[0],
    )


def solution(mesh):
    placed = (
        P(("clip", "head"), None),
        P("clip"),
        P(("clip", "head")),
        P(("clip", "head")),
        P(),
        P(),
        P(None, None, None, "head"),
        P(None, None, "head"),
        P(None, "head", None),
        P(),
        P(None, None, "head"),
        P(None, "head"),
        P(None, "head", None),
        P(),
    )
    return jax.shard_map(
        on_device,
        mesh=mesh,
        in_specs=placed,
        out_specs=(
            P(),
            P(("clip", "head"), None),
            P(),
            P(),
            P(None, None, None, "head"),
            P(None, None, "head"),
            P(None, "head", None),
            P(),
            P(None, None, "head"),
            P(None, "head"),
            P(None, "head", None),
        ),
        check_vma=False,
    )
```

```python
from functools import partial

import jax
import jax.numpy as jnp
from jax import lax
from jax.experimental import pallas as pl
from jax.experimental.pallas import tpu as pltpu
from jax.sharding import PartitionSpec as P

HD = 64
FRAMES = 16
SIDE = 16
TUBE = 4
WINDOW = 256
PAIR = 128
BAND = 64
CELL = 16
LSE_ROWS = 16

epsilon = 1e-06
masked_score = -1e30
f32 = jnp.float32
bf16 = jnp.bfloat16
VMEM_LIMIT = 56 * 1024 * 1024
TIMES = {
    "attend": 17, "feed": 23, "code_loss": 10, "feed_back": 21, "attend_back": 25,
    "grads_down": 8, "grads_up": 8, "grads_attn": 8, "emit": 3,
}
SCALE = 0.0001


def cost_of(name):
    time = TIMES[name] * SCALE
    return pl.CostEstimate(flops=int(time * 1.15e9), bytes_accessed=int(time * 3.6e6), transcendentals=0)


def dot(a, b):
    return lax.dot_general(a, b, (((1,), (0,)), ((), ())), preferred_element_type=f32)


def dot_nt(a, b):
    return lax.dot_general(a, b, (((1,), (1,)), ((), ())), preferred_element_type=f32)


def dot_tn(a, b):
    return lax.dot_general(a, b, (((0,), (0,)), ((), ())), preferred_element_type=f32)


def statistics(stream):
    centre = jnp.mean(stream, axis=-1, keepdims=True)
    centred = stream - centre
    spread = jnp.mean(centred * centred, axis=-1, keepdims=True)
    scale = lax.rsqrt(spread + epsilon)
    return centred * scale, scale


def by_eight(values):
    rows, columns = values.shape
    return jnp.sum(values.reshape(rows // 8, 8, columns), axis=0)


def gather_sums(acc_ref, values):
    first = pl.program_id(0) == 0
    parts = jnp.concatenate([by_eight(v) for v in values], axis=1)

    @pl.when(first)
    def _():
        acc_ref[...] = parts

    @pl.when(jnp.logical_not(first))
    def _():
        acc_ref[...] += parts


ORDER = (1, 3, 0, 2)


def step_rows():
    return pl.ds(pl.multiple_of(pl.program_id(0) * WINDOW, WINDOW), WINDOW)


def put_parts(leaving_ref, staying_ref, gradient_of):
    for n, k in enumerate(ORDER):
        (leaving_ref if n < 2 else staying_ref)[n % 2] = gradient_of(k).astype(bf16)


def parts_outs(width):
    spec = pl.BlockSpec((2, width, width), lambda i, s: (0, 0, 0))
    return [((2, width, width), bf16, spec)] * 2


def last_step():
    return pl.program_id(0) == pl.num_programs(0) - 1


def norm_back(stream, gain, grad):
    normal, scale = statistics(stream)
    scaled = grad * gain
    mean_plain = jnp.mean(scaled, axis=-1, keepdims=True)
    mean_normal = jnp.mean(scaled * normal, axis=-1, keepdims=True)
    inner = scale * (scaled - mean_plain - normal * mean_normal)
    return inner, grad * normal


def gelu_both(hidden):
    root = 0.7978845608028654
    cubic = 0.044715
    square = hidden * hidden
    bend = jnp.tanh(hidden * (root + root * cubic * square))
    rise = 0.5 + 0.5 * bend
    active = hidden * rise
    slope = rise + (active - active * rise) * (2.0 * root + 6.0 * root * cubic * square)
    return active.astype(bf16), slope.astype(bf16)


def allowed_of(place_ref):
    head_index = place_ref[0]
    frame_count = place_ref[1]

    def valid(axis):
        position = lax.broadcasted_iota(jnp.int32, (WINDOW, WINDOW), axis)
        frame = 4 * ((position >> 6) ^ head_index) + ((position >> 4) & 3)
        return frame < frame_count

    return jnp.logical_or(valid(0), jnp.logical_not(valid(1)))


def shuffle_of(place_ref, axis):
    arranged = lax.broadcasted_iota(jnp.int32, (WINDOW, WINDOW), axis)
    plain = lax.broadcasted_iota(jnp.int32, (WINDOW, WINDOW), 1 - axis)
    band = (arranged >> 6) ^ place_ref[0]
    source = band * BAND + ((arranged >> 2) & 3) * 16 + ((arranged >> 4) & 3) * 4 + (arranged & 3)
    return (source == plain).astype(f32).astype(bf16)


def assemble_qkv(packs, scratch):
    width = scratch.shape[1]
    share = width // 4
    for k in range(4):
        for j in range(3):
            start = j * width + k * share
            scratch[start : start + share, :] = packs[k][j * share : (j + 1) * share, :]


def assemble_out(packs, scratch):
    share = scratch.shape[0] // 4
    for k in range(4):
        scratch[k * share : (k + 1) * share, :] = packs[k][3 * share :, :]


def stack_heads(pair):
    low = lax.broadcasted_iota(jnp.int32, pair.shape, 1) < HD
    zero = jnp.zeros((), bf16)
    return jnp.concatenate([jnp.where(low, pair, zero), jnp.where(low, zero, pair)], axis=0)


def attend_core(qkv, allowed, att_ref, lse_ref, part_ref):
    width = att_ref.shape[1]
    pairs = width // PAIR

    def part(j, pair):
        return qkv[:, j * width + pair * PAIR : j * width + (pair + 1) * PAIR]

    def scores_of(pair):
        query = part(0, pair) * jnp.asarray(HD ** (-0.5), bf16)
        return dot_nt(stack_heads(part(1, pair)), query)

    ahead = scores_of(0)
    for pair in range(pairs):
        scores = ahead
        if pair + 1 < pairs:
            ahead = scores_of(pair + 1)
        probs = []
        for half in range(2):
            mine = scores[half * WINDOW : (half + 1) * WINDOW]
            if allowed is not None:
                mine = jnp.where(allowed, mine, masked_score)
            top = jnp.max(mine, axis=0, keepdims=True)
            terms = jnp.exp(mine - top)
            total = jnp.sum(terms, axis=0, keepdims=True)
            probs.append((terms * (1.0 / total)).astype(bf16))
            head = 2 * pair + half
            lse_ref[head : head + 1, :] = top + jnp.log(total)
        out = dot_tn(jnp.concatenate(probs, axis=0), stack_heads(part(2, pair)))
        att_ref[:, pair * PAIR : (pair + 1) * PAIR] = out.astype(bf16)
    share = width // 4
    for k in range(4):
        part_ref[k] = att_ref[:, k * share : (k + 1) * share]


def attend_kernel(layer, place_ref, *refs):
    if layer == 0:
        tokens_ref, marks_ref, *refs = refs
        shuffle = shuffle_of(place_ref, 0)
        stream = dot(shuffle, tokens_ref[...])
    else:
        pieces, refs = refs[:4], refs[4:]
        stream = jnp.concatenate(
            [p[...].reshape(BAND, p.shape[-1]) for p in pieces], axis=0
        ).astype(f32)
    gain_ref, shift_ref, s0, s1, s2, s3, p0, p1, p2, p3, x_ref, normed_ref, qkv_ref, att_ref, lse_ref, part_ref, *refs = refs
    *mark_refs, scratch = refs
    share = scratch.shape[1] // 4

    @pl.when(pl.program_id(0) == 0)
    def _():
        assemble_qkv((p0, p1, p2, p3), scratch)

    if layer == 0:
        chosen = shuffle_of(place_ref, 1).astype(f32)
        marks = jnp.sum(chosen * marks_ref[...], axis=0, keepdims=True)
        for k in range(4):
            mark_refs[k][pl.ds(pl.program_id(0), 1), :] = marks[:, k * BAND : (k + 1) * BAND]
    x_ref[...] = stream.astype(bf16)
    normal, _ = statistics(stream)
    normed = (normal * gain_ref[layer, 0:1] + shift_ref[layer, 0:1]).astype(bf16)
    normed_ref[...] = normed
    start = 2 * layer * share
    smalls = (s0, s1, s2, s3)
    bias = jnp.concatenate(
        [r[2:3, start : start + share] for r in smalls]
        + [jnp.zeros((1, 4 * share), f32)]
        + [r[2:3, start + share : start + 2 * share] for r in smalls],
        axis=1,
    )
    qkv = (dot_nt(normed, scratch[...]) + bias).astype(bf16)
    qkv_ref[...] = qkv
    allowed = allowed_of(place_ref) if layer == 1 else None
    attend_core(qkv, allowed, att_ref, lse_ref, part_ref)


def whole(array):
    zeros = (0,) * array.ndim
    return pl.BlockSpec(array.shape, lambda i, s: zeros)


def rows_of(columns, rows=WINDOW):
    return pl.BlockSpec((rows, columns), lambda i, s: (i, 0))


def parts_of(columns):
    return pl.BlockSpec((4, WINDOW, columns), lambda i, s: (0, i, 0))


def tube_of(columns):
    return pl.BlockSpec((4, 1, CELL, columns), lambda i, s: (0, i, 0, 0))


def sums_of(columns):
    return pl.BlockSpec((8, columns), lambda i, s: (0, 0))


def call(kernel, name, place, steps, operands, outs, scratch=(), aliases={}):
    return pl.pallas_call(
        kernel,
        grid_spec=pltpu.PrefetchScalarGridSpec(
            num_scalar_prefetch=1,
            grid=(steps,),
            in_specs=[spec for _, spec in operands],
            out_specs=[spec for _, _, spec in outs],
            scratch_shapes=list(scratch),
        ),
        out_shape=[jax.ShapeDtypeStruct(shape, dtype) for shape, dtype, _ in outs],
        compiler_params=pltpu.CompilerParams(vmem_limit_bytes=VMEM_LIMIT),
        cost_estimate=cost_of(name),
        input_output_aliases=aliases,
        name=name,
    )(place, *[array for array, _ in operands])


def attend(layer, place, inputs, gain, shift, smalls, packs):
    width = gain.shape[-1]
    rows = 4 * WINDOW
    if layer == 0:
        tokens, marks = inputs
        first = [(tokens, rows_of(width)), (marks, rows_of(1))]
    else:
        first = [(p, tube_of(width)) for p in inputs]
    operands = first + [(a, whole(a)) for a in (gain, shift, *smalls, *packs)]
    outs = [
        ((rows, width), bf16, rows_of(width)),
        ((rows, width), bf16, rows_of(width)),
        ((rows, 3 * width), bf16, rows_of(3 * width)),
        ((rows, width), bf16, rows_of(width)),
        ((4 * LSE_ROWS, WINDOW), f32, rows_of(WINDOW, LSE_ROWS)),
        ((4, rows, width // 4), bf16, parts_of(width // 4)),
    ]
    if layer == 0:
        outs += [((4, BAND), f32, pl.BlockSpec((4, BAND), lambda i, s: (0, 0)))] * 4
    return call(
        partial(attend_kernel, layer), "attend", place, 4, operands, outs,
        [pltpu.VMEM((3 * width, width), bf16)],
    )


def attend_back_core(qkv, grad, lse_ref, allowed):
    width = grad.shape[1]
    pairs = width // PAIR

    def part(j, pair):
        return qkv[:, j * width + pair * PAIR : j * width + (pair + 1) * PAIR]

    def first_of(pair):
        query = part(0, pair) * jnp.asarray(HD ** (-0.5), bf16)
        grad_part = grad[:, pair * PAIR : (pair + 1) * PAIR]
        keys = stack_heads(part(1, pair))
        scores = dot_nt(keys, query)
        grad_probs = dot_nt(stack_heads(part(2, pair)), grad_part)
        return query, grad_part, keys, scores, grad_probs

    low = lax.broadcasted_iota(jnp.int32, (WINDOW, PAIR), 1) < HD
    results = [[], [], []]
    ahead = first_of(0)
    for pair in range(pairs):
        query, grad_part, keys, scores, grad_probs = ahead
        if pair + 1 < pairs:
            ahead = first_of(pair + 1)
        all_probs, all_scores = [], []
        for half in range(2):
            rows = slice(half * WINDOW, (half + 1) * WINDOW)
            mine = scores[rows]
            if allowed is not None:
                mine = jnp.where(allowed, mine, masked_score)
            head = 2 * pair + half
            probs = jnp.exp(mine - lse_ref[head : head + 1, :])
            grad_mine = grad_probs[rows]
            delta = jnp.sum(probs * grad_mine, axis=0, keepdims=True)
            all_probs.append(probs.astype(bf16))
            all_scores.append((probs * (grad_mine - delta)).astype(bf16))
        probs = jnp.concatenate(all_probs, axis=0)
        grad_scores = jnp.concatenate(all_scores, axis=0)
        grad_query = dot_tn(grad_scores, keys) * HD ** (-0.5)
        grad_key = dot(grad_scores, query)
        grad_value = dot(probs, grad_part)
        results[0].append(grad_query.astype(bf16))
        results[1].append(jnp.where(low, grad_key[:WINDOW], grad_key[WINDOW:]).astype(bf16))
        results[2].append(jnp.where(low, grad_value[:WINDOW], grad_value[WINDOW:]).astype(bf16))
    return [jnp.concatenate(part, axis=1) for part in results]


def attend_back_kernel(layer, place_ref, *refs):
    (stream_ref, g1_ref, x_ref, qkv_ref, lse_ref, gain_ref, p0, p1, p2, p3, *outs) = refs
    if layer == 1:
        side_ref, *outs = outs
        pieces, outs = outs[:4], outs[4:]
        sums_ref, scratch, out_scratch, acc = outs
        rows = slice(None)
    else:
        (
            normed_ref, part_ref, final_ref, sums_ref, leaving_ref, staying_ref,
            scratch, out_scratch, acc, side_ref, all_normed, all_parts, all_g1,
        ) = outs
        rows = step_rows()
        all_normed[rows, :] = normed_ref[...]
        all_g1[rows, :] = g1_ref[...]
        for k in range(4):
            all_parts[k, rows, :] = part_ref[k]
    width = stream_ref.shape[1]
    share = width // 4

    @pl.when(pl.program_id(0) == 0)
    def _():
        assemble_qkv((p0, p1, p2, p3), scratch)
        assemble_out((p0, p1, p2, p3), out_scratch)

    grad_att = dot_nt(g1_ref[...], out_scratch[...]).astype(bf16)
    allowed = allowed_of(place_ref) if layer == 1 else None
    parts = attend_back_core(qkv_ref[...], grad_att, lse_ref, allowed)
    for k in range(4):
        for j in range(3):
            side_ref[k, rows, j * share : (j + 1) * share] = parts[j][:, k * share : (k + 1) * share]
    joined = jnp.concatenate(parts, axis=1)
    grad_normed = dot(joined, scratch[...])
    inner, scaled = norm_back(x_ref[...].astype(f32), gain_ref[layer, 0:1], grad_normed)
    gather_sums(acc, [parts[0].astype(f32), parts[2].astype(f32), scaled, grad_normed])
    stream = stream_ref[...] + inner
    if layer == 1:
        for k in range(4):
            pieces[k][...] = (
                stream[k * BAND : (k + 1) * BAND].astype(bf16).reshape(4, 1, CELL, width)
            )
    else:
        shuffle = shuffle_of(place_ref, 1)
        high = stream.astype(bf16)
        low = (stream - high.astype(f32)).astype(bf16)
        final_ref[...] = dot(shuffle, high) + dot(shuffle, low)

    @pl.when(last_step())
    def _():
        total = jnp.sum(acc[...], axis=0, keepdims=True)
        sums_ref[...] = jnp.zeros(sums_ref.shape, f32)
        for k in range(4):
            query = total[:, k * share : (k + 1) * share]
            value = total[:, width + k * share : width + (k + 1) * share]
            sums_ref[pl.ds(place_ref[0] ^ k, 1), : 2 * share] = jnp.concatenate([query, value], axis=1)
        sums_ref[4:5, :] = total[:, 2 * width : 3 * width]
        sums_ref[5:6, :] = total[:, 3 * width :]
        if layer == 0:

            def gradient_of(k):
                upper = dot_tn(side_ref[k], all_normed[...])
                lower = dot_tn(all_parts[k], all_g1[...])
                return jnp.concatenate([upper, lower], axis=0)

            put_parts(leaving_ref, staying_ref, gradient_of)


def attend_back(layer, place, stream, g1, x, qkv, lse, gain, packs, normed, attended):
    rows, width = stream.shape
    share = width // 4
    operands = [
        (stream, rows_of(width)),
        (g1, rows_of(width)),
        (x, rows_of(width)),
        (qkv, rows_of(3 * width)),
        (lse, rows_of(WINDOW, LSE_ROWS)),
    ] + [(a, whole(a)) for a in (gain, *packs)]
    sums = [((8, width), f32, sums_of(width))]
    scratch = [
        pltpu.VMEM((3 * width, width), bf16), pltpu.VMEM((width, width), bf16), pltpu.VMEM((8, 4 * width), f32)
    ]
    if layer == 1:
        outs = [((4, rows, 3 * share), bf16, parts_of(3 * share))]
        outs = outs + [((4, 4, CELL, width), bf16, tube_of(width))] * 4 + sums
    else:
        operands += [(normed, rows_of(width)), (attended, parts_of(share))]
        outs = [((rows, width), f32, rows_of(width))] + sums + parts_outs(width)
        scratch += [
            pltpu.VMEM((4, rows, 3 * share), bf16), pltpu.VMEM((rows, width), bf16),
            pltpu.VMEM((4, rows, share), bf16), pltpu.VMEM((rows, width), bf16),
        ]
    return call(partial(attend_back_kernel, layer), "attend_back", place, 4, operands, outs, scratch)


def feed_kernel(layer, place_ref, *refs):
    (
        x_ref, att_ref, a0, a1, a2, a3, vec_ref, gain_ref, shift_ref, s0, s1, s2, s3,
        u0, u1, u2, u3, d0, d1, d2, d3, stream_ref, normed_ref, active_ref, slope_ref, *outs
    ) = refs
    ups, downs = (u0, u1, u2, u3), (d0, d1, d2, d3)
    *pieces, scratch = outs
    width = x_ref.shape[1]

    @pl.when(pl.program_id(0) == 0)
    def _():
        share = width // 4
        for k, part in enumerate((a0, a1, a2, a3)):
            scratch[k * share : (k + 1) * share, :] = part[...]

    stream = x_ref[...].astype(f32) + dot(att_ref[...], scratch[...]) + vec_ref[layer, 0:1]
    stream_ref[...] = stream
    normal, _ = statistics(stream)
    normed = (normal * gain_ref[layer, 1:2] + shift_ref[layer, 1:2]).astype(bf16)
    normed_ref[...] = normed
    total = stream + vec_ref[layer, 1:2]
    units = u0.shape[1]
    ahead = dot(normed, ups[0][...])
    for k in range(4):
        hidden = ahead
        if k < 3:
            ahead = dot(normed, ups[k + 1][...])
        cut = slice(k * units, (k + 1) * units)
        active, slope = gelu_both(hidden + (s0, s1, s2, s3)[k][layer : layer + 1, :])
        active_ref[:, cut] = active
        slope_ref[:, cut] = slope
        total = total + dot(active, downs[k][...])
    total = total.astype(bf16)
    if layer == 0:
        for k in range(4):
            pieces[k][...] = total[k * BAND : (k + 1) * BAND].reshape(1, BAND, width)
    else:
        pieces[0][...] = total


def feed_specs(layer, packs):
    ups, downs, ups_across, downs_across = packs

    def of_layer(a):
        return (a, pl.BlockSpec((None, *a.shape[1:]), lambda i, s: (layer, 0, 0)))

    return [
        *[of_layer(a) for a in ups],
        *[(a, whole(a)) for a in ups_across],
        *[of_layer(a) for a in downs],
        *[(a, whole(a)) for a in downs_across],
    ]


def feed(layer, place, x, att, attn_packs, vecs, gain, shift, smalls, packs):
    rows, width = x.shape
    units = packs[0][0].shape[2]
    last = pl.BlockSpec((width // 4, width), lambda i, s: (3, 0))
    operands = (
        [(x, rows_of(width)), (att, rows_of(width))]
        + [(a, last) for a in attn_packs]
        + [(a, whole(a)) for a in (vecs, gain, shift, *smalls)]
        + feed_specs(layer, packs)
    )
    outs = [
        ((rows, width), f32, rows_of(width)),
        ((rows, width), bf16, rows_of(width)),
        ((rows, 4 * units), bf16, rows_of(4 * units)),
        ((rows, 4 * units), bf16, rows_of(4 * units)),
    ]
    if layer == 0:
        piece = pl.BlockSpec((1, BAND, width), lambda i, s: (i, 0, 0))
        outs = outs + [((4, BAND, width), bf16, piece)] * 4
    else:
        outs = outs + [((rows, width), bf16, rows_of(width))]
    return call(
        partial(feed_kernel, layer), "feed", place, 4, operands, outs,
        [pltpu.VMEM((width, width), bf16)],
    )


def loss_kernel(
    place_ref, final_ref, head_ref, m0, m1, m2, m3, active_ref, grad_ref, loss_ref, leaving_ref, staying_ref,
    acc, all_active, all_g2,
):
    logits = dot(final_ref[...], head_ref[...])
    spread = jnp.concatenate(
        [jnp.broadcast_to(m[f : f + 1, :], (CELL, BAND)) for m in (m0, m1, m2, m3) for f in range(4)],
        axis=0,
    )
    position = lax.broadcasted_iota(jnp.int32, (WINDOW, BAND), 0)
    lane = lax.broadcasted_iota(jnp.int32, (WINDOW, BAND), 1)
    mine = lane == pl.program_id(0) * CELL + (position & (CELL - 1))
    mark = jnp.sum(jnp.where(mine, spread, 0.0), axis=1, keepdims=True).astype(jnp.int32)
    place_of = lax.broadcasted_iota(jnp.int32, (WINDOW, 1), 0)
    frame = 4 * ((place_of >> 6) ^ place_ref[0]) + ((place_of >> 4) & 3)
    weight = jnp.where(frame < place_ref[1], (mark & 1).astype(f32), 0.0)
    top = jnp.max(logits, axis=1, keepdims=True)
    terms = jnp.exp(logits - top)
    total = jnp.sum(terms, axis=1, keepdims=True)
    code = lax.broadcasted_iota(jnp.int32, logits.shape, 1)
    chosen = code == (mark >> 1)
    picked = jnp.sum(jnp.where(chosen, logits, 0.0), axis=1, keepdims=True)
    entry = weight * (top + jnp.log(total) - picked)
    soft = terms * (1.0 / total)
    grad_logits = (weight * (soft - jnp.where(chosen, 1.0, 0.0))).astype(bf16)
    grad = dot_nt(grad_logits, head_ref[...])
    grad_ref[...] = grad
    all_g2[step_rows(), :] = grad.astype(bf16)
    all_active[step_rows(), :] = active_ref[...]
    gather_sums(acc, [jnp.broadcast_to(entry, (WINDOW, PAIR))])

    @pl.when(last_step())
    def _():
        total = jnp.sum(acc[...], axis=0, keepdims=True)
        loss_ref[...] = jnp.broadcast_to(total[:, :1], loss_ref.shape)
        width = grad_ref.shape[1]
        put_parts(
            leaving_ref, staying_ref,
            lambda k: dot_tn(all_active[:, k * width : (k + 1) * width], all_g2[...]),
        )


def code_loss(place, final, code_head, marks, active):
    rows, width = final.shape
    operands = [(final, rows_of(width))] + [(a, whole(a)) for a in (code_head, *marks)]
    operands += [(active, rows_of(active.shape[1]))]
    outs = [
        ((rows, width), f32, rows_of(width)),
        ((8, width), f32, sums_of(width)),
    ] + parts_outs(width)
    scratch = [
        pltpu.VMEM((8, PAIR), f32), pltpu.VMEM(active.shape, bf16), pltpu.VMEM((rows, width), bf16)
    ]
    return call(loss_kernel, "code_loss", place, 4, operands, outs, scratch)


def feed_back_kernel(layer, place_ref, *refs):
    if layer == 1:
        grad_ref, *refs = refs
        grad = grad_ref[...]
    else:
        grad_ref, *refs = refs
        grad = grad_ref[...].astype(f32)
    (
        slope_ref, stream_ref, normed_ref, gain_ref, u0, u1, u2, u3, d0, d1, d2, d3, next_ref, g1_ref,
        sums_ref, leaving_ref, staying_ref, acc, all_hidden, all_normed,
    ) = refs
    all_normed[step_rows(), :] = normed_ref[...]
    g2 = grad.astype(bf16)
    units = u0.shape[1]
    grad_normed = jnp.zeros(grad.shape, f32)
    sums = []
    ups, downs = (u0, u1, u2, u3), (d0, d1, d2, d3)
    ahead = dot_nt(g2, downs[0][...])
    for k in range(4):
        grad_active = ahead
        if k < 3:
            ahead = dot_nt(g2, downs[k + 1][...])
        cut = slice(k * units, (k + 1) * units)
        grad_hidden = (grad_active * slope_ref[:, cut].astype(f32)).astype(bf16)
        all_hidden[step_rows(), cut] = grad_hidden
        sums.append(grad_hidden.astype(f32))
        grad_normed = grad_normed + dot_nt(grad_hidden, ups[k][...])
    inner, scaled = norm_back(stream_ref[...], gain_ref[layer, 1:2], grad_normed)
    grad = grad + inner
    next_ref[...] = grad
    g1 = grad.astype(bf16)
    g1_ref[...] = g1
    gather_sums(acc, sums + [scaled, grad_normed, g2.astype(f32), g1.astype(f32)])

    @pl.when(last_step())
    def _():
        total = jnp.sum(acc[...], axis=0, keepdims=True)
        for k in range(4):
            sums_ref[pl.ds(place_ref[0] ^ k, 1), :] = total[:, k * units : (k + 1) * units]
            start = 4 * units + k * grad.shape[1]
            sums_ref[4 + k : 5 + k, :] = total[:, start : start + grad.shape[1]]
        put_parts(
            leaving_ref, staying_ref,
            lambda k: dot_tn(all_normed[...], all_hidden[:, k * units : (k + 1) * units]),
        )


def feed_back(layer, place, grad, slope, stream, normed, gain, packs):
    rows, width = stream.shape
    units = packs[0][0].shape[2]
    operands = (
        [(grad, rows_of(width)), (slope, rows_of(4 * units)), (stream, rows_of(width)), (normed, rows_of(width))]
        + [(gain, whole(gain))]
        + feed_specs(layer, packs)
    )
    outs = [
        ((rows, width), f32, rows_of(width)),
        ((rows, width), bf16, rows_of(width)),
        ((8, width), f32, sums_of(width)),
    ] + parts_outs(width)
    scratch = [
        pltpu.VMEM((8, 4 * units + 4 * width), f32),
        pltpu.VMEM((rows, 4 * units), bf16),
        pltpu.VMEM((rows, width), bf16),
    ]
    return call(partial(feed_back_kernel, layer), "feed_back", place, 4, operands, outs, scratch)


def grad_kernel(kind, place_ref, *refs):
    *inputs, leaving_ref, staying_ref = refs
    if kind == "attn":
        side_ref, normed_ref, part_ref, g1_ref = inputs
        upper = dot_tn(side_ref[...], normed_ref[...])
        lower = dot_tn(part_ref[...], g1_ref[...])
        value = jnp.concatenate([upper, lower], axis=0)
    else:
        left_ref, right_ref = inputs
        value = dot_tn(left_ref[...], right_ref[...])
    value = value.astype(bf16)
    step = pl.program_id(0)

    @pl.when(step < 2)
    def _():
        leaving_ref[...] = value

    @pl.when(step >= 2)
    def _():
        staying_ref[...] = value


def grads(kind, place, arrays, width):
    rows = arrays[1].shape[0]

    def part_at(i):
        return jnp.where(i < 2, 2 * i + 1, 2 * i - 4)

    part = pl.BlockSpec((rows, width), lambda i, s: (0, part_at(i)))

    def of_part(a):
        return pl.BlockSpec((None, *a.shape[1:]), lambda i, s: (part_at(i), 0, 0))

    if kind == "attn":
        side, normed, attended, g1 = arrays
        specs = [of_part(side), whole(normed), of_part(attended), whole(g1)]
    elif kind == "up":
        specs = [whole(arrays[0]), part]
    else:
        specs = [part, whole(arrays[1])]
    block = (None, width, width)
    outs = [
        ((2, width, width), bf16, pl.BlockSpec(block, lambda i, s: (jnp.minimum(i, 1), 0, 0))),
        ((2, width, width), bf16, pl.BlockSpec(block, lambda i, s: (jnp.maximum(i - 2, 0), 0, 0))),
    ]
    return call(
        partial(grad_kernel, kind), "grads_" + kind, place, 4, list(zip(arrays, specs)), outs
    )


def emit_kernel(attention, aliased, place_ref, mine_ref, other_ref, *refs):
    outs = refs[aliased:]
    half, width = mine_ref.shape
    upper = place_ref[2] == 1
    mine, other = mine_ref[...].astype(f32), other_ref[...].astype(f32)
    low, high = jnp.where(upper, other, mine), jnp.where(upper, mine, other)
    if attention:
        qkv_ref, out_ref = outs
        share = width // 4
        qkv_ref[0, 0], qkv_ref[0, 1] = low[:share], low[share:]
        qkv_ref[0, 2], out_ref[0] = high[:share], high[share:]
    else:
        outs[0][0, :half] = low
        outs[0][0, half:] = high


def emit(place, layer, attention, summed, earlier):
    width = summed[0].shape[1]
    share = width // 4
    if attention:
        outs = [
            ((2, 3, share, width), f32, pl.BlockSpec((1, 3, share, width), lambda i, s: (layer, 0, 0, 0))),
            ((2, share, width), f32, pl.BlockSpec((1, share, width), lambda i, s: (layer, 0, 0))),
        ]
    else:
        outs = [((2, width, width), f32, pl.BlockSpec((1, width, width), lambda i, s: (layer, 0, 0)))]
    operands = [(a, whole(a)) for a in summed]
    aliases = {}
    if earlier is not None:
        aliases = {3 + n: n for n in range(len(earlier))}
        operands += [(e, pl.BlockSpec(memory_space=pl.ANY)) for e in earlier]
    return call(
        partial(emit_kernel, attention, len(aliases)), "emit", place, 1, operands, outs, aliases=aliases
    )


def head_swap(values, distance):
    count = lax.axis_size("head")
    return lax.ppermute(values, "head", [(i, i ^ distance) for i in range(count)])


def clip_swap(values, distance):
    count = lax.axis_size("clip")
    return lax.ppermute(values, "clip", [(i, i ^ distance) for i in range(count)])


class Order:
    def __init__(self):
        self.last = ()
        self.pending = []

    def run(self, step, *values):
        values, _ = lax.optimization_barrier((values, self.last))
        out = step(*values)
        self.last = (jax.tree.leaves(out)[0],)
        return out

    def send(self, swap, values, distance):
        values, _ = lax.optimization_barrier((values, self.last))
        out = swap(values, distance)
        self.pending.append(out)
        return out

    def close(self):
        self.last = self.last + tuple(self.pending)
        self.pending = []


def split_halves(total, upper):
    half = total.shape[0] // 2
    low, high = total[:half], total[half:]
    return jnp.where(upper, low, high).astype(bf16), jnp.where(upper, high, low).astype(bf16)


def join_halves(mine, other, upper):
    return jnp.concatenate(
        [jnp.where(upper, other, mine), jnp.where(upper, mine, other)], axis=0
    )


class Pack:
    def __init__(self, order, leaving, staying):
        self.order = order
        self.out, self.kept = leaving, staying
        levels = lax.axis_size("clip").bit_length() - 1
        clip = lax.axis_index("clip")
        self.uppers = [((clip >> n) & 1) == 1 for n in range(levels)]
        down = [("halve", n) for n in range(levels - 1)]
        up = [("join", n) for n in reversed(range(levels - 1))]
        self.stages = ["core", "across"] + down + [("all", levels - 1)] + up
        self.at = 0

    def total(self):
        if self.at == 2:
            return (self.kept[0].astype(f32) + self.near[0].astype(f32)) + self.moved.astype(f32)
        return self.sum.astype(f32) + self.moved.astype(f32)

    def prepare(self):
        stage = self.stages[self.at]
        run = self.order.run
        if stage == "core":
            self.leaving = self.out
        elif stage == "across":
            self.leaving = run(
                lambda kept, near: (kept[1].astype(f32) + near[1].astype(f32)).astype(bf16),
                self.kept, self.near,
            )
        else:
            kind, level = stage
            upper = self.uppers[level]
            if self.at == 2:
                start = lambda kept, near, moved: (
                    kept[0].astype(f32) + near[0].astype(f32) + moved.astype(f32)
                )
                values = (self.kept, self.near, self.moved)
            else:
                start = lambda total, moved: total.astype(f32) + moved.astype(f32)
                values = (self.sum, self.moved)
            if kind == "halve":
                self.leaving, self.sum = run(lambda *v: split_halves(start(*v), upper), *values)
            elif kind == "all" or self.stages[self.at - 1][0] == "all":
                self.leaving = self.sum = run(lambda *v: start(*v).astype(bf16), *values)
            else:
                before = self.uppers[self.stages[self.at - 1][1]]
                self.leaving = self.sum = run(
                    lambda mine, other: join_halves(mine, other, before), self.sum, self.moved
                )

    def launch(self):
        stage = self.stages[self.at]
        send = self.order.send
        if stage == "core":
            self.near = send(head_swap, self.leaving, 1)
        elif stage == "across":
            self.moved = send(head_swap, self.leaving, 2)
        else:
            self.moved = send(clip_swap, self.leaving, 1 << stage[1])
        self.at += 1

    def done(self):
        return self.at == len(self.stages)

    def whole(self):
        assert self.done()
        return self.sum, self.moved


def on_device(
    tokens,
    frame_counts,
    token_mask,
    targets,
    norm_gain,
    norm_bias,
    w_qkv,
    qv_bias,
    w_out,
    vec_bias,
    w_up,
    up_bias,
    w_down,
    code_head,
):
    head_index = lax.axis_index("head")
    width = tokens.shape[1]
    share = w_out.shape[1]
    upper = lax.axis_index("clip") & 1
    place = jnp.stack(
        [head_index.astype(jnp.int32), frame_counts[0], upper.astype(jnp.int32)]
    )
    order = Order()

    def tied(values, *after):
        return lax.optimization_barrier((values, after))[0]

    clip_count = lax.axis_size("clip")
    own_small = jnp.concatenate([up_bias, qv_bias.reshape(1, width)], axis=0)
    clip_index = lax.axis_index("clip")

    def chunk(matrix):
        piece = matrix.shape[0] // clip_count
        return lax.dynamic_slice_in_dim(matrix, clip_index * piece, piece, 0)

    def over_clips(chunk_across):
        return lax.all_gather(chunk_across, "clip", axis=0, tiled=True)

    y_place, z_place = clip_index & 1, (clip_index >> 1) & 1

    def quarter(matrix):
        rows = matrix.shape[0] // 4
        return lax.dynamic_slice_in_dim(matrix, (2 * y_place + z_place) * rows, rows, 0)

    def over_neighbours(first):
        second = clip_swap(first, 1)
        others = clip_swap(jnp.concatenate([first, second], axis=0), 2)
        rows = first.shape[0]
        pieces = []
        for y in range(2):
            for z in range(2):
                same = z_place == z
                mine = jnp.where(same, first, others[:rows])
                next_one = jnp.where(same, second, others[rows:])
                pieces.append(jnp.where(y_place == y, mine, next_one))
        return jnp.concatenate(pieces, axis=0)

    def attn_pack(layer):
        transposed = w_qkv[layer].swapaxes(1, 2).reshape(-1, width)
        return jnp.concatenate([transposed, w_out[layer]], axis=0)

    def spread(own, across):
        return [own, head_swap(own, 1), across, head_swap(across, 1)]

    chunk_0 = head_swap(quarter(w_up[0]), 2)
    smalls = spread(own_small, head_swap(own_small, 2))
    own = tied(attn_pack(0), chunk_0, smalls[2])
    later = jnp.concatenate([chunk(w_up[1]), chunk(w_down[1])], axis=0)
    marks = (2 * targets + token_mask).astype(f32).reshape(-1, 1)
    across, first_down, later, marks, place, up_across = lax.optimization_barrier(
        (head_swap(own, 2), w_down[0], later, marks, place, over_neighbours(chunk_0))
    )
    attn = [spread(own, across), None]
    order.last = (attn[0][2],)
    down_across = order.send(head_swap, first_down, 2)
    order.last = (smalls[1], smalls[3], attn[0][1], attn[0][3])
    ups = [w_up, order.send(head_swap, w_up, 1)]
    downs = [w_down, order.send(head_swap, w_down, 1)]
    up_diagonal = order.send(head_swap, up_across, 1)
    packs = [None, None]

    kept = []
    inputs = (tokens, marks)
    for layer in range(2):
        x, normed, qkv, att, lse, att_parts, *mark_pieces = order.run(
            lambda *a: attend(layer, place, a, norm_gain, norm_bias, smalls, attn[layer]), *inputs
        )
        order.close()
        if layer == 0:
            marks = [mark_pieces[0]] + [head_swap(mark_pieces[k], k) for k in (1, 2, 3)]
            chunk_1 = order.send(head_swap, later, 2)
            up_x, down_x = up_across, down_across
            up_pair = [up_x, up_diagonal]
        else:
            pieces = gathered.reshape(clip_count, 2, -1, width)
            up_x, down_x = tied((pieces[:, 0].reshape(-1, width), pieces[:, 1].reshape(-1, width)), x)
            up_pair = [up_x, order.send(head_swap, up_x, 1)]
        packs[layer] = (
            ups, downs,
            up_pair,
            [down_x, order.send(head_swap, down_x, 1)],
        )
        order.close()
        if layer == 0:
            gathered = over_clips(tied(chunk_1, up_across))
            own = attn_pack(1)
            attn_across = order.send(head_swap, own, 2)
            attn[1] = [own, head_swap(own, 1), attn_across]
        stream, normed2, active, slope, *outs = order.run(
            lambda a, b: feed(
                layer, place, a, b, attn[layer], vec_bias, norm_gain, norm_bias, smalls, packs[layer]
            ),
            x, att,
        )
        kept.append((x, normed, qkv, att_parts, lse, stream, normed2, active, slope))
        if layer == 0:
            order.close()
            attn[1].append(order.send(head_swap, attn_across, 1))
            inputs = [outs[0]] + [order.send(head_swap, outs[k], k) for k in (1, 2, 3)]
            inputs = [p.reshape(4, 4, CELL, width) for p in inputs]
            order.close()
    grad, loss_sum, *parts = order.run(
        lambda a: code_loss(place, a, code_head, marks, active), outs[0]
    )
    down_1 = Pack(order, *parts)

    def run_feed_back(layer, grad):
        x, normed, qkv, att, lse, stream, normed2, active, slope = kept[layer]
        return order.run(
            lambda a: feed_back(layer, place, a, slope, stream, normed2, norm_gain, packs[layer]), grad
        )

    def run_attend_back(layer, grad_next, g1):
        x, normed, qkv, att, lse, *_ = kept[layer]
        return order.run(
            lambda a, b: attend_back(
                layer, place, a, b, x, qkv, lse, norm_gain, attn[layer], normed, att
            ),
            grad_next, g1,
        )

    def pack(kind, *arrays):
        return Pack(order, *order.run(lambda *a: grads(kind, place, a, width), *arrays))

    def move(*ones):
        for one in ones:
            one.prepare()
        for one in ones:
            one.launch()

    move(down_1)
    order.close()
    move(down_1)
    grad_next, g1, feed_sum_1, *parts = run_feed_back(1, grad)
    up_1 = Pack(order, *parts)
    order.close()
    move(up_1)
    order.close()
    move(up_1, down_1)
    side, *outs, attn_sum_1 = run_attend_back(1, grad_next, g1)
    order.close()

    grad = [outs[0]] + [order.send(head_swap, outs[k], k) for k in (1, 2, 3)]
    grad = [p.reshape(4, BAND, width) for p in grad]
    move(up_1, down_1)
    attn_1 = pack("attn", side, kept[1][1], kept[1][3], g1)
    order.close()

    move(attn_1, up_1)
    g2 = jnp.stack(grad, axis=1).reshape(-1, width)
    down_0 = pack("down", kept[0][7], g2)
    order.close()
    move(attn_1, down_0, down_1, up_1)
    grad_next, g1, feed_sum_0, *parts = run_feed_back(0, g2)
    up_0 = Pack(order, *parts)
    order.close()
    move(down_0, up_0, attn_1, down_1, up_1)
    grad_input, attn_sum_0, *parts = run_attend_back(0, grad_next, g1)
    attn_0 = Pack(order, *parts)
    order.close()
    move(up_0, attn_0, down_0, attn_1, down_1)
    order.close()
    move(attn_0, up_0, down_0, attn_1, up_1)
    order.close()

    packed = jnp.concatenate([feed_sum_0, feed_sum_1, attn_sum_0, attn_sum_1, loss_sum], axis=0)
    swaps = [(head_swap, 1), (head_swap, 2)]
    swaps += [(clip_swap, 1 << n) for n in range(clip_count.bit_length() - 1)]

    def pack_step():
        swap, distance = swaps.pop(0)
        return packed + order.send(swap, packed, distance)

    early = [(up_1, False), (down_1, False), (attn_1, True)]
    ready = {}
    moving = [attn_0, up_0, down_0, attn_1, up_1, down_1]
    while swaps or not all(one.done() for one in moving):
        move(*[one for one in moving if not one.done()])
        if swaps:
            packed = pack_step()
        if early and early[0][0].done():
            one, attention = early.pop(0)
            ready[one] = order.run(lambda *a: emit(place, 1, attention, a, None), *one.whole())
        order.close()
    for one, attention in early:
        ready[one] = emit(place, 1, attention, one.whole(), None)

    attn_out = emit(place, 0, True, attn_0.whole(), ready[attn_1])
    up_out = emit(place, 0, False, up_0.whole(), ready[up_1])
    down_out = emit(place, 0, False, down_0.whole(), ready[down_1])

    feed_sums = packed[:16].reshape(2, 8, width)
    attn_sums = packed[16:32].reshape(2, 8, width)
    loss_total = packed[32, 0]
    own_feed = lax.dynamic_index_in_dim(feed_sums, head_index, 1, keepdims=False)
    own_attn = lax.dynamic_index_in_dim(attn_sums, head_index, 1, keepdims=False)
    slot_total = clip_count * frame_counts.shape[0] * FRAMES * SIDE * SIDE

    return (
        loss_total / slot_total,
        grad_input,
        jnp.stack([attn_sums[:, 4], feed_sums[:, 4]], axis=1),
        jnp.stack([attn_sums[:, 5], feed_sums[:, 5]], axis=1),
        attn_out[0].swapaxes(2, 3),
        own_attn[:, : 2 * share].reshape(2, 2, share),
        attn_out[1],
        jnp.stack([feed_sums[:, 7], feed_sums[:, 6]], axis=1),
        up_out[0],
        own_feed,
        down_out[0],
    )


def solution(mesh):
    placed = (
        P(("clip", "head"), None),
        P("clip"),
        P(("clip", "head")),
        P(("clip", "head")),
        P(),
        P(),
        P(None, None, None, "head"),
        P(None, None, "head"),
        P(None, "head", None),
        P(),
        P(None, None, "head"),
        P(None, "head"),
        P(None, "head", None),
        P(),
    )
    return jax.shard_map(
        on_device,
        mesh=mesh,
        in_specs=placed,
        out_specs=(
            P(),
            P(("clip", "head"), None),
            P(),
            P(),
            P(None, None, None, "head"),
            P(None, None, "head"),
            P(None, "head", None),
            P(),
            P(None, None, "head"),
            P(None, "head"),
            P(None, "head", None),
        ),
        check_vma=False,
    )
```

```python
from functools import partial

import jax
import jax.numpy as jnp
from jax import lax
from jax.experimental import pallas as pl
from jax.experimental.pallas import tpu as pltpu
from jax.sharding import PartitionSpec as P

HD = 64
FRAMES = 16
SIDE = 16
TUBE = 4
WINDOW = 256
PAIR = 128
BAND = 64
CELL = 16
LSE_ROWS = 16

epsilon = 1e-06
masked_score = -1e30
f32 = jnp.float32
bf16 = jnp.bfloat16
VMEM_LIMIT = 56 * 1024 * 1024
TIMES = {
    "attend": 17, "feed": 23, "code_loss": 10, "feed_back": 21, "attend_back": 25,
    "grads_down": 8, "grads_up": 8, "grads_attn": 8, "emit": 3,
}
SCALE = 0.0001


def cost_of(name):
    time = TIMES[name] * SCALE
    return pl.CostEstimate(flops=int(time * 1.15e9), bytes_accessed=int(time * 3.6e6), transcendentals=0)


def dot(a, b):
    return lax.dot_general(a, b, (((1,), (0,)), ((), ())), preferred_element_type=f32)


def dot_nt(a, b):
    return lax.dot_general(a, b, (((1,), (1,)), ((), ())), preferred_element_type=f32)


def dot_tn(a, b):
    return lax.dot_general(a, b, (((0,), (0,)), ((), ())), preferred_element_type=f32)


def statistics(stream):
    centre = jnp.mean(stream, axis=-1, keepdims=True)
    centred = stream - centre
    spread = jnp.mean(centred * centred, axis=-1, keepdims=True)
    scale = lax.rsqrt(spread + epsilon)
    return centred * scale, scale


def by_eight(values):
    rows, columns = values.shape
    return jnp.sum(values.reshape(rows // 8, 8, columns), axis=0)


def gather_sums(acc_ref, values):
    first = pl.program_id(0) == 0
    parts = jnp.concatenate([by_eight(v) for v in values], axis=1)

    @pl.when(first)
    def _():
        acc_ref[...] = parts

    @pl.when(jnp.logical_not(first))
    def _():
        acc_ref[...] += parts


ORDER = (1, 3, 0, 2)


def step_rows():
    return pl.ds(pl.multiple_of(pl.program_id(0) * WINDOW, WINDOW), WINDOW)


def put_parts(leaving_ref, staying_ref, gradient_of):
    for n, k in enumerate(ORDER):
        (leaving_ref if n < 2 else staying_ref)[n % 2] = gradient_of(k).astype(bf16)


def parts_outs(width):
    spec = pl.BlockSpec((2, width, width), lambda i, s: (0, 0, 0))
    return [((2, width, width), bf16, spec)] * 2


def last_step():
    return pl.program_id(0) == pl.num_programs(0) - 1


def norm_back(stream, gain, grad):
    normal, scale = statistics(stream)
    scaled = grad * gain
    mean_plain = jnp.mean(scaled, axis=-1, keepdims=True)
    mean_normal = jnp.mean(scaled * normal, axis=-1, keepdims=True)
    inner = scale * (scaled - mean_plain - normal * mean_normal)
    return inner, grad * normal


def gelu_both(hidden):
    root = 0.7978845608028654
    cubic = 0.044715
    square = hidden * hidden
    bend = jnp.tanh(hidden * (root + root * cubic * square))
    rise = 0.5 + 0.5 * bend
    active = hidden * rise
    slope = rise + (active - active * rise) * (2.0 * root + 6.0 * root * cubic * square)
    return active.astype(bf16), slope.astype(bf16)


def allowed_of(place_ref):
    head_index = place_ref[0]
    frame_count = place_ref[1]

    def valid(axis):
        position = lax.broadcasted_iota(jnp.int32, (WINDOW, WINDOW), axis)
        frame = 4 * ((position >> 6) ^ head_index) + ((position >> 4) & 3)
        return frame < frame_count

    return jnp.logical_or(valid(0), jnp.logical_not(valid(1)))


def shuffle_of(place_ref, axis):
    arranged = lax.broadcasted_iota(jnp.int32, (WINDOW, WINDOW), axis)
    plain = lax.broadcasted_iota(jnp.int32, (WINDOW, WINDOW), 1 - axis)
    band = (arranged >> 6) ^ place_ref[0]
    source = band * BAND + ((arranged >> 2) & 3) * 16 + ((arranged >> 4) & 3) * 4 + (arranged & 3)
    return (source == plain).astype(f32).astype(bf16)


def assemble_qkv(packs, scratch):
    width = scratch.shape[1]
    share = width // 4
    for k in range(4):
        for j in range(3):
            start = j * width + k * share
            scratch[start : start + share, :] = packs[k][j * share : (j + 1) * share, :]


def assemble_out(packs, scratch):
    share = scratch.shape[0] // 4
    for k in range(4):
        scratch[k * share : (k + 1) * share, :] = packs[k][3 * share :, :]


def stack_heads(pair):
    low = lax.broadcasted_iota(jnp.int32, pair.shape, 1) < HD
    zero = jnp.zeros((), bf16)
    return jnp.concatenate([jnp.where(low, pair, zero), jnp.where(low, zero, pair)], axis=0)


def attend_core(qkv, allowed, att_ref, lse_ref, part_ref):
    width = att_ref.shape[1]
    pairs = width // PAIR

    def part(j, pair):
        return qkv[:, j * width + pair * PAIR : j * width + (pair + 1) * PAIR]

    def scores_of(pair):
        query = part(0, pair) * jnp.asarray(HD ** (-0.5), bf16)
        return dot_nt(stack_heads(part(1, pair)), query)

    ahead = scores_of(0)
    for pair in range(pairs):
        scores = ahead
        if pair + 1 < pairs:
            ahead = scores_of(pair + 1)
        probs = []
        for half in range(2):
            mine = scores[half * WINDOW : (half + 1) * WINDOW]
            if allowed is not None:
                mine = jnp.where(allowed, mine, masked_score)
            top = jnp.max(mine, axis=0, keepdims=True)
            terms = jnp.exp(mine - top)
            total = jnp.sum(terms, axis=0, keepdims=True)
            probs.append((terms * (1.0 / total)).astype(bf16))
            head = 2 * pair + half
            lse_ref[head : head + 1, :] = top + jnp.log(total)
        out = dot_tn(jnp.concatenate(probs, axis=0), stack_heads(part(2, pair)))
        att_ref[:, pair * PAIR : (pair + 1) * PAIR] = out.astype(bf16)
    share = width // 4
    for k in range(4):
        part_ref[k] = att_ref[:, k * share : (k + 1) * share]


def attend_kernel(layer, place_ref, *refs):
    if layer == 0:
        tokens_ref, marks_ref, *refs = refs
        shuffle = shuffle_of(place_ref, 0)
        stream = dot(shuffle, tokens_ref[...])
    else:
        pieces, refs = refs[:4], refs[4:]
        stream = jnp.concatenate(
            [p[...].reshape(BAND, p.shape[-1]) for p in pieces], axis=0
        ).astype(f32)
    gain_ref, shift_ref, s0, s1, s2, s3, p0, p1, p2, p3, x_ref, normed_ref, qkv_ref, att_ref, lse_ref, part_ref, *refs = refs
    *mark_refs, scratch = refs
    share = scratch.shape[1] // 4

    @pl.when(pl.program_id(0) == 0)
    def _():
        assemble_qkv((p0, p1, p2, p3), scratch)

    if layer == 0:
        chosen = shuffle_of(place_ref, 1).astype(f32)
        marks = jnp.sum(chosen * marks_ref[...], axis=0, keepdims=True)
        for k in range(4):
            mark_refs[k][pl.ds(pl.program_id(0), 1), :] = marks[:, k * BAND : (k + 1) * BAND]
    x_ref[...] = stream.astype(bf16)
    normal, _ = statistics(stream)
    normed = (normal * gain_ref[layer, 0:1] + shift_ref[layer, 0:1]).astype(bf16)
    normed_ref[...] = normed
    start = 2 * layer * share
    smalls = (s0, s1, s2, s3)
    bias = jnp.concatenate(
        [r[2:3, start : start + share] for r in smalls]
        + [jnp.zeros((1, 4 * share), f32)]
        + [r[2:3, start + share : start + 2 * share] for r in smalls],
        axis=1,
    )
    qkv = (dot_nt(normed, scratch[...]) + bias).astype(bf16)
    qkv_ref[...] = qkv
    allowed = allowed_of(place_ref) if layer == 1 else None
    attend_core(qkv, allowed, att_ref, lse_ref, part_ref)


def whole(array):
    zeros = (0,) * array.ndim
    return pl.BlockSpec(array.shape, lambda i, s: zeros)


def rows_of(columns, rows=WINDOW):
    return pl.BlockSpec((rows, columns), lambda i, s: (i, 0))


def parts_of(columns):
    return pl.BlockSpec((4, WINDOW, columns), lambda i, s: (0, i, 0))


def tube_of(columns):
    return pl.BlockSpec((4, 1, CELL, columns), lambda i, s: (0, i, 0, 0))


def sums_of(columns):
    return pl.BlockSpec((8, columns), lambda i, s: (0, 0))


def call(kernel, name, place, steps, operands, outs, scratch=(), aliases={}):
    return pl.pallas_call(
        kernel,
        grid_spec=pltpu.PrefetchScalarGridSpec(
            num_scalar_prefetch=1,
            grid=(steps,),
            in_specs=[spec for _, spec in operands],
            out_specs=[spec for _, _, spec in outs],
            scratch_shapes=list(scratch),
        ),
        out_shape=[jax.ShapeDtypeStruct(shape, dtype) for shape, dtype, _ in outs],
        compiler_params=pltpu.CompilerParams(vmem_limit_bytes=VMEM_LIMIT),
        cost_estimate=cost_of(name),
        input_output_aliases=aliases,
        name=name,
    )(place, *[array for array, _ in operands])


def attend(layer, place, inputs, gain, shift, smalls, packs):
    width = gain.shape[-1]
    rows = 4 * WINDOW
    if layer == 0:
        tokens, marks = inputs
        first = [(tokens, rows_of(width)), (marks, rows_of(1))]
    else:
        first = [(p, tube_of(width)) for p in inputs]
    operands = first + [(a, whole(a)) for a in (gain, shift, *smalls, *packs)]
    outs = [
        ((rows, width), bf16, rows_of(width)),
        ((rows, width), bf16, rows_of(width)),
        ((rows, 3 * width), bf16, rows_of(3 * width)),
        ((rows, width), bf16, rows_of(width)),
        ((4 * LSE_ROWS, WINDOW), f32, rows_of(WINDOW, LSE_ROWS)),
        ((4, rows, width // 4), bf16, parts_of(width // 4)),
    ]
    if layer == 0:
        outs += [((4, BAND), f32, pl.BlockSpec((4, BAND), lambda i, s: (0, 0)))] * 4
    return call(
        partial(attend_kernel, layer), "attend", place, 4, operands, outs,
        [pltpu.VMEM((3 * width, width), bf16)],
    )


def attend_back_core(qkv, grad, lse_ref, allowed):
    width = grad.shape[1]
    pairs = width // PAIR

    def part(j, pair):
        return qkv[:, j * width + pair * PAIR : j * width + (pair + 1) * PAIR]

    def first_of(pair):
        query = part(0, pair) * jnp.asarray(HD ** (-0.5), bf16)
        grad_part = grad[:, pair * PAIR : (pair + 1) * PAIR]
        keys = stack_heads(part(1, pair))
        scores = dot_nt(keys, query)
        grad_probs = dot_nt(stack_heads(part(2, pair)), grad_part)
        return query, grad_part, keys, scores, grad_probs

    low = lax.broadcasted_iota(jnp.int32, (WINDOW, PAIR), 1) < HD
    results = [[], [], []]
    ahead = first_of(0)
    for pair in range(pairs):
        query, grad_part, keys, scores, grad_probs = ahead
        if pair + 1 < pairs:
            ahead = first_of(pair + 1)
        all_probs, all_scores = [], []
        for half in range(2):
            rows = slice(half * WINDOW, (half + 1) * WINDOW)
            mine = scores[rows]
            if allowed is not None:
                mine = jnp.where(allowed, mine, masked_score)
            head = 2 * pair + half
            probs = jnp.exp(mine - lse_ref[head : head + 1, :])
            grad_mine = grad_probs[rows]
            delta = jnp.sum(probs * grad_mine, axis=0, keepdims=True)
            all_probs.append(probs.astype(bf16))
            all_scores.append((probs * (grad_mine - delta)).astype(bf16))
        probs = jnp.concatenate(all_probs, axis=0)
        grad_scores = jnp.concatenate(all_scores, axis=0)
        grad_query = dot_tn(grad_scores, keys) * HD ** (-0.5)
        grad_key = dot(grad_scores, query)
        grad_value = dot(probs, grad_part)
        results[0].append(grad_query.astype(bf16))
        results[1].append(jnp.where(low, grad_key[:WINDOW], grad_key[WINDOW:]).astype(bf16))
        results[2].append(jnp.where(low, grad_value[:WINDOW], grad_value[WINDOW:]).astype(bf16))
    return [jnp.concatenate(part, axis=1) for part in results]


def attend_back_kernel(layer, place_ref, *refs):
    (stream_ref, g1_ref, x_ref, qkv_ref, lse_ref, gain_ref, p0, p1, p2, p3, *outs) = refs
    if layer == 1:
        side_ref, *outs = outs
        pieces, outs = outs[:4], outs[4:]
        sums_ref, scratch, out_scratch, acc = outs
        rows = slice(None)
    else:
        (
            normed_ref, part_ref, final_ref, sums_ref, leaving_ref, staying_ref,
            scratch, out_scratch, acc, side_ref, all_normed, all_parts, all_g1,
        ) = outs
        rows = step_rows()
        all_normed[rows, :] = normed_ref[...]
        all_g1[rows, :] = g1_ref[...]
        for k in range(4):
            all_parts[k, rows, :] = part_ref[k]
    width = stream_ref.shape[1]
    share = width // 4

    @pl.when(pl.program_id(0) == 0)
    def _():
        assemble_qkv((p0, p1, p2, p3), scratch)
        assemble_out((p0, p1, p2, p3), out_scratch)

    grad_att = dot_nt(g1_ref[...], out_scratch[...]).astype(bf16)
    allowed = allowed_of(place_ref) if layer == 1 else None
    parts = attend_back_core(qkv_ref[...], grad_att, lse_ref, allowed)
    for k in range(4):
        for j in range(3):
            side_ref[k, rows, j * share : (j + 1) * share] = parts[j][:, k * share : (k + 1) * share]
    joined = jnp.concatenate(parts, axis=1)
    grad_normed = dot(joined, scratch[...])
    inner, scaled = norm_back(x_ref[...].astype(f32), gain_ref[layer, 0:1], grad_normed)
    gather_sums(acc, [parts[0].astype(f32), parts[2].astype(f32), scaled, grad_normed])
    stream = stream_ref[...] + inner
    if layer == 1:
        for k in range(4):
            pieces[k][...] = (
                stream[k * BAND : (k + 1) * BAND].astype(bf16).reshape(4, 1, CELL, width)
            )
    else:
        shuffle = shuffle_of(place_ref, 1)
        high = stream.astype(bf16)
        low = (stream - high.astype(f32)).astype(bf16)
        final_ref[...] = dot(shuffle, high) + dot(shuffle, low)

    @pl.when(last_step())
    def _():
        total = jnp.sum(acc[...], axis=0, keepdims=True)
        sums_ref[...] = jnp.zeros(sums_ref.shape, f32)
        for k in range(4):
            query = total[:, k * share : (k + 1) * share]
            value = total[:, width + k * share : width + (k + 1) * share]
            sums_ref[pl.ds(place_ref[0] ^ k, 1), : 2 * share] = jnp.concatenate([query, value], axis=1)
        sums_ref[4:5, :] = total[:, 2 * width : 3 * width]
        sums_ref[5:6, :] = total[:, 3 * width :]
        if layer == 0:

            def gradient_of(k):
                upper = dot_tn(side_ref[k], all_normed[...])
                lower = dot_tn(all_parts[k], all_g1[...])
                return jnp.concatenate([upper, lower], axis=0)

            put_parts(leaving_ref, staying_ref, gradient_of)


def attend_back(layer, place, stream, g1, x, qkv, lse, gain, packs, normed, attended):
    rows, width = stream.shape
    share = width // 4
    operands = [
        (stream, rows_of(width)),
        (g1, rows_of(width)),
        (x, rows_of(width)),
        (qkv, rows_of(3 * width)),
        (lse, rows_of(WINDOW, LSE_ROWS)),
    ] + [(a, whole(a)) for a in (gain, *packs)]
    sums = [((8, width), f32, sums_of(width))]
    scratch = [
        pltpu.VMEM((3 * width, width), bf16), pltpu.VMEM((width, width), bf16), pltpu.VMEM((8, 4 * width), f32)
    ]
    if layer == 1:
        outs = [((4, rows, 3 * share), bf16, parts_of(3 * share))]
        outs = outs + [((4, 4, CELL, width), bf16, tube_of(width))] * 4 + sums
    else:
        operands += [(normed, rows_of(width)), (attended, parts_of(share))]
        outs = [((rows, width), f32, rows_of(width))] + sums + parts_outs(width)
        scratch += [
            pltpu.VMEM((4, rows, 3 * share), bf16), pltpu.VMEM((rows, width), bf16),
            pltpu.VMEM((4, rows, share), bf16), pltpu.VMEM((rows, width), bf16),
        ]
    return call(partial(attend_back_kernel, layer), "attend_back", place, 4, operands, outs, scratch)


def feed_kernel(layer, place_ref, *refs):
    (
        x_ref, att_ref, a0, a1, a2, a3, vec_ref, gain_ref, shift_ref, s0, s1, s2, s3,
        u0, u1, u2, u3, d0, d1, d2, d3, stream_ref, normed_ref, active_ref, slope_ref, *outs
    ) = refs
    ups, downs = (u0, u1, u2, u3), (d0, d1, d2, d3)
    *pieces, scratch = outs
    width = x_ref.shape[1]

    @pl.when(pl.program_id(0) == 0)
    def _():
        share = width // 4
        for k, part in enumerate((a0, a1, a2, a3)):
            scratch[k * share : (k + 1) * share, :] = part[...]

    stream = x_ref[...].astype(f32) + dot(att_ref[...], scratch[...]) + vec_ref[layer, 0:1]
    stream_ref[...] = stream
    normal, _ = statistics(stream)
    normed = (normal * gain_ref[layer, 1:2] + shift_ref[layer, 1:2]).astype(bf16)
    normed_ref[...] = normed
    total = stream + vec_ref[layer, 1:2]
    units = u0.shape[1]
    ahead = dot(normed, ups[0][...])
    for k in range(4):
        hidden = ahead
        if k < 3:
            ahead = dot(normed, ups[k + 1][...])
        cut = slice(k * units, (k + 1) * units)
        active, slope = gelu_both(hidden + (s0, s1, s2, s3)[k][layer : layer + 1, :])
        active_ref[:, cut] = active
        slope_ref[:, cut] = slope
        total = total + dot(active, downs[k][...])
    total = total.astype(bf16)
    if layer == 0:
        for k in range(4):
            pieces[k][...] = total[k * BAND : (k + 1) * BAND].reshape(1, BAND, width)
    else:
        pieces[0][...] = total


def feed_specs(layer, packs):
    ups, downs, ups_across, downs_across = packs

    def of_layer(a):
        return (a, pl.BlockSpec((None, *a.shape[1:]), lambda i, s: (layer, 0, 0)))

    return [
        *[of_layer(a) for a in ups],
        *[(a, whole(a)) for a in ups_across],
        *[of_layer(a) for a in downs],
        *[(a, whole(a)) for a in downs_across],
    ]


def feed(layer, place, x, att, attn_packs, vecs, gain, shift, smalls, packs):
    rows, width = x.shape
    units = packs[0][0].shape[2]
    last = pl.BlockSpec((width // 4, width), lambda i, s: (3, 0))
    operands = (
        [(x, rows_of(width)), (att, rows_of(width))]
        + [(a, last) for a in attn_packs]
        + [(a, whole(a)) for a in (vecs, gain, shift, *smalls)]
        + feed_specs(layer, packs)
    )
    outs = [
        ((rows, width), f32, rows_of(width)),
        ((rows, width), bf16, rows_of(width)),
        ((rows, 4 * units), bf16, rows_of(4 * units)),
        ((rows, 4 * units), bf16, rows_of(4 * units)),
    ]
    if layer == 0:
        piece = pl.BlockSpec((1, BAND, width), lambda i, s: (i, 0, 0))
        outs = outs + [((4, BAND, width), bf16, piece)] * 4
    else:
        outs = outs + [((rows, width), bf16, rows_of(width))]
    return call(
        partial(feed_kernel, layer), "feed", place, 4, operands, outs,
        [pltpu.VMEM((width, width), bf16)],
    )


def loss_kernel(
    place_ref, final_ref, head_ref, m0, m1, m2, m3, active_ref, grad_ref, loss_ref, leaving_ref, staying_ref,
    acc, all_active, all_g2,
):
    logits = dot(final_ref[...], head_ref[...])
    spread = jnp.concatenate(
        [jnp.broadcast_to(m[f : f + 1, :], (CELL, BAND)) for m in (m0, m1, m2, m3) for f in range(4)],
        axis=0,
    )
    position = lax.broadcasted_iota(jnp.int32, (WINDOW, BAND), 0)
    lane = lax.broadcasted_iota(jnp.int32, (WINDOW, BAND), 1)
    mine = lane == pl.program_id(0) * CELL + (position & (CELL - 1))
    mark = jnp.sum(jnp.where(mine, spread, 0.0), axis=1, keepdims=True).astype(jnp.int32)
    place_of = lax.broadcasted_iota(jnp.int32, (WINDOW, 1), 0)
    frame = 4 * ((place_of >> 6) ^ place_ref[0]) + ((place_of >> 4) & 3)
    weight = jnp.where(frame < place_ref[1], (mark & 1).astype(f32), 0.0)
    top = jnp.max(logits, axis=1, keepdims=True)
    terms = jnp.exp(logits - top)
    total = jnp.sum(terms, axis=1, keepdims=True)
    code = lax.broadcasted_iota(jnp.int32, logits.shape, 1)
    chosen = code == (mark >> 1)
    picked = jnp.sum(jnp.where(chosen, logits, 0.0), axis=1, keepdims=True)
    entry = weight * (top + jnp.log(total) - picked)
    soft = terms * (1.0 / total)
    grad_logits = (weight * (soft - jnp.where(chosen, 1.0, 0.0))).astype(bf16)
    grad = dot_nt(grad_logits, head_ref[...])
    grad_ref[...] = grad
    all_g2[step_rows(), :] = grad.astype(bf16)
    all_active[step_rows(), :] = active_ref[...]
    gather_sums(acc, [jnp.broadcast_to(entry, (WINDOW, PAIR))])

    @pl.when(last_step())
    def _():
        total = jnp.sum(acc[...], axis=0, keepdims=True)
        loss_ref[...] = jnp.broadcast_to(total[:, :1], loss_ref.shape)
        width = grad_ref.shape[1]
        put_parts(
            leaving_ref, staying_ref,
            lambda k: dot_tn(all_active[:, k * width : (k + 1) * width], all_g2[...]),
        )


def code_loss(place, final, code_head, marks, active):
    rows, width = final.shape
    operands = [(final, rows_of(width))] + [(a, whole(a)) for a in (code_head, *marks)]
    operands += [(active, rows_of(active.shape[1]))]
    outs = [
        ((rows, width), f32, rows_of(width)),
        ((8, width), f32, sums_of(width)),
    ] + parts_outs(width)
    scratch = [
        pltpu.VMEM((8, PAIR), f32), pltpu.VMEM(active.shape, bf16), pltpu.VMEM((rows, width), bf16)
    ]
    return call(loss_kernel, "code_loss", place, 4, operands, outs, scratch)


def feed_back_kernel(layer, place_ref, *refs):
    if layer == 1:
        grad_ref, *refs = refs
        grad = grad_ref[...]
    else:
        grad_ref, *refs = refs
        grad = grad_ref[...].astype(f32)
    (
        slope_ref, stream_ref, normed_ref, gain_ref, u0, u1, u2, u3, d0, d1, d2, d3, next_ref, g1_ref,
        sums_ref, leaving_ref, staying_ref, acc, all_hidden, all_normed,
    ) = refs
    all_normed[step_rows(), :] = normed_ref[...]
    g2 = grad.astype(bf16)
    units = u0.shape[1]
    grad_normed = jnp.zeros(grad.shape, f32)
    sums = []
    ups, downs = (u0, u1, u2, u3), (d0, d1, d2, d3)
    ahead = dot_nt(g2, downs[0][...])
    for k in range(4):
        grad_active = ahead
        if k < 3:
            ahead = dot_nt(g2, downs[k + 1][...])
        cut = slice(k * units, (k + 1) * units)
        grad_hidden = (grad_active * slope_ref[:, cut].astype(f32)).astype(bf16)
        all_hidden[step_rows(), cut] = grad_hidden
        sums.append(grad_hidden.astype(f32))
        grad_normed = grad_normed + dot_nt(grad_hidden, ups[k][...])
    inner, scaled = norm_back(stream_ref[...], gain_ref[layer, 1:2], grad_normed)
    grad = grad + inner
    next_ref[...] = grad
    g1 = grad.astype(bf16)
    g1_ref[...] = g1
    gather_sums(acc, sums + [scaled, grad_normed, g2.astype(f32), g1.astype(f32)])

    @pl.when(last_step())
    def _():
        total = jnp.sum(acc[...], axis=0, keepdims=True)
        for k in range(4):
            sums_ref[pl.ds(place_ref[0] ^ k, 1), :] = total[:, k * units : (k + 1) * units]
            start = 4 * units + k * grad.shape[1]
            sums_ref[4 + k : 5 + k, :] = total[:, start : start + grad.shape[1]]
        put_parts(
            leaving_ref, staying_ref,
            lambda k: dot_tn(all_normed[...], all_hidden[:, k * units : (k + 1) * units]),
        )


def feed_back(layer, place, grad, slope, stream, normed, gain, packs):
    rows, width = stream.shape
    units = packs[0][0].shape[2]
    operands = (
        [(grad, rows_of(width)), (slope, rows_of(4 * units)), (stream, rows_of(width)), (normed, rows_of(width))]
        + [(gain, whole(gain))]
        + feed_specs(layer, packs)
    )
    outs = [
        ((rows, width), f32, rows_of(width)),
        ((rows, width), bf16, rows_of(width)),
        ((8, width), f32, sums_of(width)),
    ] + parts_outs(width)
    scratch = [
        pltpu.VMEM((8, 4 * units + 4 * width), f32),
        pltpu.VMEM((rows, 4 * units), bf16),
        pltpu.VMEM((rows, width), bf16),
    ]
    return call(partial(feed_back_kernel, layer), "feed_back", place, 4, operands, outs, scratch)


def grad_kernel(kind, place_ref, *refs):
    *inputs, leaving_ref, staying_ref = refs
    if kind == "attn":
        side_ref, normed_ref, part_ref, g1_ref = inputs
        upper = dot_tn(side_ref[...], normed_ref[...])
        lower = dot_tn(part_ref[...], g1_ref[...])
        value = jnp.concatenate([upper, lower], axis=0)
    else:
        left_ref, right_ref = inputs
        value = dot_tn(left_ref[...], right_ref[...])
    value = value.astype(bf16)
    step = pl.program_id(0)

    @pl.when(step < 2)
    def _():
        leaving_ref[...] = value

    @pl.when(step >= 2)
    def _():
        staying_ref[...] = value


def grads(kind, place, arrays, width):
    rows = arrays[1].shape[0]

    def part_at(i):
        return jnp.where(i < 2, 2 * i + 1, 2 * i - 4)

    part = pl.BlockSpec((rows, width), lambda i, s: (0, part_at(i)))

    def of_part(a):
        return pl.BlockSpec((None, *a.shape[1:]), lambda i, s: (part_at(i), 0, 0))

    if kind == "attn":
        side, normed, attended, g1 = arrays
        specs = [of_part(side), whole(normed), of_part(attended), whole(g1)]
    elif kind == "up":
        specs = [whole(arrays[0]), part]
    else:
        specs = [part, whole(arrays[1])]
    block = (None, width, width)
    outs = [
        ((2, width, width), bf16, pl.BlockSpec(block, lambda i, s: (jnp.minimum(i, 1), 0, 0))),
        ((2, width, width), bf16, pl.BlockSpec(block, lambda i, s: (jnp.maximum(i - 2, 0), 0, 0))),
    ]
    return call(
        partial(grad_kernel, kind), "grads_" + kind, place, 4, list(zip(arrays, specs)), outs
    )


def emit_kernel(attention, aliased, place_ref, mine_ref, other_ref, *refs):
    outs = refs[aliased:]
    half, width = mine_ref.shape
    upper = place_ref[2] == 1
    mine, other = mine_ref[...].astype(f32), other_ref[...].astype(f32)
    low, high = jnp.where(upper, other, mine), jnp.where(upper, mine, other)
    if attention:
        qkv_ref, out_ref = outs
        share = width // 4
        qkv_ref[0, 0], qkv_ref[0, 1] = low[:share], low[share:]
        qkv_ref[0, 2], out_ref[0] = high[:share], high[share:]
    else:
        outs[0][0, :half] = low
        outs[0][0, half:] = high


def emit(place, layer, attention, summed, earlier):
    width = summed[0].shape[1]
    share = width // 4
    if attention:
        outs = [
            ((2, 3, share, width), f32, pl.BlockSpec((1, 3, share, width), lambda i, s: (layer, 0, 0, 0))),
            ((2, share, width), f32, pl.BlockSpec((1, share, width), lambda i, s: (layer, 0, 0))),
        ]
    else:
        outs = [((2, width, width), f32, pl.BlockSpec((1, width, width), lambda i, s: (layer, 0, 0)))]
    operands = [(a, whole(a)) for a in summed]
    aliases = {}
    if earlier is not None:
        aliases = {3 + n: n for n in range(len(earlier))}
        operands += [(e, pl.BlockSpec(memory_space=pl.ANY)) for e in earlier]
    return call(
        partial(emit_kernel, attention, len(aliases)), "emit", place, 1, operands, outs, aliases=aliases
    )


def head_swap(values, distance):
    count = lax.axis_size("head")
    return lax.ppermute(values, "head", [(i, i ^ distance) for i in range(count)])


def clip_swap(values, distance):
    count = lax.axis_size("clip")
    return lax.ppermute(values, "clip", [(i, i ^ distance) for i in range(count)])


class Order:
    def __init__(self):
        self.last = ()
        self.pending = []

    def run(self, step, *values):
        values, _ = lax.optimization_barrier((values, self.last))
        out = step(*values)
        self.last = (jax.tree.leaves(out)[0],)
        return out

    def send(self, swap, values, distance):
        values, _ = lax.optimization_barrier((values, self.last))
        out = swap(values, distance)
        self.pending.append(out)
        return out

    def close(self):
        self.last = self.last + tuple(self.pending)
        self.pending = []


def split_halves(total, upper):
    half = total.shape[0] // 2
    low, high = total[:half], total[half:]
    return jnp.where(upper, low, high).astype(bf16), jnp.where(upper, high, low).astype(bf16)


def join_halves(mine, other, upper):
    return jnp.concatenate(
        [jnp.where(upper, other, mine), jnp.where(upper, mine, other)], axis=0
    )


class Pack:
    def __init__(self, order, leaving, staying, halving=True):
        self.order = order
        self.out, self.kept = leaving, staying
        levels = lax.axis_size("clip").bit_length() - 1
        clip = lax.axis_index("clip")
        self.uppers = [((clip >> n) & 1) == 1 for n in range(levels)]
        depth = levels - 1 if halving else 1
        down = [("halve", n) for n in range(depth)]
        level = [("all", n) for n in range(depth, levels)]
        up = [("join", n) for n in reversed(range(depth))]
        self.stages = ["core", "across"] + down + level + up
        self.at = 0
        self.prepared = False

    def prepare(self):
        if self.prepared:
            return
        self.prepared = True
        stage = self.stages[self.at]
        run = self.order.run
        if stage == "core":
            self.leaving = self.out
        elif stage == "across":
            self.leaving = run(
                lambda kept, near: (kept[1].astype(f32) + near[1].astype(f32)).astype(bf16),
                self.kept, self.near,
            )
        else:
            kind, level = stage
            upper = self.uppers[level]
            if self.at == 2:
                start = lambda kept, near, moved: (
                    kept[0].astype(f32) + near[0].astype(f32) + moved.astype(f32)
                )
                values = (self.kept, self.near, self.moved)
            else:
                start = lambda total, moved: total.astype(f32) + moved.astype(f32)
                values = (self.sum, self.moved)
            if kind == "halve":
                self.leaving, self.sum = run(lambda *v: split_halves(start(*v), upper), *values)
            elif kind == "all" or self.stages[self.at - 1][0] == "all":
                self.leaving = self.sum = run(lambda *v: start(*v).astype(bf16), *values)
            else:
                before = self.uppers[self.stages[self.at - 1][1]]
                self.leaving = self.sum = run(
                    lambda mine, other: join_halves(mine, other, before), self.sum, self.moved
                )

    def launch(self):
        stage = self.stages[self.at]
        send = self.order.send
        if stage == "core":
            self.near = send(head_swap, self.leaving, 1)
        elif stage == "across":
            self.moved = send(head_swap, self.leaving, 2)
        else:
            self.moved = send(clip_swap, self.leaving, 1 << stage[1])
        self.at += 1
        self.prepared = False

    def done(self):
        return self.at == len(self.stages)

    def whole(self):
        assert self.done()
        return self.sum, self.moved


def on_device(
    tokens,
    frame_counts,
    token_mask,
    targets,
    norm_gain,
    norm_bias,
    w_qkv,
    qv_bias,
    w_out,
    vec_bias,
    w_up,
    up_bias,
    w_down,
    code_head,
):
    head_index = lax.axis_index("head")
    width = tokens.shape[1]
    share = w_out.shape[1]
    upper = lax.axis_index("clip") & 1
    place = jnp.stack(
        [head_index.astype(jnp.int32), frame_counts[0], upper.astype(jnp.int32)]
    )
    order = Order()

    def tied(values, *after):
        return lax.optimization_barrier((values, after))[0]

    clip_count = lax.axis_size("clip")
    own_small = jnp.concatenate([up_bias, qv_bias.reshape(1, width)], axis=0)
    clip_index = lax.axis_index("clip")

    def chunk(matrix):
        piece = matrix.shape[0] // clip_count
        return lax.dynamic_slice_in_dim(matrix, clip_index * piece, piece, 0)

    def over_clips(chunk_across):
        return lax.all_gather(chunk_across, "clip", axis=0, tiled=True)

    y_place, z_place = clip_index & 1, (clip_index >> 1) & 1

    def quarter(matrix):
        rows = matrix.shape[0] // 4
        return lax.dynamic_slice_in_dim(matrix, (2 * y_place + z_place) * rows, rows, 0)

    def along_y(first):
        return jnp.concatenate([first, clip_swap(first, 1)], axis=0)

    def by_place(pair, others):
        rows = pair.shape[0] // 2
        pieces = []
        for y in range(2):
            for z in range(2):
                same = z_place == z
                mine = jnp.where(same, pair[:rows], others[:rows])
                next_one = jnp.where(same, pair[rows:], others[rows:])
                pieces.append(jnp.where(y_place == y, mine, next_one))
        return jnp.concatenate(pieces, axis=0)

    def attn_pack(layer):
        transposed = w_qkv[layer].swapaxes(1, 2).reshape(-1, width)
        return jnp.concatenate([transposed, w_out[layer]], axis=0)

    def spread(own, across):
        return [own, head_swap(own, 1), across, head_swap(across, 1)]

    quarters = jnp.concatenate([quarter(w_up[0]), quarter(w_down[0])], axis=0)
    quarters = head_swap(quarters, 2)
    smalls = spread(own_small, head_swap(own_small, 2))
    own = tied(attn_pack(0), quarters, smalls[2])
    later = jnp.concatenate([chunk(w_up[1]), chunk(w_down[1])], axis=0)
    marks = (2 * targets + token_mask).astype(f32).reshape(-1, 1)
    rows = quarters.shape[0] // 2
    beyond_y = clip_swap(quarters, 1)
    up_pair = jnp.concatenate([quarters[:rows], beyond_y[:rows]], axis=0)
    down_pair = jnp.concatenate([quarters[rows:], beyond_y[rows:]], axis=0)
    across, later, marks, place, up_pair, up_others, down_pair = lax.optimization_barrier(
        (head_swap(own, 2), later, marks, place, up_pair, clip_swap(up_pair, 2), down_pair)
    )
    attn = [spread(own, across), None]
    order.last = (across,)
    down_others = order.send(clip_swap, down_pair, 2)
    chunk_1 = order.send(head_swap, later, 2)
    order.last = (smalls[1], smalls[3], attn[0][1], attn[0][3])
    ups = [w_up, order.send(head_swap, w_up, 1)]
    downs = [w_down, order.send(head_swap, w_down, 1)]
    packs = [None, None]

    def feed_packs(up_x, down_x):
        return (
            ups, downs,
            [up_x, order.send(head_swap, up_x, 1)],
            [down_x, order.send(head_swap, down_x, 1)],
        )

    kept = []
    inputs = (tokens, marks)
    for layer in range(2):
        x, normed, qkv, att, lse, att_parts, *mark_pieces = order.run(
            lambda *a: attend(layer, place, a, norm_gain, norm_bias, smalls, attn[layer]), *inputs
        )
        order.close()
        if layer == 0:
            gathered = over_clips(tied(chunk_1, x))
            marks = [mark_pieces[0]] + [head_swap(mark_pieces[k], k) for k in (1, 2, 3)]
            up_x, down_x = order.run(
                lambda a, b, c, d: (by_place(a, b), by_place(c, d)),
                up_pair, up_others, down_pair, down_others,
            )
            packs[0] = feed_packs(up_x, down_x)
            order.close()
            own = attn_pack(1)
            attn_across = order.send(head_swap, own, 2)
            attn[1] = [own, head_swap(own, 1), attn_across]
        stream, normed2, active, slope, *outs = order.run(
            lambda a, b: feed(
                layer, place, a, b, attn[layer], vec_bias, norm_gain, norm_bias, smalls, packs[layer]
            ),
            x, att,
        )
        kept.append((x, normed, qkv, att_parts, lse, stream, normed2, active, slope))
        if layer == 0:
            order.close()
            pieces = gathered.reshape(clip_count, 2, -1, width)
            attn[1].append(order.send(head_swap, attn_across, 1))
            inputs = [outs[0]] + [order.send(head_swap, outs[k], k) for k in (1, 2, 3)]
            inputs = [p.reshape(4, 4, CELL, width) for p in inputs]
            order.close()
            packs[1] = feed_packs(pieces[:, 0].reshape(-1, width), pieces[:, 1].reshape(-1, width))
    grad, loss_sum, *parts = order.run(
        lambda a: code_loss(place, a, code_head, marks, active), outs[0]
    )
    down_1 = Pack(order, *parts, halving=False)

    def run_feed_back(layer, grad):
        x, normed, qkv, att, lse, stream, normed2, active, slope = kept[layer]
        return order.run(
            lambda a: feed_back(layer, place, a, slope, stream, normed2, norm_gain, packs[layer]), grad
        )

    def run_attend_back(layer, grad_next, g1):
        x, normed, qkv, att, lse, *_ = kept[layer]
        return order.run(
            lambda a, b: attend_back(
                layer, place, a, b, x, qkv, lse, norm_gain, attn[layer], normed, att
            ),
            grad_next, g1,
        )

    def pack(kind, *arrays, halving=True):
        parts = order.run(lambda *a: grads(kind, place, a, width), *arrays)
        return Pack(order, *parts, halving=halving)

    def move(*ones):
        for one in ones:
            one.prepare()
        for one in ones:
            one.launch()

    move(down_1)
    order.close()
    move(down_1)
    grad_next, g1, feed_sum_1, *parts = run_feed_back(1, grad)
    up_1 = Pack(order, *parts, halving=False)
    order.close()
    move(up_1)
    down_1.prepare()
    order.close()
    move(up_1, down_1)
    side, *outs, attn_sum_1 = run_attend_back(1, grad_next, g1)
    order.close()

    grad = [outs[0]] + [order.send(head_swap, outs[k], k) for k in (1, 2, 3)]
    grad = [p.reshape(4, BAND, width) for p in grad]
    move(up_1, down_1)
    attn_1 = pack("attn", side, kept[1][1], kept[1][3], g1, halving=False)
    order.close()

    move(attn_1)
    g2 = jnp.stack(grad, axis=1).reshape(-1, width)
    down_0 = pack("down", kept[0][7], g2)
    order.close()
    move(attn_1, down_0, down_1, up_1)
    grad_next, g1, feed_sum_0, *parts = run_feed_back(0, g2)
    up_0 = Pack(order, *parts)
    order.close()
    move(down_0, up_0, attn_1, down_1, up_1)
    grad_input, attn_sum_0, *parts = run_attend_back(0, grad_next, g1)
    attn_0 = Pack(order, *parts)
    order.close()
    move(up_0, attn_0, down_0, attn_1, up_1)
    order.close()
    move(attn_0, up_0, down_0, attn_1)
    order.close()

    packed = jnp.concatenate([feed_sum_0, feed_sum_1, attn_sum_0, attn_sum_1, loss_sum], axis=0)
    swaps = [(head_swap, 1), (head_swap, 2)]
    swaps += [(clip_swap, 1 << n) for n in range(clip_count.bit_length() - 1)]

    def pack_step():
        swap, distance = swaps.pop(0)
        return packed + order.send(swap, packed, distance)

    ready = {}

    def write(one, layer, attention, earlier):
        ready[one] = order.run(lambda *a: emit(place, layer, attention, a, earlier), *one.whole())

    late = [down_1, up_1]
    moving = [attn_0, up_0, down_0]
    wait = 0
    while swaps or not all(one.done() for one in moving + late + [attn_1]):
        move(*[one for one in moving + late if not one.done()])
        if wait:
            move(*[one for one in [attn_1] if not one.done()])
        wait += 1
        if swaps:
            packed = pack_step()
        for one in late:
            if one.done() and one not in ready:
                write(one, 1, False, None)
                break
        if attn_1.done() and wait > 2 and attn_1 not in ready:
            write(attn_1, 1, True, None)
        for one, earlier in ((down_0, down_1), (up_0, up_1)):
            if one.done() and one not in ready and earlier in ready and one.closed:
                write(one, 0, False, ready[earlier])
                break
        order.close()
        for one in moving:
            one.closed = one.done()

    for one, layer, attention, earlier in (
        (down_1, 1, False, None), (up_1, 1, False, None), (attn_1, 1, True, None),
        (down_0, 0, False, down_1), (up_0, 0, False, up_1), (attn_0, 0, True, attn_1),
    ):
        if one not in ready:
            write(one, layer, attention, ready.get(earlier))

    attn_out, up_out, down_out = ready[attn_0], ready[up_0], ready[down_0]

    feed_sums = packed[:16].reshape(2, 8, width)
    attn_sums = packed[16:32].reshape(2, 8, width)
    loss_total = packed[32, 0]
    own_feed = lax.dynamic_index_in_dim(feed_sums, head_index, 1, keepdims=False)
    own_attn = lax.dynamic_index_in_dim(attn_sums, head_index, 1, keepdims=False)
    slot_total = clip_count * frame_counts.shape[0] * FRAMES * SIDE * SIDE

    return (
        loss_total / slot_total,
        grad_input,
        jnp.stack([attn_sums[:, 4], feed_sums[:, 4]], axis=1),
        jnp.stack([attn_sums[:, 5], feed_sums[:, 5]], axis=1),
        attn_out[0].swapaxes(2, 3),
        own_attn[:, : 2 * share].reshape(2, 2, share),
        attn_out[1],
        jnp.stack([feed_sums[:, 7], feed_sums[:, 6]], axis=1),
        up_out[0],
        own_feed,
        down_out[0],
    )


def solution(mesh):
    placed = (
        P(("clip", "head"), None),
        P("clip"),
        P(("clip", "head")),
        P(("clip", "head")),
        P(),
        P(),
        P(None, None, None, "head"),
        P(None, None, "head"),
        P(None, "head", None),
        P(),
        P(None, None, "head"),
        P(None, "head"),
        P(None, "head", None),
        P(),
    )
    return jax.shard_map(
        on_device,
        mesh=mesh,
        in_specs=placed,
        out_specs=(
            P(),
            P(("clip", "head"), None),
            P(),
            P(),
            P(None, None, None, "head"),
            P(None, None, "head"),
            P(None, "head", None),
            P(),
            P(None, None, "head"),
            P(None, "head"),
            P(None, "head", None),
        ),
        check_vma=False,
    )
```

```python
from functools import partial

import jax
import jax.numpy as jnp
from jax import lax
from jax.experimental import pallas as pl
from jax.experimental.pallas import tpu as pltpu
from jax.sharding import PartitionSpec as P

HD = 64
FRAMES = 16
SIDE = 16
TUBE = 4
WINDOW = 256
PAIR = 128
BAND = 64
CELL = 16
LSE_ROWS = 16

epsilon = 1e-06
masked_score = -1e30
f32 = jnp.float32
bf16 = jnp.bfloat16
VMEM_LIMIT = 56 * 1024 * 1024
TIMES = {
    "attend": 17, "feed": 23, "code_loss": 10, "feed_back": 21, "attend_back": 25,
    "grads_down": 8, "grads_up": 8, "grads_attn": 8, "emit": 3,
}
SCALE = 0.0001


def cost_of(name):
    time = TIMES[name] * SCALE
    return pl.CostEstimate(flops=int(time * 1.15e9), bytes_accessed=int(time * 3.6e6), transcendentals=0)


def dot(a, b):
    return lax.dot_general(a, b, (((1,), (0,)), ((), ())), preferred_element_type=f32)


def dot_nt(a, b):
    return lax.dot_general(a, b, (((1,), (1,)), ((), ())), preferred_element_type=f32)


def dot_tn(a, b):
    return lax.dot_general(a, b, (((0,), (0,)), ((), ())), preferred_element_type=f32)


def statistics(stream):
    centre = jnp.mean(stream, axis=-1, keepdims=True)
    centred = stream - centre
    spread = jnp.mean(centred * centred, axis=-1, keepdims=True)
    scale = lax.rsqrt(spread + epsilon)
    return centred * scale, scale


def by_eight(values):
    rows, columns = values.shape
    return jnp.sum(values.reshape(rows // 8, 8, columns), axis=0)


def gather_sums(acc_ref, values):
    first = pl.program_id(0) == 0
    parts = jnp.concatenate([by_eight(v) for v in values], axis=1)

    @pl.when(first)
    def _():
        acc_ref[...] = parts

    @pl.when(jnp.logical_not(first))
    def _():
        acc_ref[...] += parts


ORDER = (1, 3, 0, 2)


def step_rows():
    return pl.ds(pl.multiple_of(pl.program_id(0) * WINDOW, WINDOW), WINDOW)


def put_parts(leaving_ref, staying_ref, gradient_of):
    for n, k in enumerate(ORDER):
        (leaving_ref if n < 2 else staying_ref)[n % 2] = gradient_of(k).astype(bf16)


def parts_outs(width):
    spec = pl.BlockSpec((2, width, width), lambda i, s: (0, 0, 0))
    return [((2, width, width), bf16, spec)] * 2


def last_step():
    return pl.program_id(0) == pl.num_programs(0) - 1


def norm_back(stream, gain, grad):
    normal, scale = statistics(stream)
    scaled = grad * gain
    mean_plain = jnp.mean(scaled, axis=-1, keepdims=True)
    mean_normal = jnp.mean(scaled * normal, axis=-1, keepdims=True)
    inner = scale * (scaled - mean_plain - normal * mean_normal)
    return inner, grad * normal


def gelu_both(hidden):
    root = 0.7978845608028654
    cubic = 0.044715
    square = hidden * hidden
    bend = jnp.tanh(hidden * (root + root * cubic * square))
    rise = 0.5 + 0.5 * bend
    active = hidden * rise
    slope = rise + (active - active * rise) * (2.0 * root + 6.0 * root * cubic * square)
    return active.astype(bf16), slope.astype(bf16)


def allowed_of(place_ref):
    head_index = place_ref[0]
    frame_count = place_ref[1]

    def valid(axis):
        position = lax.broadcasted_iota(jnp.int32, (WINDOW, WINDOW), axis)
        frame = 4 * ((position >> 6) ^ head_index) + ((position >> 4) & 3)
        return frame < frame_count

    return jnp.logical_or(valid(0), jnp.logical_not(valid(1)))


def shuffle_of(place_ref, axis):
    arranged = lax.broadcasted_iota(jnp.int32, (WINDOW, WINDOW), axis)
    plain = lax.broadcasted_iota(jnp.int32, (WINDOW, WINDOW), 1 - axis)
    band = (arranged >> 6) ^ place_ref[0]
    source = band * BAND + ((arranged >> 2) & 3) * 16 + ((arranged >> 4) & 3) * 4 + (arranged & 3)
    return (source == plain).astype(f32).astype(bf16)


def assemble_qkv(packs, scratch):
    width = scratch.shape[1]
    share = width // 4
    for k in range(4):
        for j in range(3):
            start = j * width + k * share
            scratch[start : start + share, :] = packs[k][j * share : (j + 1) * share, :]


def assemble_out(packs, scratch):
    share = scratch.shape[0] // 4
    for k in range(4):
        scratch[k * share : (k + 1) * share, :] = packs[k][3 * share :, :]


def stack_heads(pair):
    low = lax.broadcasted_iota(jnp.int32, pair.shape, 1) < HD
    zero = jnp.zeros((), bf16)
    return jnp.concatenate([jnp.where(low, pair, zero), jnp.where(low, zero, pair)], axis=0)


def attend_core(qkv, allowed, att_ref, lse_ref, part_ref):
    width = att_ref.shape[1]
    pairs = width // PAIR

    def part(j, pair):
        return qkv[:, j * width + pair * PAIR : j * width + (pair + 1) * PAIR]

    def scores_of(pair):
        query = part(0, pair) * jnp.asarray(HD ** (-0.5), bf16)
        return dot_nt(stack_heads(part(1, pair)), query)

    ahead = scores_of(0)
    for pair in range(pairs):
        scores = ahead
        if pair + 1 < pairs:
            ahead = scores_of(pair + 1)
        probs = []
        for half in range(2):
            mine = scores[half * WINDOW : (half + 1) * WINDOW]
            if allowed is not None:
                mine = jnp.where(allowed, mine, masked_score)
            top = jnp.max(mine, axis=0, keepdims=True)
            terms = jnp.exp(mine - top)
            total = jnp.sum(terms, axis=0, keepdims=True)
            probs.append((terms * (1.0 / total)).astype(bf16))
            head = 2 * pair + half
            lse_ref[head : head + 1, :] = top + jnp.log(total)
        out = dot_tn(jnp.concatenate(probs, axis=0), stack_heads(part(2, pair)))
        att_ref[:, pair * PAIR : (pair + 1) * PAIR] = out.astype(bf16)
    share = width // 4
    for k in range(4):
        part_ref[k] = att_ref[:, k * share : (k + 1) * share]


def attend_kernel(layer, place_ref, *refs):
    if layer == 0:
        tokens_ref, marks_ref, *refs = refs
        shuffle = shuffle_of(place_ref, 0)
        stream = dot(shuffle, tokens_ref[...])
    else:
        pieces, refs = refs[:4], refs[4:]
        stream = jnp.concatenate(
            [p[...].reshape(BAND, p.shape[-1]) for p in pieces], axis=0
        ).astype(f32)
    gain_ref, shift_ref, s0, s1, s2, s3, p0, p1, p2, p3, x_ref, normed_ref, qkv_ref, att_ref, lse_ref, part_ref, *refs = refs
    *mark_refs, scratch = refs
    share = scratch.shape[1] // 4

    @pl.when(pl.program_id(0) == 0)
    def _():
        assemble_qkv((p0, p1, p2, p3), scratch)

    if layer == 0:
        given = marks_ref[pl.ds(pl.program_id(0), 1), :]
        high = given >> 4
        both = jnp.concatenate([high, given - 16 * high], axis=0).astype(f32).astype(bf16)
        both = dot(both, shuffle_of(place_ref, 1))
        marks = 16.0 * both[0:1] + both[1:2]
        for k in range(4):
            mark_refs[k][pl.ds(pl.program_id(0), 1), :] = marks[:, k * BAND : (k + 1) * BAND]
    x_ref[...] = stream.astype(bf16)
    normal, _ = statistics(stream)
    normed = (normal * gain_ref[layer, 0:1] + shift_ref[layer, 0:1]).astype(bf16)
    normed_ref[...] = normed
    start = 2 * layer * share
    smalls = (s0, s1, s2, s3)
    bias = jnp.concatenate(
        [r[2:3, start : start + share] for r in smalls]
        + [jnp.zeros((1, 4 * share), f32)]
        + [r[2:3, start + share : start + 2 * share] for r in smalls],
        axis=1,
    )
    qkv = (dot_nt(normed, scratch[...]) + bias).astype(bf16)
    qkv_ref[...] = qkv
    allowed = allowed_of(place_ref) if layer == 1 else None
    attend_core(qkv, allowed, att_ref, lse_ref, part_ref)


def whole(array):
    zeros = (0,) * array.ndim
    return pl.BlockSpec(array.shape, lambda i, s: zeros)


def rows_of(columns, rows=WINDOW):
    return pl.BlockSpec((rows, columns), lambda i, s: (i, 0))


def parts_of(columns):
    return pl.BlockSpec((4, WINDOW, columns), lambda i, s: (0, i, 0))


def tube_of(columns):
    return pl.BlockSpec((4, 1, CELL, columns), lambda i, s: (0, i, 0, 0))


def sums_of(columns):
    return pl.BlockSpec((8, columns), lambda i, s: (0, 0))


def call(kernel, name, place, steps, operands, outs, scratch=(), aliases={}):
    return pl.pallas_call(
        kernel,
        grid_spec=pltpu.PrefetchScalarGridSpec(
            num_scalar_prefetch=1,
            grid=(steps,),
            in_specs=[spec for _, spec in operands],
            out_specs=[spec for _, _, spec in outs],
            scratch_shapes=list(scratch),
        ),
        out_shape=[jax.ShapeDtypeStruct(shape, dtype) for shape, dtype, _ in outs],
        compiler_params=pltpu.CompilerParams(vmem_limit_bytes=VMEM_LIMIT),
        cost_estimate=cost_of(name),
        input_output_aliases=aliases,
        name=name,
    )(place, *[array for array, _ in operands])


def attend(layer, place, inputs, gain, shift, smalls, packs):
    width = gain.shape[-1]
    rows = 4 * WINDOW
    if layer == 0:
        tokens, marks = inputs
        first = [(tokens, rows_of(width)), (marks, whole(marks))]
    else:
        first = [(p, tube_of(width)) for p in inputs]
    operands = first + [(a, whole(a)) for a in (gain, shift, *smalls, *packs)]
    outs = [
        ((rows, width), bf16, rows_of(width)),
        ((rows, width), bf16, rows_of(width)),
        ((rows, 3 * width), bf16, rows_of(3 * width)),
        ((rows, width), bf16, rows_of(width)),
        ((4 * LSE_ROWS, WINDOW), f32, rows_of(WINDOW, LSE_ROWS)),
        ((4, rows, width // 4), bf16, parts_of(width // 4)),
    ]
    if layer == 0:
        outs += [((4, BAND), f32, pl.BlockSpec((4, BAND), lambda i, s: (0, 0)))] * 4
    return call(
        partial(attend_kernel, layer), "attend", place, 4, operands, outs,
        [pltpu.VMEM((3 * width, width), bf16)],
    )


def attend_back_core(qkv, grad, lse_ref, allowed):
    width = grad.shape[1]
    pairs = width // PAIR

    def part(j, pair):
        return qkv[:, j * width + pair * PAIR : j * width + (pair + 1) * PAIR]

    def first_of(pair):
        query = part(0, pair) * jnp.asarray(HD ** (-0.5), bf16)
        grad_part = grad[:, pair * PAIR : (pair + 1) * PAIR]
        keys = stack_heads(part(1, pair))
        scores = dot_nt(keys, query)
        grad_probs = dot_nt(stack_heads(part(2, pair)), grad_part)
        return query, grad_part, keys, scores, grad_probs

    low = lax.broadcasted_iota(jnp.int32, (WINDOW, PAIR), 1) < HD
    results = [[], [], []]
    ahead = first_of(0)
    for pair in range(pairs):
        query, grad_part, keys, scores, grad_probs = ahead
        if pair + 1 < pairs:
            ahead = first_of(pair + 1)
        all_probs, all_scores = [], []
        for half in range(2):
            rows = slice(half * WINDOW, (half + 1) * WINDOW)
            mine = scores[rows]
            if allowed is not None:
                mine = jnp.where(allowed, mine, masked_score)
            head = 2 * pair + half
            probs = jnp.exp(mine - lse_ref[head : head + 1, :])
            grad_mine = grad_probs[rows]
            delta = jnp.sum(probs * grad_mine, axis=0, keepdims=True)
            all_probs.append(probs.astype(bf16))
            all_scores.append((probs * (grad_mine - delta)).astype(bf16))
        probs = jnp.concatenate(all_probs, axis=0)
        grad_scores = jnp.concatenate(all_scores, axis=0)
        grad_query = dot_tn(grad_scores, keys) * HD ** (-0.5)
        grad_key = dot(grad_scores, query)
        grad_value = dot(probs, grad_part)
        results[0].append(grad_query.astype(bf16))
        results[1].append(jnp.where(low, grad_key[:WINDOW], grad_key[WINDOW:]).astype(bf16))
        results[2].append(jnp.where(low, grad_value[:WINDOW], grad_value[WINDOW:]).astype(bf16))
    return [jnp.concatenate(part, axis=1) for part in results]


def attend_back_kernel(layer, place_ref, *refs):
    (stream_ref, g1_ref, x_ref, qkv_ref, lse_ref, gain_ref, p0, p1, p2, p3, *outs) = refs
    if layer == 1:
        side_ref, *outs = outs
        pieces, outs = outs[:4], outs[4:]
        sums_ref, scratch, out_scratch, acc = outs
        rows = slice(None)
    else:
        (
            normed_ref, part_ref, final_ref, sums_ref, leaving_ref, staying_ref,
            scratch, out_scratch, acc, side_ref, all_normed, all_parts, all_g1,
        ) = outs
        rows = step_rows()
        all_normed[rows, :] = normed_ref[...]
        all_g1[rows, :] = g1_ref[...]
        for k in range(4):
            all_parts[k, rows, :] = part_ref[k]
    width = stream_ref.shape[1]
    share = width // 4

    @pl.when(pl.program_id(0) == 0)
    def _():
        assemble_qkv((p0, p1, p2, p3), scratch)
        assemble_out((p0, p1, p2, p3), out_scratch)

    grad_att = dot_nt(g1_ref[...], out_scratch[...]).astype(bf16)
    allowed = allowed_of(place_ref) if layer == 1 else None
    parts = attend_back_core(qkv_ref[...], grad_att, lse_ref, allowed)
    for k in range(4):
        for j in range(3):
            side_ref[k, rows, j * share : (j + 1) * share] = parts[j][:, k * share : (k + 1) * share]
    joined = jnp.concatenate(parts, axis=1)
    grad_normed = dot(joined, scratch[...])
    inner, scaled = norm_back(x_ref[...].astype(f32), gain_ref[layer, 0:1], grad_normed)
    gather_sums(acc, [parts[0].astype(f32), parts[2].astype(f32), scaled, grad_normed])
    stream = stream_ref[...] + inner
    if layer == 1:
        for k in range(4):
            pieces[k][...] = (
                stream[k * BAND : (k + 1) * BAND].astype(bf16).reshape(4, 1, CELL, width)
            )
    else:
        shuffle = shuffle_of(place_ref, 1)
        high = stream.astype(bf16)
        low = (stream - high.astype(f32)).astype(bf16)
        final_ref[...] = dot(shuffle, high) + dot(shuffle, low)

    @pl.when(last_step())
    def _():
        total = jnp.sum(acc[...], axis=0, keepdims=True)
        sums_ref[...] = jnp.zeros(sums_ref.shape, f32)
        for k in range(4):
            query = total[:, k * share : (k + 1) * share]
            value = total[:, width + k * share : width + (k + 1) * share]
            sums_ref[pl.ds(place_ref[0] ^ k, 1), : 2 * share] = jnp.concatenate([query, value], axis=1)
        sums_ref[4:5, :] = total[:, 2 * width : 3 * width]
        sums_ref[5:6, :] = total[:, 3 * width :]
        if layer == 0:

            def gradient_of(k):
                upper = dot_tn(side_ref[k], all_normed[...])
                lower = dot_tn(all_parts[k], all_g1[...])
                return jnp.concatenate([upper, lower], axis=0)

            put_parts(leaving_ref, staying_ref, gradient_of)


def attend_back(layer, place, stream, g1, x, qkv, lse, gain, packs, normed, attended):
    rows, width = stream.shape
    share = width // 4
    operands = [
        (stream, rows_of(width)),
        (g1, rows_of(width)),
        (x, rows_of(width)),
        (qkv, rows_of(3 * width)),
        (lse, rows_of(WINDOW, LSE_ROWS)),
    ] + [(a, whole(a)) for a in (gain, *packs)]
    sums = [((8, width), f32, sums_of(width))]
    scratch = [
        pltpu.VMEM((3 * width, width), bf16), pltpu.VMEM((width, width), bf16), pltpu.VMEM((8, 4 * width), f32)
    ]
    if layer == 1:
        outs = [((4, rows, 3 * share), bf16, parts_of(3 * share))]
        outs = outs + [((4, 4, CELL, width), bf16, tube_of(width))] * 4 + sums
    else:
        operands += [(normed, rows_of(width)), (attended, parts_of(share))]
        outs = [((rows, width), f32, rows_of(width))] + sums + parts_outs(width)
        scratch += [
            pltpu.VMEM((4, rows, 3 * share), bf16), pltpu.VMEM((rows, width), bf16),
            pltpu.VMEM((4, rows, share), bf16), pltpu.VMEM((rows, width), bf16),
        ]
    return call(partial(attend_back_kernel, layer), "attend_back", place, 4, operands, outs, scratch)


def feed_kernel(layer, place_ref, *refs):
    (
        x_ref, att_ref, a0, a1, a2, a3, vec_ref, gain_ref, shift_ref, s0, s1, s2, s3,
        u0, u1, u2, u3, d0, d1, d2, d3, stream_ref, normed_ref, active_ref, slope_ref, *outs
    ) = refs
    ups, downs = (u0, u1, u2, u3), (d0, d1, d2, d3)
    *pieces, scratch = outs
    width = x_ref.shape[1]

    @pl.when(pl.program_id(0) == 0)
    def _():
        share = width // 4
        for k, part in enumerate((a0, a1, a2, a3)):
            scratch[k * share : (k + 1) * share, :] = part[...]

    stream = x_ref[...].astype(f32) + dot(att_ref[...], scratch[...]) + vec_ref[layer, 0:1]
    stream_ref[...] = stream
    normal, _ = statistics(stream)
    normed = (normal * gain_ref[layer, 1:2] + shift_ref[layer, 1:2]).astype(bf16)
    normed_ref[...] = normed
    total = stream + vec_ref[layer, 1:2]
    units = u0.shape[1]
    ahead = dot(normed, ups[0][...])
    for k in range(4):
        hidden = ahead
        if k < 3:
            ahead = dot(normed, ups[k + 1][...])
        cut = slice(k * units, (k + 1) * units)
        active, slope = gelu_both(hidden + (s0, s1, s2, s3)[k][layer : layer + 1, :])
        active_ref[:, cut] = active
        slope_ref[:, cut] = slope
        total = total + dot(active, downs[k][...])
    total = total.astype(bf16)
    if layer == 0:
        for k in range(4):
            pieces[k][...] = total[k * BAND : (k + 1) * BAND].reshape(1, BAND, width)
    else:
        pieces[0][...] = total


def feed_specs(layer, packs):
    ups, downs, ups_across, downs_across = packs

    def of_layer(a):
        return (a, pl.BlockSpec((None, *a.shape[1:]), lambda i, s: (layer, 0, 0)))

    return [
        *[of_layer(a) for a in ups],
        *[(a, whole(a)) for a in ups_across],
        *[of_layer(a) for a in downs],
        *[(a, whole(a)) for a in downs_across],
    ]


def feed(layer, place, x, att, attn_packs, vecs, gain, shift, smalls, packs):
    rows, width = x.shape
    units = packs[0][0].shape[2]
    last = pl.BlockSpec((width // 4, width), lambda i, s: (3, 0))
    operands = (
        [(x, rows_of(width)), (att, rows_of(width))]
        + [(a, last) for a in attn_packs]
        + [(a, whole(a)) for a in (vecs, gain, shift, *smalls)]
        + feed_specs(layer, packs)
    )
    outs = [
        ((rows, width), f32, rows_of(width)),
        ((rows, width), bf16, rows_of(width)),
        ((rows, 4 * units), bf16, rows_of(4 * units)),
        ((rows, 4 * units), bf16, rows_of(4 * units)),
    ]
    if layer == 0:
        piece = pl.BlockSpec((1, BAND, width), lambda i, s: (i, 0, 0))
        outs = outs + [((4, BAND, width), bf16, piece)] * 4
    else:
        outs = outs + [((rows, width), bf16, rows_of(width))]
    return call(
        partial(feed_kernel, layer), "feed", place, 4, operands, outs,
        [pltpu.VMEM((width, width), bf16)],
    )


def loss_kernel(
    place_ref, final_ref, head_ref, m0, m1, m2, m3, active_ref, grad_ref, loss_ref, leaving_ref, staying_ref,
    acc, all_active, all_g2,
):
    logits = dot(final_ref[...], head_ref[...])
    spread = jnp.concatenate(
        [jnp.broadcast_to(m[f : f + 1, :], (CELL, BAND)) for m in (m0, m1, m2, m3) for f in range(4)],
        axis=0,
    )
    position = lax.broadcasted_iota(jnp.int32, (WINDOW, BAND), 0)
    lane = lax.broadcasted_iota(jnp.int32, (WINDOW, BAND), 1)
    mine = lane == pl.program_id(0) * CELL + (position & (CELL - 1))
    mark = jnp.sum(jnp.where(mine, spread, 0.0), axis=1, keepdims=True).astype(jnp.int32)
    place_of = lax.broadcasted_iota(jnp.int32, (WINDOW, 1), 0)
    frame = 4 * ((place_of >> 6) ^ place_ref[0]) + ((place_of >> 4) & 3)
    weight = jnp.where(frame < place_ref[1], (mark & 1).astype(f32), 0.0)
    top = jnp.max(logits, axis=1, keepdims=True)
    terms = jnp.exp(logits - top)
    total = jnp.sum(terms, axis=1, keepdims=True)
    code = lax.broadcasted_iota(jnp.int32, logits.shape, 1)
    chosen = code == (mark >> 1)
    picked = jnp.sum(jnp.where(chosen, logits, 0.0), axis=1, keepdims=True)
    entry = weight * (top + jnp.log(total) - picked)
    soft = terms * (1.0 / total)
    grad_logits = (weight * (soft - jnp.where(chosen, 1.0, 0.0))).astype(bf16)
    grad = dot_nt(grad_logits, head_ref[...])
    grad_ref[...] = grad
    all_g2[step_rows(), :] = grad.astype(bf16)
    all_active[step_rows(), :] = active_ref[...]
    gather_sums(acc, [jnp.broadcast_to(entry, (WINDOW, PAIR))])

    @pl.when(last_step())
    def _():
        total = jnp.sum(acc[...], axis=0, keepdims=True)
        loss_ref[...] = jnp.broadcast_to(total[:, :1], loss_ref.shape)
        width = grad_ref.shape[1]
        put_parts(
            leaving_ref, staying_ref,
            lambda k: dot_tn(all_active[:, k * width : (k + 1) * width], all_g2[...]),
        )


def code_loss(place, final, code_head, marks, active):
    rows, width = final.shape
    operands = [(final, rows_of(width))] + [(a, whole(a)) for a in (code_head, *marks)]
    operands += [(active, rows_of(active.shape[1]))]
    outs = [
        ((rows, width), f32, rows_of(width)),
        ((8, width), f32, sums_of(width)),
    ] + parts_outs(width)
    scratch = [
        pltpu.VMEM((8, PAIR), f32), pltpu.VMEM(active.shape, bf16), pltpu.VMEM((rows, width), bf16)
    ]
    return call(loss_kernel, "code_loss", place, 4, operands, outs, scratch)


def feed_back_kernel(layer, place_ref, *refs):
    if layer == 1:
        grad_ref, *refs = refs
        grad = grad_ref[...]
    else:
        grad_ref, *refs = refs
        grad = grad_ref[...].astype(f32)
    (
        slope_ref, stream_ref, normed_ref, gain_ref, u0, u1, u2, u3, d0, d1, d2, d3, next_ref, g1_ref,
        sums_ref, leaving_ref, staying_ref, acc, all_hidden, all_normed,
    ) = refs
    all_normed[step_rows(), :] = normed_ref[...]
    g2 = grad.astype(bf16)
    units = u0.shape[1]
    grad_normed = jnp.zeros(grad.shape, f32)
    sums = []
    ups, downs = (u0, u1, u2, u3), (d0, d1, d2, d3)
    ahead = dot_nt(g2, downs[0][...])
    for k in range(4):
        grad_active = ahead
        if k < 3:
            ahead = dot_nt(g2, downs[k + 1][...])
        cut = slice(k * units, (k + 1) * units)
        grad_hidden = (grad_active * slope_ref[:, cut].astype(f32)).astype(bf16)
        all_hidden[step_rows(), cut] = grad_hidden
        sums.append(grad_hidden.astype(f32))
        grad_normed = grad_normed + dot_nt(grad_hidden, ups[k][...])
    inner, scaled = norm_back(stream_ref[...], gain_ref[layer, 1:2], grad_normed)
    grad = grad + inner
    next_ref[...] = grad
    g1 = grad.astype(bf16)
    g1_ref[...] = g1
    gather_sums(acc, sums + [scaled, grad_normed, g2.astype(f32), g1.astype(f32)])

    @pl.when(last_step())
    def _():
        total = jnp.sum(acc[...], axis=0, keepdims=True)
        for k in range(4):
            sums_ref[pl.ds(place_ref[0] ^ k, 1), :] = total[:, k * units : (k + 1) * units]
            start = 4 * units + k * grad.shape[1]
            sums_ref[4 + k : 5 + k, :] = total[:, start : start + grad.shape[1]]
        put_parts(
            leaving_ref, staying_ref,
            lambda k: dot_tn(all_normed[...], all_hidden[:, k * units : (k + 1) * units]),
        )


def feed_back(layer, place, grad, slope, stream, normed, gain, packs):
    rows, width = stream.shape
    units = packs[0][0].shape[2]
    operands = (
        [(grad, rows_of(width)), (slope, rows_of(4 * units)), (stream, rows_of(width)), (normed, rows_of(width))]
        + [(gain, whole(gain))]
        + feed_specs(layer, packs)
    )
    outs = [
        ((rows, width), f32, rows_of(width)),
        ((rows, width), bf16, rows_of(width)),
        ((8, width), f32, sums_of(width)),
    ] + parts_outs(width)
    scratch = [
        pltpu.VMEM((8, 4 * units + 4 * width), f32),
        pltpu.VMEM((rows, 4 * units), bf16),
        pltpu.VMEM((rows, width), bf16),
    ]
    return call(partial(feed_back_kernel, layer), "feed_back", place, 4, operands, outs, scratch)


def grad_kernel(kind, place_ref, *refs):
    *inputs, leaving_ref, staying_ref = refs
    if kind == "attn":
        side_ref, normed_ref, part_ref, g1_ref = inputs
        upper = dot_tn(side_ref[...], normed_ref[...])
        lower = dot_tn(part_ref[...], g1_ref[...])
        value = jnp.concatenate([upper, lower], axis=0)
    else:
        left_ref, right_ref = inputs
        value = dot_tn(left_ref[...], right_ref[...])
    value = value.astype(bf16)
    step = pl.program_id(0)

    @pl.when(step < 2)
    def _():
        leaving_ref[...] = value

    @pl.when(step >= 2)
    def _():
        staying_ref[...] = value


def grads(kind, place, arrays, width):
    rows = arrays[1].shape[0]

    def part_at(i):
        return jnp.where(i < 2, 2 * i + 1, 2 * i - 4)

    part = pl.BlockSpec((rows, width), lambda i, s: (0, part_at(i)))

    def of_part(a):
        return pl.BlockSpec((None, *a.shape[1:]), lambda i, s: (part_at(i), 0, 0))

    if kind == "attn":
        side, normed, attended, g1 = arrays
        specs = [of_part(side), whole(normed), of_part(attended), whole(g1)]
    elif kind == "up":
        specs = [whole(arrays[0]), part]
    else:
        specs = [part, whole(arrays[1])]
    block = (None, width, width)
    outs = [
        ((2, width, width), bf16, pl.BlockSpec(block, lambda i, s: (jnp.minimum(i, 1), 0, 0))),
        ((2, width, width), bf16, pl.BlockSpec(block, lambda i, s: (jnp.maximum(i - 2, 0), 0, 0))),
    ]
    return call(
        partial(grad_kernel, kind), "grads_" + kind, place, 4, list(zip(arrays, specs)), outs
    )


def emit_kernel(attention, aliased, place_ref, mine_ref, other_ref, *refs):
    outs = refs[aliased:]
    half, width = mine_ref.shape
    upper = place_ref[2] == 1
    mine, other = mine_ref[...].astype(f32), other_ref[...].astype(f32)
    low, high = jnp.where(upper, other, mine), jnp.where(upper, mine, other)
    if attention:
        qkv_ref, out_ref = outs
        share = width // 4
        qkv_ref[0, 0], qkv_ref[0, 1] = low[:share], low[share:]
        qkv_ref[0, 2], out_ref[0] = high[:share], high[share:]
    else:
        outs[0][0, :half] = low
        outs[0][0, half:] = high


def emit(place, layer, attention, summed, earlier):
    width = summed[0].shape[1]
    share = width // 4
    if attention:
        outs = [
            ((2, 3, share, width), f32, pl.BlockSpec((1, 3, share, width), lambda i, s: (layer, 0, 0, 0))),
            ((2, share, width), f32, pl.BlockSpec((1, share, width), lambda i, s: (layer, 0, 0))),
        ]
    else:
        outs = [((2, width, width), f32, pl.BlockSpec((1, width, width), lambda i, s: (layer, 0, 0)))]
    operands = [(a, whole(a)) for a in summed]
    aliases = {}
    if earlier is not None:
        aliases = {3 + n: n for n in range(len(earlier))}
        operands += [(e, pl.BlockSpec(memory_space=pl.ANY)) for e in earlier]
    return call(
        partial(emit_kernel, attention, len(aliases)), "emit", place, 1, operands, outs, aliases=aliases
    )


def head_swap(values, distance):
    count = lax.axis_size("head")
    return lax.ppermute(values, "head", [(i, i ^ distance) for i in range(count)])


def clip_swap(values, distance):
    count = lax.axis_size("clip")
    return lax.ppermute(values, "clip", [(i, i ^ distance) for i in range(count)])


class Order:
    def __init__(self):
        self.last = ()
        self.pending = []

    def run(self, step, *values):
        values, _ = lax.optimization_barrier((values, self.last))
        out = step(*values)
        self.last = (jax.tree.leaves(out)[0],)
        return out

    def send(self, swap, values, distance):
        values, _ = lax.optimization_barrier((values, self.last))
        out = swap(values, distance)
        self.pending.append(out)
        return out

    def close(self):
        self.last = self.last + tuple(self.pending)
        self.pending = []


def split_halves(total, upper):
    half = total.shape[-2] // 2
    low, high = total[..., :half, :], total[..., half:, :]
    return jnp.where(upper, low, high).astype(bf16), jnp.where(upper, high, low).astype(bf16)


def join_halves(mine, other, upper):
    return jnp.concatenate(
        [jnp.where(upper, other, mine), jnp.where(upper, mine, other)], axis=0
    )


class Pack:
    def __init__(self, order, leaving, staying, halving=True, late=False):
        self.order = order
        self.late = late
        self.out, self.kept = leaving, staying
        levels = lax.axis_size("clip").bit_length() - 1
        clip = lax.axis_index("clip")
        self.uppers = [((clip >> n) & 1) == 1 for n in range(levels)]
        depth = levels - 1 if halving else 1
        down = [("halve", n) for n in range(depth)]
        level = [("all", n) for n in range(depth, levels)]
        up = [("join", n) for n in reversed(range(depth))]
        if late:
            self.stages = ["core"] + down + ["across"] + level + up
        else:
            self.stages = ["core", "across"] + down + level + up
        self.at = 0
        self.prepared = False

    def prepare(self):
        if self.prepared:
            return
        self.prepared = True
        stage = self.stages[self.at]
        run = self.order.run
        if stage == "core":
            self.leaving = self.out
        elif self.late and stage == "across":

            def parted(total, moved):
                total = total.astype(f32) + moved.astype(f32)
                return total[1].astype(bf16), total[0].astype(bf16)

            self.leaving, self.sum = run(parted, self.sum, self.moved)
        elif self.late and self.at == 1:
            upper = self.uppers[stage[1]]

            def halved(kept, near):
                return split_halves(kept.astype(f32) + near.astype(f32), upper)

            self.leaving, self.sum = run(halved, self.kept, self.near)
        elif stage == "across":
            self.leaving = run(
                lambda kept, near: (kept[1].astype(f32) + near[1].astype(f32)).astype(bf16),
                self.kept, self.near,
            )
        else:
            kind, level = stage
            upper = self.uppers[level]
            if self.at == 2 and not self.late:
                start = lambda kept, near, moved: (
                    kept[0].astype(f32) + near[0].astype(f32) + moved.astype(f32)
                )
                values = (self.kept, self.near, self.moved)
            else:
                start = lambda total, moved: total.astype(f32) + moved.astype(f32)
                values = (self.sum, self.moved)
            if kind == "halve":
                self.leaving, self.sum = run(lambda *v: split_halves(start(*v), upper), *values)
            elif kind == "all" or self.stages[self.at - 1][0] == "all":
                self.leaving = self.sum = run(lambda *v: start(*v).astype(bf16), *values)
            else:
                before = self.uppers[self.stages[self.at - 1][1]]
                self.leaving = self.sum = run(
                    lambda mine, other: join_halves(mine, other, before), self.sum, self.moved
                )

    def launch(self):
        stage = self.stages[self.at]
        send = self.order.send
        if stage == "core":
            self.near = send(head_swap, self.leaving, 1)
        elif stage == "across":
            self.moved = send(head_swap, self.leaving, 2)
        else:
            self.moved = send(clip_swap, self.leaving, 1 << stage[1])
        self.at += 1
        self.prepared = False

    def done(self):
        return self.at == len(self.stages)

    def whole(self):
        assert self.done()
        return self.sum, self.moved


def on_device(
    tokens,
    frame_counts,
    token_mask,
    targets,
    norm_gain,
    norm_bias,
    w_qkv,
    qv_bias,
    w_out,
    vec_bias,
    w_up,
    up_bias,
    w_down,
    code_head,
):
    head_index = lax.axis_index("head")
    width = tokens.shape[1]
    share = w_out.shape[1]
    upper = lax.axis_index("clip") & 1
    place = jnp.stack(
        [head_index.astype(jnp.int32), frame_counts[0], upper.astype(jnp.int32)]
    )
    order = Order()

    def tied(values, *after):
        return lax.optimization_barrier((values, after))[0]

    clip_count = lax.axis_size("clip")
    own_small = jnp.concatenate([up_bias, qv_bias.reshape(1, width)], axis=0)
    clip_index = lax.axis_index("clip")

    def chunk(matrix):
        piece = matrix.shape[0] // clip_count
        return lax.dynamic_slice_in_dim(matrix, clip_index * piece, piece, 0)

    def over_clips(chunk_across):
        return lax.all_gather(chunk_across, "clip", axis=0, tiled=True)

    y_place, z_place = clip_index & 1, (clip_index >> 1) & 1

    def quarter(matrix):
        rows = matrix.shape[0] // 4
        return lax.dynamic_slice_in_dim(matrix, (2 * y_place + z_place) * rows, rows, 0)

    def along_y(first):
        return jnp.concatenate([first, clip_swap(first, 1)], axis=0)

    def by_place(pair, others):
        rows = pair.shape[0] // 2
        pieces = []
        for y in range(2):
            for z in range(2):
                same = z_place == z
                mine = jnp.where(same, pair[:rows], others[:rows])
                next_one = jnp.where(same, pair[rows:], others[rows:])
                pieces.append(jnp.where(y_place == y, mine, next_one))
        return jnp.concatenate(pieces, axis=0)

    def attn_pack(layer):
        transposed = w_qkv[layer].swapaxes(1, 2).reshape(-1, width)
        return jnp.concatenate([transposed, w_out[layer]], axis=0)

    def spread(own, across):
        return [own, head_swap(own, 1), across, head_swap(across, 1)]

    up_quarter = head_swap(quarter(w_up[0]), 2)
    down_quarter = head_swap(quarter(w_down[0]), 2)
    up_quarter, down_quarter, own, own_small = lax.optimization_barrier(
        (up_quarter, down_quarter, attn_pack(0), own_small)
    )
    smalls = spread(own_small, head_swap(own_small, 2))
    later = jnp.concatenate([chunk(w_up[1]), chunk(w_down[1])], axis=0)
    marks = (2 * targets + token_mask).reshape(4, WINDOW)
    up_pair, down_pair = along_y(up_quarter), along_y(down_quarter)
    up_x = by_place(up_pair, clip_swap(up_pair, 2))
    across, later, marks, place, up_x, down_pair = lax.optimization_barrier(
        (head_swap(own, 2), later, marks, place, up_x, down_pair)
    )
    attn = [spread(own, across), None]
    order.last = (across,)
    down_others = order.send(clip_swap, down_pair, 2)
    chunk_1 = order.send(head_swap, later, 2)
    order.last = (smalls[1], smalls[3], attn[0][1], attn[0][3])
    ups = [w_up, order.send(head_swap, w_up, 1)]
    downs = [w_down, order.send(head_swap, w_down, 1)]
    up_diagonal = order.send(head_swap, up_x, 1)
    packs = [None, None]

    def feed_packs(up_x, down_x):
        return (
            ups, downs,
            [up_x, order.send(head_swap, up_x, 1)],
            [down_x, order.send(head_swap, down_x, 1)],
        )

    kept = []
    inputs = (tokens, marks)
    for layer in range(2):
        x, normed, qkv, att, lse, att_parts, *mark_pieces = order.run(
            lambda *a: attend(layer, place, a, norm_gain, norm_bias, smalls, attn[layer]), *inputs
        )
        order.close()
        if layer == 0:
            gathered = over_clips(tied(chunk_1, x))
            marks = [mark_pieces[0]] + [head_swap(mark_pieces[k], k) for k in (1, 2, 3)]
            down_x = order.run(by_place, down_pair, down_others)
            packs[0] = (ups, downs, [up_x, up_diagonal], [down_x, order.send(head_swap, down_x, 1)])
            order.close()
            own = attn_pack(1)
            attn_across = order.send(head_swap, own, 2)
            attn[1] = [own, head_swap(own, 1), attn_across]
        stream, normed2, active, slope, *outs = order.run(
            lambda a, b: feed(
                layer, place, a, b, attn[layer], vec_bias, norm_gain, norm_bias, smalls, packs[layer]
            ),
            x, att,
        )
        kept.append((x, normed, qkv, att_parts, lse, stream, normed2, active, slope))
        if layer == 0:
            order.close()
            pieces = gathered.reshape(clip_count, 2, -1, width)
            attn[1].append(order.send(head_swap, attn_across, 1))
            inputs = [outs[0]] + [order.send(head_swap, outs[k], k) for k in (1, 2, 3)]
            inputs = [p.reshape(4, 4, CELL, width) for p in inputs]
            order.close()
            packs[1] = feed_packs(pieces[:, 0].reshape(-1, width), pieces[:, 1].reshape(-1, width))
    grad, loss_sum, *parts = order.run(
        lambda a: code_loss(place, a, code_head, marks, active), outs[0]
    )
    down_1 = Pack(order, *parts, halving=False)

    def run_feed_back(layer, grad):
        x, normed, qkv, att, lse, stream, normed2, active, slope = kept[layer]
        return order.run(
            lambda a: feed_back(layer, place, a, slope, stream, normed2, norm_gain, packs[layer]), grad
        )

    def run_attend_back(layer, grad_next, g1):
        x, normed, qkv, att, lse, *_ = kept[layer]
        return order.run(
            lambda a, b: attend_back(
                layer, place, a, b, x, qkv, lse, norm_gain, attn[layer], normed, att
            ),
            grad_next, g1,
        )

    def pack(kind, *arrays, **options):
        parts = order.run(lambda *a: grads(kind, place, a, width), *arrays)
        return Pack(order, *parts, **options)

    def move(*ones):
        for one in ones:
            one.prepare()
        for one in ones:
            one.launch()

    move(down_1)
    order.close()
    move(down_1)
    grad_next, g1, feed_sum_1, *parts = run_feed_back(1, grad)
    up_1 = Pack(order, *parts, halving=False)
    order.close()
    move(up_1)
    down_1.prepare()
    order.close()
    move(up_1, down_1)
    side, *outs, attn_sum_1 = run_attend_back(1, grad_next, g1)
    order.close()

    grad = [outs[0]] + [order.send(head_swap, outs[k], k) for k in (1, 2, 3)]
    grad = [p.reshape(4, BAND, width) for p in grad]
    move(up_1, down_1)
    attn_1 = pack("attn", side, kept[1][1], kept[1][3], g1, late=True)
    order.close()

    move(attn_1)
    g2 = jnp.stack(grad, axis=1).reshape(-1, width)
    down_0 = pack("down", kept[0][7], g2)
    order.close()
    move(down_0)
    for one in (attn_1, down_1, up_1):
        one.prepare()
    order.close()
    move(down_0, attn_1, down_1, up_1)
    grad_next, g1, feed_sum_0, *parts = run_feed_back(0, g2)
    up_0 = Pack(order, *parts)
    order.close()
    move(up_0)
    for one in (down_0, attn_1, up_1, down_1):
        one.prepare()
    order.close()
    move(up_0, down_0, attn_1, up_1, down_1)
    grad_input, attn_sum_0, *parts = run_attend_back(0, grad_next, g1)
    attn_0 = Pack(order, *parts)
    order.close()
    move(attn_0)
    move(attn_1)
    for one in (up_0, down_0, up_1):
        one.prepare()
    order.close()
    move(attn_0, up_0, down_0, attn_1, up_1)
    order.close()

    packed = jnp.concatenate([feed_sum_0, feed_sum_1, attn_sum_0, attn_sum_1, loss_sum], axis=0)
    swaps = [(head_swap, 1), (head_swap, 2)]
    swaps += [(clip_swap, 1 << n) for n in range(clip_count.bit_length() - 1)]

    def pack_step():
        swap, distance = swaps.pop(0)
        return packed + order.send(swap, packed, distance)

    ready = {}

    def write(one, layer, attention, earlier):
        ready[one] = order.run(lambda *a: emit(place, layer, attention, a, earlier), *one.whole())

    late = [down_1, up_1]
    moving = [attn_0, up_0, down_0]
    wait = 0
    while swaps or not all(one.done() for one in moving + late + [attn_1]):
        move(*[one for one in moving + [attn_1] + late if not one.done()])
        wait += 1
        if swaps:
            packed = pack_step()
        for one in late:
            if one.done() and one not in ready:
                write(one, 1, False, None)
                break
        if attn_1.done() and wait > 2 and attn_1 not in ready:
            write(attn_1, 1, True, None)
        for one, earlier in ((down_0, down_1), (up_0, up_1)):
            if one.done() and one not in ready and earlier in ready and one.closed:
                write(one, 0, False, ready[earlier])
                break
        order.close()
        for one in moving:
            one.closed = one.done()

    for one, layer, attention, earlier in (
        (down_1, 1, False, None), (up_1, 1, False, None), (attn_1, 1, True, None),
        (down_0, 0, False, down_1), (up_0, 0, False, up_1), (attn_0, 0, True, attn_1),
    ):
        if one not in ready:
            write(one, layer, attention, ready.get(earlier))

    attn_out, up_out, down_out = ready[attn_0], ready[up_0], ready[down_0]

    feed_sums = packed[:16].reshape(2, 8, width)
    attn_sums = packed[16:32].reshape(2, 8, width)
    loss_total = packed[32, 0]
    own_feed = lax.dynamic_index_in_dim(feed_sums, head_index, 1, keepdims=False)
    own_attn = lax.dynamic_index_in_dim(attn_sums, head_index, 1, keepdims=False)
    slot_total = clip_count * frame_counts.shape[0] * FRAMES * SIDE * SIDE

    return (
        loss_total / slot_total,
        grad_input,
        jnp.stack([attn_sums[:, 4], feed_sums[:, 4]], axis=1),
        jnp.stack([attn_sums[:, 5], feed_sums[:, 5]], axis=1),
        attn_out[0].swapaxes(2, 3),
        own_attn[:, : 2 * share].reshape(2, 2, share),
        attn_out[1],
        jnp.stack([feed_sums[:, 7], feed_sums[:, 6]], axis=1),
        up_out[0],
        own_feed,
        down_out[0],
    )


def solution(mesh):
    placed = (
        P(("clip", "head"), None),
        P("clip"),
        P(("clip", "head")),
        P(("clip", "head")),
        P(),
        P(),
        P(None, None, None, "head"),
        P(None, None, "head"),
        P(None, "head", None),
        P(),
        P(None, None, "head"),
        P(None, "head"),
        P(None, "head", None),
        P(),
    )
    return jax.shard_map(
        on_device,
        mesh=mesh,
        in_specs=placed,
        out_specs=(
            P(),
            P(("clip", "head"), None),
            P(),
            P(),
            P(None, None, None, "head"),
            P(None, None, "head"),
            P(None, "head", None),
            P(),
            P(None, None, "head"),
            P(None, "head"),
            P(None, "head", None),
        ),
        check_vma=False,
    )
```

```python
from functools import partial

import jax
import jax.numpy as jnp
from jax import lax
from jax.experimental import pallas as pl
from jax.experimental.pallas import tpu as pltpu
from jax.sharding import PartitionSpec as P

HD = 64
FRAMES = 16
SIDE = 16
TUBE = 4
WINDOW = 256
PAIR = 128
BAND = 64
CELL = 16
LSE_ROWS = 16
SMALLS = 3

epsilon = 1e-06
masked_score = -1e30
f32 = jnp.float32
bf16 = jnp.bfloat16
VMEM_LIMIT = 44 * 1024 * 1024
TIMES = {
    "attend": 17, "feed": 23, "code_loss": 18, "feed_back": 26, "attend_back": 25,
    "grads_down": 10, "grads_attn": 11, "emit": 3,
}
SCALE = 1.0


def cost_of(name):
    time = TIMES[name] * SCALE
    return pl.CostEstimate(flops=int(time * 1.15e9), bytes_accessed=int(time * 3.6e6), transcendentals=0)


def dot(a, b):
    return lax.dot_general(a, b, (((1,), (0,)), ((), ())), preferred_element_type=f32)


def dot_nt(a, b):
    return lax.dot_general(a, b, (((1,), (1,)), ((), ())), preferred_element_type=f32)


def dot_tn(a, b):
    return lax.dot_general(a, b, (((0,), (0,)), ((), ())), preferred_element_type=f32)


def statistics(stream):
    centre = jnp.mean(stream, axis=-1, keepdims=True)
    centred = stream - centre
    spread = jnp.mean(centred * centred, axis=-1, keepdims=True)
    scale = lax.rsqrt(spread + epsilon)
    return centred * scale, scale


def by_eight(values):
    rows, columns = values.shape
    return jnp.sum(values.reshape(rows // 8, 8, columns), axis=0)


def gather_sums(acc_ref, values):
    first = pl.program_id(0) == 0
    parts = jnp.concatenate([by_eight(v) for v in values], axis=1)

    @pl.when(first)
    def _():
        acc_ref[...] = parts

    @pl.when(jnp.logical_not(first))
    def _():
        acc_ref[...] += parts


ORDER = (1, 3, 0, 2)


def step_rows():
    return pl.ds(pl.multiple_of(pl.program_id(0) * WINDOW, WINDOW), WINDOW)


def put_parts(leaving_ref, staying_ref, buf, sem, gradient_of):
    copies = []
    for n, k in enumerate(ORDER):
        buf[n] = gradient_of(k).astype(bf16)
        target = (leaving_ref if n < 2 else staying_ref).at[n % 2]
        copy = pltpu.make_async_copy(buf.at[n], target, sem.at[n])
        copy.start()
        copies.append(copy)
    for copy in copies:
        copy.wait()


def parts_outs(width):
    return [((2, width, width), bf16, pl.BlockSpec(memory_space=pl.ANY))] * 2


def parts_scratch(width):
    return [pltpu.VMEM((4, width, width), bf16), pltpu.SemaphoreType.DMA((4,))]


def last_step():
    return pl.program_id(0) == pl.num_programs(0) - 1


def norm_back(stream, gain, grad):
    normal, scale = statistics(stream)
    scaled = grad * gain
    mean_plain = jnp.mean(scaled, axis=-1, keepdims=True)
    mean_normal = jnp.mean(scaled * normal, axis=-1, keepdims=True)
    inner = scale * (scaled - mean_plain - normal * mean_normal)
    return inner, grad * normal


def gelu_both(hidden):
    root = 0.7978845608028654
    cubic = 0.044715
    square = hidden * hidden
    bend = jnp.tanh(hidden * (root + root * cubic * square))
    rise = 0.5 + 0.5 * bend
    active = hidden * rise
    slope = rise + (active - active * rise) * (2.0 * root + 6.0 * root * cubic * square)
    return active.astype(bf16), slope.astype(bf16)


def allowed_of(place_ref):
    head_index = place_ref[0]
    frame_count = place_ref[1]

    def valid(axis):
        position = lax.broadcasted_iota(jnp.int32, (WINDOW, WINDOW), axis)
        frame = 4 * ((position >> 6) ^ head_index) + ((position >> 4) & 3)
        return frame < frame_count

    return jnp.logical_or(valid(0), jnp.logical_not(valid(1)))


def shuffle_of(place_ref, axis):
    arranged = lax.broadcasted_iota(jnp.int32, (WINDOW, WINDOW), axis)
    plain = lax.broadcasted_iota(jnp.int32, (WINDOW, WINDOW), 1 - axis)
    band = (arranged >> 6) ^ place_ref[0]
    source = band * BAND + ((arranged >> 2) & 3) * 16 + ((arranged >> 4) & 3) * 4 + (arranged & 3)
    return (source == plain).astype(f32).astype(bf16)


def small_rows(ref, start, count=1):
    terms = [ref[SMALLS * n + start : SMALLS * n + start + count, :].astype(f32) for n in range(3)]
    return terms[0] + terms[1] + terms[2]


def small_of(a):
    rows, width = a.shape
    return pl.BlockSpec((CELL, width), lambda i, s: (rows // CELL - 1, 0))


def assemble_qkv(packs, scratch):
    width = scratch.shape[1]
    share = width // 4
    for k in range(4):
        for j in range(3):
            start = j * width + k * share
            scratch[start : start + share, :] = packs[k][j * share : (j + 1) * share, :]


def assemble_out(packs, scratch):
    share = scratch.shape[0] // 4
    for k in range(4):
        scratch[k * share : (k + 1) * share, :] = packs[k][3 * share : 4 * share, :]


def stack_heads(pair):
    low = lax.broadcasted_iota(jnp.int32, pair.shape, 1) < HD
    zero = jnp.zeros((), bf16)
    return jnp.concatenate([jnp.where(low, pair, zero), jnp.where(low, zero, pair)], axis=0)


def attend_core(qkv, allowed, att_ref, lse_ref, part_ref):
    width = att_ref.shape[1]
    pairs = width // PAIR

    def part(j, pair):
        return qkv[:, j * width + pair * PAIR : j * width + (pair + 1) * PAIR]

    def scores_of(pair):
        query = part(0, pair) * jnp.asarray(HD ** (-0.5), bf16)
        return dot_nt(stack_heads(part(1, pair)), query)

    ahead = scores_of(0)
    for pair in range(pairs):
        scores = ahead
        if pair + 1 < pairs:
            ahead = scores_of(pair + 1)
        probs = []
        for half in range(2):
            mine = scores[half * WINDOW : (half + 1) * WINDOW]
            if allowed is not None:
                mine = jnp.where(allowed, mine, masked_score)
            top = jnp.max(mine, axis=0, keepdims=True)
            terms = jnp.exp(mine - top)
            total = jnp.sum(terms, axis=0, keepdims=True)
            probs.append((terms * (1.0 / total)).astype(bf16))
            head = 2 * pair + half
            lse_ref[head : head + 1, :] = top + jnp.log(total)
        out = dot_tn(jnp.concatenate(probs, axis=0), stack_heads(part(2, pair)))
        att_ref[:, pair * PAIR : (pair + 1) * PAIR] = out.astype(bf16)
    share = width // 4
    for k in range(4):
        part_ref[k] = att_ref[:, k * share : (k + 1) * share]


def attend_kernel(layer, place_ref, *refs):
    if layer == 0:
        tokens_ref, marks_ref, *refs = refs
        shuffle = shuffle_of(place_ref, 0)
        stream = dot(shuffle, tokens_ref[...])
    else:
        pieces, refs = refs[:4], refs[4:]
        stream = jnp.concatenate(
            [p[...].reshape(BAND, p.shape[-1]) for p in pieces], axis=0
        ).astype(f32)
    gain_ref, shift_ref, s0, s1, s2, s3, p0, p1, p2, p3, x_ref, normed_ref, qkv_ref, att_ref, lse_ref, part_ref, *refs = refs
    *mark_refs, scratch = refs
    share = scratch.shape[1] // 4

    @pl.when(pl.program_id(0) == 0)
    def _():
        assemble_qkv((p0, p1, p2, p3), scratch)

    if layer == 0:
        given = marks_ref[pl.ds(pl.program_id(0), 1), :]
        high = given >> 4
        both = jnp.concatenate([high, given - 16 * high], axis=0).astype(f32).astype(bf16)
        both = dot(both, shuffle_of(place_ref, 1))
        marks = 16.0 * both[0:1] + both[1:2]
        for k in range(4):
            mark_refs[k][pl.ds(pl.program_id(0), 1), :] = marks[:, k * BAND : (k + 1) * BAND]
    x_ref[...] = stream.astype(bf16)
    normal, _ = statistics(stream)
    normed = (normal * gain_ref[layer, 0:1] + shift_ref[layer, 0:1]).astype(bf16)
    normed_ref[...] = normed
    start = 2 * layer * share
    smalls = [small_rows(r, 2) for r in (s0, s1, s2, s3)]
    bias = jnp.concatenate(
        [r[:, start : start + share] for r in smalls]
        + [jnp.zeros((1, 4 * share), f32)]
        + [r[:, start + share : start + 2 * share] for r in smalls],
        axis=1,
    )
    qkv = (dot_nt(normed, scratch[...]) + bias).astype(bf16)
    qkv_ref[...] = qkv
    allowed = allowed_of(place_ref) if layer == 1 else None
    attend_core(qkv, allowed, att_ref, lse_ref, part_ref)


def whole(array):
    zeros = (0,) * array.ndim
    return pl.BlockSpec(array.shape, lambda i, s: zeros, pipeline_mode=pl.Buffered(1))


def rows_of(columns, rows=WINDOW):
    return pl.BlockSpec((rows, columns), lambda i, s: (i, 0))


def parts_of(columns):
    return pl.BlockSpec((4, WINDOW, columns), lambda i, s: (0, i, 0))


def tube_of(columns):
    return pl.BlockSpec((4, 1, CELL, columns), lambda i, s: (0, i, 0, 0))


def sums_of(columns):
    return pl.BlockSpec((8, columns), lambda i, s: (0, 0))


def call(kernel, name, place, steps, operands, outs, scratch=(), aliases={}):
    return pl.pallas_call(
        kernel,
        grid_spec=pltpu.PrefetchScalarGridSpec(
            num_scalar_prefetch=1,
            grid=(steps,),
            in_specs=[spec for _, spec in operands],
            out_specs=[spec for _, _, spec in outs],
            scratch_shapes=list(scratch),
        ),
        out_shape=[jax.ShapeDtypeStruct(shape, dtype) for shape, dtype, _ in outs],
        compiler_params=pltpu.CompilerParams(vmem_limit_bytes=VMEM_LIMIT),
        cost_estimate=cost_of(name),
        input_output_aliases=aliases,
        name=name,
    )(place, *[array for array, _ in operands])


def attend(layer, place, inputs, gain, shift, smalls, packs):
    width = gain.shape[-1]
    rows = 4 * WINDOW
    if layer == 0:
        tokens, marks = inputs
        first = [(tokens, rows_of(width)), (marks, whole(marks))]
    else:
        first = [(p, tube_of(width)) for p in inputs]
    operands = first + [(a, whole(a)) for a in (gain, shift)]
    operands += [(a, small_of(a)) for a in smalls] + [(a, whole(a)) for a in packs]
    outs = [
        ((rows, width), bf16, rows_of(width)),
        ((rows, width), bf16, rows_of(width)),
        ((rows, 3 * width), bf16, rows_of(3 * width)),
        ((rows, width), bf16, rows_of(width)),
        ((4 * LSE_ROWS, WINDOW), f32, rows_of(WINDOW, LSE_ROWS)),
        ((4, rows, width // 4), bf16, parts_of(width // 4)),
    ]
    if layer == 0:
        outs += [((4, BAND), f32, pl.BlockSpec((4, BAND), lambda i, s: (0, 0)))] * 4
    return call(
        partial(attend_kernel, layer), "attend", place, 4, operands, outs,
        [pltpu.VMEM((3 * width, width), bf16)],
    )


def attend_back_core(qkv, grad, lse_ref, allowed):
    width = grad.shape[1]
    pairs = width // PAIR

    def part(j, pair):
        return qkv[:, j * width + pair * PAIR : j * width + (pair + 1) * PAIR]

    def first_of(pair):
        query = part(0, pair) * jnp.asarray(HD ** (-0.5), bf16)
        grad_part = grad[:, pair * PAIR : (pair + 1) * PAIR]
        keys = stack_heads(part(1, pair))
        scores = dot_nt(keys, query)
        grad_probs = dot_nt(stack_heads(part(2, pair)), grad_part)
        return query, grad_part, keys, scores, grad_probs

    low = lax.broadcasted_iota(jnp.int32, (WINDOW, PAIR), 1) < HD
    results = [[], [], []]
    ahead = first_of(0)
    for pair in range(pairs):
        query, grad_part, keys, scores, grad_probs = ahead
        if pair + 1 < pairs:
            ahead = first_of(pair + 1)
        all_probs, all_scores = [], []
        for half in range(2):
            rows = slice(half * WINDOW, (half + 1) * WINDOW)
            mine = scores[rows]
            if allowed is not None:
                mine = jnp.where(allowed, mine, masked_score)
            head = 2 * pair + half
            probs = jnp.exp(mine - lse_ref[head : head + 1, :])
            grad_mine = grad_probs[rows]
            delta = jnp.sum(probs * grad_mine, axis=0, keepdims=True)
            all_probs.append(probs.astype(bf16))
            all_scores.append((probs * (grad_mine - delta)).astype(bf16))
        probs = jnp.concatenate(all_probs, axis=0)
        grad_scores = jnp.concatenate(all_scores, axis=0)
        grad_query = dot_tn(grad_scores, keys) * HD ** (-0.5)
        grad_key = dot(grad_scores, query)
        grad_value = dot(probs, grad_part)
        results[0].append(grad_query.astype(bf16))
        results[1].append(jnp.where(low, grad_key[:WINDOW], grad_key[WINDOW:]).astype(bf16))
        results[2].append(jnp.where(low, grad_value[:WINDOW], grad_value[WINDOW:]).astype(bf16))
    return [jnp.concatenate(part, axis=1) for part in results]


def attend_back_kernel(layer, place_ref, *refs):
    (stream_ref, g1_ref, x_ref, qkv_ref, lse_ref, gain_ref, p0, p1, p2, p3, *outs) = refs
    if layer == 1:
        side_ref, *outs = outs
        pieces, outs = outs[:4], outs[4:]
        sums_ref, scratch, out_scratch, acc = outs
        rows = slice(None)
    else:
        (
            normed_ref, part_ref, final_ref, sums_ref, leaving_ref, staying_ref,
            scratch, out_scratch, acc, side_ref, all_normed, all_parts, all_g1, buf, sem,
        ) = outs
        rows = step_rows()
        all_normed[rows, :] = normed_ref[...]
        all_g1[rows, :] = g1_ref[...]
        for k in range(4):
            all_parts[k, rows, :] = part_ref[k]
    width = stream_ref.shape[1]
    share = width // 4

    @pl.when(pl.program_id(0) == 0)
    def _():
        assemble_qkv((p0, p1, p2, p3), scratch)
        assemble_out((p0, p1, p2, p3), out_scratch)

    grad_att = dot_nt(g1_ref[...], out_scratch[...]).astype(bf16)
    allowed = allowed_of(place_ref) if layer == 1 else None
    parts = attend_back_core(qkv_ref[...], grad_att, lse_ref, allowed)
    for k in range(4):
        for j in range(3):
            side_ref[k, rows, j * share : (j + 1) * share] = parts[j][:, k * share : (k + 1) * share]
    joined = jnp.concatenate(parts, axis=1)
    grad_normed = dot(joined, scratch[...])
    inner, scaled = norm_back(x_ref[...].astype(f32), gain_ref[layer, 0:1], grad_normed)
    gather_sums(acc, [parts[0].astype(f32), parts[2].astype(f32), scaled, grad_normed])
    stream = stream_ref[...] + inner
    if layer == 1:
        for k in range(4):
            pieces[k][...] = (
                stream[k * BAND : (k + 1) * BAND].astype(bf16).reshape(4, 1, CELL, width)
            )
    else:
        shuffle = shuffle_of(place_ref, 1)
        high = stream.astype(bf16)
        low = (stream - high.astype(f32)).astype(bf16)
        final_ref[...] = dot(shuffle, high) + dot(shuffle, low)

    @pl.when(last_step())
    def _():
        total = jnp.sum(acc[...], axis=0, keepdims=True)
        sums_ref[...] = jnp.zeros(sums_ref.shape, f32)
        for k in range(4):
            query = total[:, k * share : (k + 1) * share]
            value = total[:, width + k * share : width + (k + 1) * share]
            sums_ref[pl.ds(place_ref[0] ^ k, 1), : 2 * share] = jnp.concatenate([query, value], axis=1)
        sums_ref[4:5, :] = total[:, 2 * width : 3 * width]
        sums_ref[5:6, :] = total[:, 3 * width :]
        if layer == 0:

            def gradient_of(k):
                upper = dot_tn(side_ref[k], all_normed[...])
                lower = dot_tn(all_parts[k], all_g1[...])
                return jnp.concatenate([upper, lower], axis=0)

            put_parts(leaving_ref, staying_ref, buf, sem, gradient_of)


def attend_back(layer, place, stream, g1, x, qkv, lse, gain, packs, normed, attended):
    rows, width = stream.shape
    share = width // 4
    operands = [
        (stream, rows_of(width)),
        (g1, rows_of(width)),
        (x, rows_of(width)),
        (qkv, rows_of(3 * width)),
        (lse, rows_of(WINDOW, LSE_ROWS)),
    ] + [(a, whole(a)) for a in (gain, *packs)]
    sums = [((8, width), f32, sums_of(width))]
    scratch = [
        pltpu.VMEM((3 * width, width), bf16), pltpu.VMEM((width, width), bf16), pltpu.VMEM((8, 4 * width), f32)
    ]
    if layer == 1:
        outs = [((4, rows, 3 * share), bf16, parts_of(3 * share))]
        outs = outs + [((4, 4, CELL, width), bf16, tube_of(width))] * 4 + sums
    else:
        operands += [(normed, rows_of(width)), (attended, parts_of(share))]
        outs = [((rows, width), f32, rows_of(width))] + sums + parts_outs(width)
        scratch += [
            pltpu.VMEM((4, rows, 3 * share), bf16), pltpu.VMEM((rows, width), bf16),
            pltpu.VMEM((4, rows, share), bf16), pltpu.VMEM((rows, width), bf16),
        ] + parts_scratch(width)
    return call(partial(attend_back_kernel, layer), "attend_back", place, 4, operands, outs, scratch)


def feed_kernel(layer, place_ref, *refs):
    (
        x_ref, att_ref, a0, a1, a2, a3, vec_ref, gain_ref, shift_ref, s0, s1, s2, s3,
        u0, u1, u2, u3, d0, d1, d2, d3, stream_ref, normed_ref, active_ref, slope_ref, *outs
    ) = refs
    ups, downs = (u0, u1, u2, u3), (d0, d1, d2, d3)
    *pieces, scratch = outs
    width = x_ref.shape[1]

    @pl.when(pl.program_id(0) == 0)
    def _():
        share = width // 4
        for k, part in enumerate((a0, a1, a2, a3)):
            scratch[k * share : (k + 1) * share, :] = part[...]

    stream = x_ref[...].astype(f32) + dot(att_ref[...], scratch[...]) + vec_ref[layer, 0:1]
    stream_ref[...] = stream
    normal, _ = statistics(stream)
    normed = (normal * gain_ref[layer, 1:2] + shift_ref[layer, 1:2]).astype(bf16)
    normed_ref[...] = normed
    total = stream + vec_ref[layer, 1:2]
    units = u0.shape[1]
    ahead = dot(normed, ups[0][...])
    for k in range(4):
        hidden = ahead
        if k < 3:
            ahead = dot(normed, ups[k + 1][...])
        cut = slice(k * units, (k + 1) * units)
        active, slope = gelu_both(hidden + small_rows((s0, s1, s2, s3)[k], layer))
        active_ref[:, cut] = active
        slope_ref[:, cut] = slope
        total = total + dot(active, downs[k][...])
    total = total.astype(bf16)
    if layer == 0:
        for k in range(4):
            pieces[k][...] = total[k * BAND : (k + 1) * BAND].reshape(1, BAND, width)
    else:
        pieces[0][...] = total


def feed_specs(layer, packs):
    ups, downs, ups_across, downs_across = packs

    def of_layer(a):
        return (a, pl.BlockSpec(
            (None, *a.shape[1:]), lambda i, s: (layer, 0, 0), pipeline_mode=pl.Buffered(1)
        ))

    return [
        *[of_layer(a) for a in ups],
        *[(a, whole(a)) for a in ups_across],
        *[of_layer(a) for a in downs],
        *[(a, whole(a)) for a in downs_across],
    ]


def feed(layer, place, x, att, attn_packs, vecs, gain, shift, smalls, packs):
    rows, width = x.shape
    units = packs[0][0].shape[2]
    last = pl.BlockSpec((width // 4, width), lambda i, s: (3, 0))
    operands = (
        [(x, rows_of(width)), (att, rows_of(width))]
        + [(a, last) for a in attn_packs]
        + [(a, whole(a)) for a in (vecs, gain, shift)]
        + [(a, small_of(a)) for a in smalls]
        + feed_specs(layer, packs)
    )
    outs = [
        ((rows, width), f32, rows_of(width)),
        ((rows, width), bf16, rows_of(width)),
        ((rows, 4 * units), bf16, rows_of(4 * units)),
        ((rows, 4 * units), bf16, rows_of(4 * units)),
    ]
    if layer == 0:
        piece = pl.BlockSpec((1, BAND, width), lambda i, s: (i, 0, 0))
        outs = outs + [((4, BAND, width), bf16, piece)] * 4
    else:
        outs = outs + [((rows, width), bf16, rows_of(width))]
    return call(
        partial(feed_kernel, layer), "feed", place, 4, operands, outs,
        [pltpu.VMEM((width, width), bf16)],
    )


def loss_kernel(
    place_ref, final_ref, head_ref, m0, m1, m2, m3, active_ref, grad_ref, loss_ref, leaving_ref, staying_ref,
    acc, all_active, all_g2, buf, sem,
):
    logits = dot(final_ref[...], head_ref[...])
    spread = jnp.concatenate(
        [jnp.broadcast_to(m[f : f + 1, :], (CELL, BAND)) for m in (m0, m1, m2, m3) for f in range(4)],
        axis=0,
    )
    position = lax.broadcasted_iota(jnp.int32, (WINDOW, BAND), 0)
    lane = lax.broadcasted_iota(jnp.int32, (WINDOW, BAND), 1)
    mine = lane == pl.program_id(0) * CELL + (position & (CELL - 1))
    mark = jnp.sum(jnp.where(mine, spread, 0.0), axis=1, keepdims=True).astype(jnp.int32)
    place_of = lax.broadcasted_iota(jnp.int32, (WINDOW, 1), 0)
    frame = 4 * ((place_of >> 6) ^ place_ref[0]) + ((place_of >> 4) & 3)
    weight = jnp.where(frame < place_ref[1], (mark & 1).astype(f32), 0.0)
    top = jnp.max(logits, axis=1, keepdims=True)
    terms = jnp.exp(logits - top)
    total = jnp.sum(terms, axis=1, keepdims=True)
    code = lax.broadcasted_iota(jnp.int32, logits.shape, 1)
    chosen = code == (mark >> 1)
    picked = jnp.sum(jnp.where(chosen, logits, 0.0), axis=1, keepdims=True)
    entry = weight * (top + jnp.log(total) - picked)
    soft = terms * (1.0 / total)
    grad_logits = (weight * (soft - jnp.where(chosen, 1.0, 0.0))).astype(bf16)
    grad = dot_nt(grad_logits, head_ref[...])
    grad_ref[...] = grad
    all_g2[step_rows(), :] = grad.astype(bf16)
    all_active[step_rows(), :] = active_ref[...]
    gather_sums(acc, [jnp.broadcast_to(entry, (WINDOW, PAIR))])

    @pl.when(last_step())
    def _():
        total = jnp.sum(acc[...], axis=0, keepdims=True)
        loss_ref[...] = jnp.broadcast_to(total[:, :1], loss_ref.shape)
        width = grad_ref.shape[1]
        put_parts(
            leaving_ref, staying_ref, buf, sem,
            lambda k: dot_tn(all_active[:, k * width : (k + 1) * width], all_g2[...]),
        )


def code_loss(place, final, code_head, marks, active):
    rows, width = final.shape
    operands = [(final, rows_of(width))] + [(a, whole(a)) for a in (code_head, *marks)]
    operands += [(active, rows_of(active.shape[1]))]
    outs = [
        ((rows, width), f32, rows_of(width)),
        ((8, width), f32, sums_of(width)),
    ] + parts_outs(width)
    scratch = [
        pltpu.VMEM((8, PAIR), f32), pltpu.VMEM(active.shape, bf16), pltpu.VMEM((rows, width), bf16)
    ] + parts_scratch(width)
    return call(loss_kernel, "code_loss", place, 4, operands, outs, scratch)


def feed_back_kernel(layer, place_ref, *refs):
    if layer == 1:
        grad_ref, *refs = refs
        grad = grad_ref[...]
    else:
        grad_ref, *refs = refs
        grad = grad_ref[...].astype(f32)
    (
        slope_ref, stream_ref, normed_ref, gain_ref, u0, u1, u2, u3, d0, d1, d2, d3, next_ref, g1_ref,
        sums_ref, leaving_ref, staying_ref, acc, all_hidden, all_normed, buf, sem,
    ) = refs
    all_normed[step_rows(), :] = normed_ref[...]
    g2 = grad.astype(bf16)
    units = u0.shape[1]
    grad_normed = jnp.zeros(grad.shape, f32)
    sums = []
    ups, downs = (u0, u1, u2, u3), (d0, d1, d2, d3)
    ahead = dot_nt(g2, downs[0][...])
    for k in range(4):
        grad_active = ahead
        if k < 3:
            ahead = dot_nt(g2, downs[k + 1][...])
        cut = slice(k * units, (k + 1) * units)
        grad_hidden = (grad_active * slope_ref[:, cut].astype(f32)).astype(bf16)
        all_hidden[step_rows(), cut] = grad_hidden
        sums.append(grad_hidden.astype(f32))
        grad_normed = grad_normed + dot_nt(grad_hidden, ups[k][...])
    inner, scaled = norm_back(stream_ref[...], gain_ref[layer, 1:2], grad_normed)
    grad = grad + inner
    next_ref[...] = grad
    g1 = grad.astype(bf16)
    g1_ref[...] = g1
    gather_sums(acc, sums + [scaled, grad_normed, g2.astype(f32), g1.astype(f32)])

    @pl.when(last_step())
    def _():
        total = jnp.sum(acc[...], axis=0, keepdims=True)
        for k in range(4):
            sums_ref[pl.ds(place_ref[0] ^ k, 1), :] = total[:, k * units : (k + 1) * units]
            start = 4 * units + k * grad.shape[1]
            sums_ref[4 + k : 5 + k, :] = total[:, start : start + grad.shape[1]]
        put_parts(
            leaving_ref, staying_ref, buf, sem,
            lambda k: dot_tn(all_normed[...], all_hidden[:, k * units : (k + 1) * units]),
        )


def feed_back(layer, place, grad, slope, stream, normed, gain, packs):
    rows, width = stream.shape
    units = packs[0][0].shape[2]
    operands = (
        [(grad, rows_of(width)), (slope, rows_of(4 * units)), (stream, rows_of(width)), (normed, rows_of(width))]
        + [(gain, whole(gain))]
        + feed_specs(layer, packs)
    )
    outs = [
        ((rows, width), f32, rows_of(width)),
        ((rows, width), bf16, rows_of(width)),
        ((8, width), f32, sums_of(width)),
    ] + parts_outs(width)
    scratch = [
        pltpu.VMEM((8, 4 * units + 4 * width), f32),
        pltpu.VMEM((rows, 4 * units), bf16),
        pltpu.VMEM((rows, width), bf16),
    ] + parts_scratch(width)
    return call(partial(feed_back_kernel, layer), "feed_back", place, 4, operands, outs, scratch)


def grad_kernel(kind, place_ref, *refs):
    *inputs, leaving_ref, staying_ref = refs
    if kind == "attn":
        side_ref, normed_ref, part_ref, g1_ref = inputs
        upper = dot_tn(side_ref[...], normed_ref[...])
        lower = dot_tn(part_ref[...], g1_ref[...])
        value = jnp.concatenate([upper, lower], axis=0)
    else:
        left_ref, right_ref = inputs
        value = dot_tn(left_ref[...], right_ref[...])
    value = value.astype(bf16)
    step = pl.program_id(0)

    @pl.when(step < 2)
    def _():
        leaving_ref[...] = value

    @pl.when(step >= 2)
    def _():
        staying_ref[...] = value


def grads(kind, place, arrays, width):
    rows = arrays[1].shape[0]

    def part_at(i):
        return jnp.where(i < 2, 2 * i + 1, 2 * i - 4)

    part = pl.BlockSpec((rows, width), lambda i, s: (0, part_at(i)))

    def of_part(a):
        return pl.BlockSpec((None, *a.shape[1:]), lambda i, s: (part_at(i), 0, 0))

    if kind == "attn":
        side, normed, attended, g1 = arrays
        specs = [of_part(side), whole(normed), of_part(attended), whole(g1)]
    elif kind == "up":
        specs = [whole(arrays[0]), part]
    else:
        specs = [part, whole(arrays[1])]
    block = (None, width, width)
    outs = [
        ((2, width, width), bf16, pl.BlockSpec(block, lambda i, s: (jnp.minimum(i, 1), 0, 0))),
        ((2, width, width), bf16, pl.BlockSpec(block, lambda i, s: (jnp.maximum(i - 2, 0), 0, 0))),
    ]
    return call(
        partial(grad_kernel, kind), "grads_" + kind, place, 4, list(zip(arrays, specs)), outs
    )


def emit_kernel(attention, aliased, place_ref, mine_ref, other_ref, *refs):
    outs = refs[aliased:]
    half, width = mine_ref.shape
    upper = place_ref[2] == 1
    mine, other = mine_ref[...].astype(f32), other_ref[...].astype(f32)
    low, high = jnp.where(upper, other, mine), jnp.where(upper, mine, other)
    if attention:
        qkv_ref, out_ref = outs
        share = width // 4
        qkv_ref[0, 0], qkv_ref[0, 1] = low[:share], low[share:]
        qkv_ref[0, 2], out_ref[0] = high[:share], high[share:]
    else:
        outs[0][0, :half] = low
        outs[0][0, half:] = high


def emit(place, layer, attention, summed, earlier):
    width = summed[0].shape[1]
    share = width // 4
    if attention:
        outs = [
            ((2, 3, share, width), f32, pl.BlockSpec((1, 3, share, width), lambda i, s: (layer, 0, 0, 0))),
            ((2, share, width), f32, pl.BlockSpec((1, share, width), lambda i, s: (layer, 0, 0))),
        ]
    else:
        outs = [((2, width, width), f32, pl.BlockSpec((1, width, width), lambda i, s: (layer, 0, 0)))]
    operands = [(a, whole(a)) for a in summed]
    aliases = {}
    if earlier is not None:
        aliases = {3 + n: n for n in range(len(earlier))}
        operands += [(e, pl.BlockSpec(memory_space=pl.ANY)) for e in earlier]
    return call(
        partial(emit_kernel, attention, len(aliases)), "emit", place, 1, operands, outs, aliases=aliases
    )


def head_swap(values, distance):
    count = lax.axis_size("head")
    return lax.ppermute(values, "head", [(i, i ^ distance) for i in range(count)])


def clip_swap(values, distance):
    count = lax.axis_size("clip")
    return lax.ppermute(values, "clip", [(i, i ^ distance) for i in range(count)])


class Order:
    def __init__(self):
        self.last = ()
        self.pending = []

    def run(self, step, *values):
        values, _ = lax.optimization_barrier((values, self.last))
        out = step(*values)
        self.last = (jax.tree.leaves(out)[0],)
        return out

    def send(self, swap, values, distance):
        values, _ = lax.optimization_barrier((values, self.last))
        out = swap(values, distance)
        self.pending.append(out)
        return out

    def close(self):
        self.last = self.last + tuple(self.pending)
        self.pending = []


def split_halves(total, upper):
    half = total.shape[-2] // 2
    low, high = total[..., :half, :], total[..., half:, :]
    return jnp.where(upper, low, high).astype(bf16), jnp.where(upper, high, low).astype(bf16)


def join_halves(mine, other, upper):
    return jnp.concatenate(
        [jnp.where(upper, other, mine), jnp.where(upper, mine, other)], axis=0
    )


class Pack:
    def __init__(self, order, leaving, staying, halving=True, late=False):
        self.order = order
        self.late = late
        self.out, self.kept = leaving, staying
        levels = lax.axis_size("clip").bit_length() - 1
        clip = lax.axis_index("clip")
        self.uppers = [((clip >> n) & 1) == 1 for n in range(levels)]
        depth = levels - 1 if halving else 1
        down = [("halve", n) for n in range(depth)]
        level = [("all", n) for n in range(depth, levels)]
        up = [("join", n) for n in reversed(range(depth))]
        if late:
            self.stages = ["core"] + down + ["across"] + level + up
        else:
            self.stages = ["core", "across"] + down + level + up
        self.at = 0
        self.prepared = False

    def prepare(self):
        if self.prepared:
            return
        self.prepared = True
        stage = self.stages[self.at]
        run = self.order.run
        if stage == "core":
            self.leaving = self.out
        elif self.late and stage == "across":

            def parted(total, moved):
                total = total.astype(f32) + moved.astype(f32)
                return total[1].astype(bf16), total[0].astype(bf16)

            self.leaving, self.sum = run(parted, self.sum, self.moved)
        elif self.late and self.at == 1:
            upper = self.uppers[stage[1]]

            def halved(kept, near):
                return split_halves(kept.astype(f32) + near.astype(f32), upper)

            self.leaving, self.sum = run(halved, self.kept, self.near)
        elif stage == "across":
            self.leaving = run(
                lambda kept, near: (kept[1].astype(f32) + near[1].astype(f32)).astype(bf16),
                self.kept, self.near,
            )
        else:
            kind, level = stage
            upper = self.uppers[level]
            if self.at == 2 and not self.late:
                start = lambda kept, near, moved: (
                    kept[0].astype(f32) + near[0].astype(f32) + moved.astype(f32)
                )
                values = (self.kept, self.near, self.moved)
            else:
                start = lambda total, moved: total.astype(f32) + moved.astype(f32)
                values = (self.sum, self.moved)
            if kind == "halve":
                self.leaving, self.sum = run(lambda *v: split_halves(start(*v), upper), *values)
            elif kind == "all" or self.stages[self.at - 1][0] == "all":
                self.leaving = self.sum = run(lambda *v: start(*v).astype(bf16), *values)
            else:
                before = self.uppers[self.stages[self.at - 1][1]]
                self.leaving = self.sum = run(
                    lambda mine, other: join_halves(mine, other, before), self.sum, self.moved
                )

    def launch(self):
        stage = self.stages[self.at]
        send = self.order.send
        if stage == "core":
            self.near = send(head_swap, self.leaving, 1)
        elif stage == "across":
            self.moved = send(head_swap, self.leaving, 2)
        else:
            self.moved = send(clip_swap, self.leaving, 1 << stage[1])
        self.at += 1
        self.prepared = False

    def done(self):
        return self.at == len(self.stages)

    def whole(self):
        assert self.done()
        return self.sum, self.moved


def on_device(
    tokens,
    frame_counts,
    token_mask,
    targets,
    norm_gain,
    norm_bias,
    w_qkv,
    qv_bias,
    w_out,
    vec_bias,
    w_up,
    up_bias,
    w_down,
    code_head,
):
    head_index = lax.axis_index("head")
    width = tokens.shape[1]
    share = w_out.shape[1]
    upper = lax.axis_index("clip") & 1
    place = jnp.stack(
        [head_index.astype(jnp.int32), frame_counts[0], upper.astype(jnp.int32)]
    )
    order = Order()

    def tied(values, *after):
        return lax.optimization_barrier((values, after))[0]

    clip_count = lax.axis_size("clip")
    own_small = jnp.concatenate([up_bias, qv_bias.reshape(1, width)], axis=0)
    clip_index = lax.axis_index("clip")

    def chunk(matrix):
        piece = matrix.shape[0] // clip_count
        return lax.dynamic_slice_in_dim(matrix, clip_index * piece, piece, 0)

    def over_clips(chunk_across):
        return lax.all_gather(chunk_across, "clip", axis=0, tiled=True)

    y_place, z_place = clip_index & 1, (clip_index >> 1) & 1

    def quarter(matrix):
        rows = matrix.shape[0] // 4
        return lax.dynamic_slice_in_dim(matrix, (2 * y_place + z_place) * rows, rows, 0)

    def along_y(first):
        return jnp.concatenate([first, clip_swap(first, 1)], axis=0)

    def by_place(pair, others):
        rows = pair.shape[0] // 2
        pieces = []
        for y in range(2):
            for z in range(2):
                same = z_place == z
                mine = jnp.where(same, pair[:rows], others[:rows])
                next_one = jnp.where(same, pair[rows:], others[rows:])
                pieces.append(jnp.where(y_place == y, mine, next_one))
        return jnp.concatenate(pieces, axis=0)

    def attn_pack(layer):
        transposed = w_qkv[layer].swapaxes(1, 2).reshape(-1, width)
        return jnp.concatenate([transposed, w_out[layer]], axis=0)

    def spread(own, across):
        return [own, head_swap(own, 1), across, head_swap(across, 1)]

    up_quarter = head_swap(quarter(w_up[0]), 2)
    down_quarter = head_swap(quarter(w_down[0]), 2)
    terms, left = [], own_small
    for _ in range(3):
        term = lax.reduce_precision(left, 8, 7)
        terms.append(term.astype(bf16))
        left = left - term
    fill = jnp.zeros((CELL - 3 * SMALLS, width), bf16)
    own = jnp.concatenate([attn_pack(0), *terms, fill], axis=0)
    up_quarter, down_quarter, own = lax.optimization_barrier((up_quarter, down_quarter, own))
    later = jnp.concatenate([chunk(w_up[1]), chunk(w_down[1])], axis=0)
    marks = (2 * targets + token_mask).reshape(4, WINDOW)
    up_pair, down_pair = along_y(up_quarter), along_y(down_quarter)
    up_x = by_place(up_pair, clip_swap(up_pair, 2))
    across, later, marks, place, up_x, down_pair = lax.optimization_barrier(
        (head_swap(own, 2), later, marks, place, up_x, down_pair)
    )
    attn = [spread(own, across), None]
    order.last = (across,)
    down_others = order.send(clip_swap, down_pair, 2)
    chunk_1 = order.send(head_swap, later, 2)
    smalls = attn[0]
    order.last = (attn[0][1], attn[0][3])
    ups = [w_up, order.send(head_swap, w_up, 1)]
    downs = [w_down, order.send(head_swap, w_down, 1)]
    up_diagonal = order.send(head_swap, up_x, 1)
    packs = [None, None]

    def feed_packs(up_x, down_x):
        return (
            ups, downs,
            [up_x, order.send(head_swap, up_x, 1)],
            [down_x, order.send(head_swap, down_x, 1)],
        )

    kept = []
    inputs = (tokens, marks)
    for layer in range(2):
        x, normed, qkv, att, lse, att_parts, *mark_pieces = order.run(
            lambda *a: attend(layer, place, a, norm_gain, norm_bias, smalls, attn[layer]), *inputs
        )
        order.close()
        if layer == 0:
            gathered = over_clips(tied(chunk_1, x))
            marks = [mark_pieces[0]] + [head_swap(mark_pieces[k], k) for k in (1, 2, 3)]
            down_x = order.run(by_place, down_pair, down_others)
            packs[0] = (ups, downs, [up_x, up_diagonal], [down_x, order.send(head_swap, down_x, 1)])
            order.close()
            own = attn_pack(1)
            attn_across = order.send(head_swap, own, 2)
            attn[1] = [own, head_swap(own, 1), attn_across]
        stream, normed2, active, slope, *outs = order.run(
            lambda a, b: feed(
                layer, place, a, b, attn[layer], vec_bias, norm_gain, norm_bias, smalls, packs[layer]
            ),
            x, att,
        )
        kept.append((x, normed, qkv, att_parts, lse, stream, normed2, active, slope))
        if layer == 0:
            order.close()
            pieces = gathered.reshape(clip_count, 2, -1, width)
            attn[1].append(order.send(head_swap, attn_across, 1))
            inputs = [outs[0]] + [order.send(head_swap, outs[k], k) for k in (1, 2, 3)]
            inputs = [p.reshape(4, 4, CELL, width) for p in inputs]
            order.close()
            packs[1] = feed_packs(pieces[:, 0].reshape(-1, width), pieces[:, 1].reshape(-1, width))
    grad, loss_sum, *parts = order.run(
        lambda a: code_loss(place, a, code_head, marks, active), outs[0]
    )
    down_1 = Pack(order, *parts, halving=False)

    def run_feed_back(layer, grad):
        x, normed, qkv, att, lse, stream, normed2, active, slope = kept[layer]
        return order.run(
            lambda a: feed_back(layer, place, a, slope, stream, normed2, norm_gain, packs[layer]), grad
        )

    def run_attend_back(layer, grad_next, g1):
        x, normed, qkv, att, lse, *_ = kept[layer]
        return order.run(
            lambda a, b: attend_back(
                layer, place, a, b, x, qkv, lse, norm_gain, attn[layer], normed, att
            ),
            grad_next, g1,
        )

    def pack(kind, *arrays, **options):
        parts = order.run(lambda *a: grads(kind, place, a, width), *arrays)
        return Pack(order, *parts, **options)

    def move(*ones):
        for one in ones:
            one.prepare()
        for one in ones:
            one.launch()

    move(down_1)
    order.close()
    move(down_1)
    grad_next, g1, feed_sum_1, *parts = run_feed_back(1, grad)
    up_1 = Pack(order, *parts, halving=False)
    order.close()
    move(up_1)
    down_1.prepare()
    order.close()
    move(up_1, down_1)
    side, *outs, attn_sum_1 = run_attend_back(1, grad_next, g1)
    order.close()

    grad = [outs[0]] + [order.send(head_swap, outs[k], k) for k in (1, 2, 3)]
    grad = [p.reshape(4, BAND, width) for p in grad]
    move(up_1, down_1)
    attn_1 = pack("attn", side, kept[1][1], kept[1][3], g1, late=True)
    order.close()

    move(attn_1)
    g2 = jnp.stack(grad, axis=1).reshape(-1, width)
    down_0 = pack("down", kept[0][7], g2)
    order.close()
    move(down_0)
    for one in (attn_1, down_1, up_1):
        one.prepare()
    order.close()
    move(down_0, attn_1, down_1, up_1)
    grad_next, g1, feed_sum_0, *parts = run_feed_back(0, g2)
    up_0 = Pack(order, *parts)
    order.close()
    move(up_0)
    for one in (down_0, attn_1, up_1, down_1):
        one.prepare()
    order.close()
    move(up_0, down_0, attn_1, up_1, down_1)
    grad_input, attn_sum_0, *parts = run_attend_back(0, grad_next, g1)
    attn_0 = Pack(order, *parts)
    order.close()
    move(attn_0)
    move(attn_1, down_0)
    for one in (up_0, up_1):
        one.prepare()
    order.close()
    move(down_0, attn_0, attn_1, up_0, up_1)
    order.close()

    packed = jnp.concatenate([feed_sum_0, feed_sum_1, attn_sum_0, attn_sum_1, loss_sum], axis=0)
    swaps = [(head_swap, 1), (head_swap, 2)]
    swaps += [(clip_swap, 1 << n) for n in range(clip_count.bit_length() - 1)]

    def pack_step():
        swap, distance = swaps.pop(0)
        return packed + order.send(swap, packed, distance)

    ready = {}

    def write(one, layer, attention, earlier):
        ready[one] = order.run(lambda *a: emit(place, layer, attention, a, earlier), *one.whole())

    late = [down_1, up_1]
    moving = [attn_0, up_0, down_0]
    everyone = moving + late + [attn_1]
    closed = [one for one in everyone if one.done()]
    jobs = [
        (down_1, 1, False, None), (up_1, 1, False, None), (down_0, 0, False, down_1),
        (attn_1, 1, True, None), (up_0, 0, False, up_1), (attn_0, 0, True, attn_1),
    ]
    wait = 0
    while swaps or not all(one.done() for one in moving + late + [attn_1]):
        held = [attn_1] if wait == 1 else []
        move(*[one for one in moving + [attn_1] + late if not one.done() and one not in held])
        wait += 1
        if swaps:
            packed = pack_step()
        for job in jobs:
            one, layer, attention, earlier = job
            if one in closed and (earlier is None or earlier in ready):
                write(one, layer, attention, ready.get(earlier))
                jobs.remove(job)
                break
        order.close()
        closed = [one for one in everyone if one.done()]

    for one, layer, attention, earlier in jobs:
        write(one, layer, attention, ready.get(earlier))

    attn_out, up_out, down_out = ready[attn_0], ready[up_0], ready[down_0]

    feed_sums = packed[:16].reshape(2, 8, width)
    attn_sums = packed[16:32].reshape(2, 8, width)
    loss_total = packed[32, 0]
    own_feed = lax.dynamic_index_in_dim(feed_sums, head_index, 1, keepdims=False)
    own_attn = lax.dynamic_index_in_dim(attn_sums, head_index, 1, keepdims=False)
    slot_total = clip_count * frame_counts.shape[0] * FRAMES * SIDE * SIDE

    return (
        loss_total / slot_total,
        grad_input,
        jnp.stack([attn_sums[:, 4], feed_sums[:, 4]], axis=1),
        jnp.stack([attn_sums[:, 5], feed_sums[:, 5]], axis=1),
        attn_out[0].swapaxes(2, 3),
        own_attn[:, : 2 * share].reshape(2, 2, share),
        attn_out[1],
        jnp.stack([feed_sums[:, 7], feed_sums[:, 6]], axis=1),
        up_out[0],
        own_feed,
        down_out[0],
    )


def solution(mesh):
    placed = (
        P(("clip", "head"), None),
        P("clip"),
        P(("clip", "head")),
        P(("clip", "head")),
        P(),
        P(),
        P(None, None, None, "head"),
        P(None, None, "head"),
        P(None, "head", None),
        P(),
        P(None, None, "head"),
        P(None, "head"),
        P(None, "head", None),
        P(),
    )
    return jax.shard_map(
        on_device,
        mesh=mesh,
        in_specs=placed,
        out_specs=(
            P(),
            P(("clip", "head"), None),
            P(),
            P(),
            P(None, None, None, "head"),
            P(None, None, "head"),
            P(None, "head", None),
            P(),
            P(None, None, "head"),
            P(None, "head"),
            P(None, "head", None),
        ),
        check_vma=False,
    )
```

```python
from functools import partial

import jax
import jax.numpy as jnp
from jax import lax
from jax.experimental import pallas as pl
from jax.experimental.pallas import tpu as pltpu
from jax.sharding import PartitionSpec as P

HD = 64
FRAMES = 16
SIDE = 16
TUBE = 4
WINDOW = 256
PAIR = 128
BAND = 64
CELL = 16
LSE_ROWS = 16
SMALLS = 3

epsilon = 1e-06
masked_score = -1e30
f32 = jnp.float32
bf16 = jnp.bfloat16
VMEM_LIMIT = 44 * 1024 * 1024
LIMITS = {"emit": 20 * 1024 * 1024, "grads_down": 24 * 1024 * 1024, "grads_attn": 24 * 1024 * 1024}
TIMES = {
    "attend": 17, "feed": 23, "code_loss": 18, "feed_back": 26, "attend_back": 25,
    "grads_down": 10, "grads_attn": 11, "emit": 3,
}
SCALE = 1.0


def cost_of(name):
    time = TIMES[name] * SCALE
    return pl.CostEstimate(flops=int(time * 1.15e9), bytes_accessed=int(time * 3.6e6), transcendentals=0)


def dot(a, b):
    return lax.dot_general(a, b, (((1,), (0,)), ((), ())), preferred_element_type=f32)


def dot_nt(a, b):
    return lax.dot_general(a, b, (((1,), (1,)), ((), ())), preferred_element_type=f32)


def dot_tn(a, b):
    return lax.dot_general(a, b, (((0,), (0,)), ((), ())), preferred_element_type=f32)


def statistics(stream):
    centre = jnp.mean(stream, axis=-1, keepdims=True)
    centred = stream - centre
    spread = jnp.mean(centred * centred, axis=-1, keepdims=True)
    scale = lax.rsqrt(spread + epsilon)
    return centred * scale, scale


def by_eight(values):
    rows, columns = values.shape
    return jnp.sum(values.reshape(rows // 8, 8, columns), axis=0)


def gather_sums(acc_ref, values):
    first = pl.program_id(0) == 0
    parts = jnp.concatenate([by_eight(v) for v in values], axis=1)

    @pl.when(first)
    def _():
        acc_ref[...] = parts

    @pl.when(jnp.logical_not(first))
    def _():
        acc_ref[...] += parts


ORDER = (1, 3, 0, 2)


def step_rows():
    return pl.ds(pl.multiple_of(pl.program_id(0) * WINDOW, WINDOW), WINDOW)


def put_parts(leaving_ref, staying_ref, buf, sem, gradient_of):
    copies = []
    for n, k in enumerate(ORDER):
        buf[n] = gradient_of(k).astype(bf16)
        target = (leaving_ref if n < 2 else staying_ref).at[n % 2]
        copy = pltpu.make_async_copy(buf.at[n], target, sem.at[n])
        copy.start()
        copies.append(copy)
    for copy in copies:
        copy.wait()


def parts_outs(width):
    return [((2, width, width), bf16, pl.BlockSpec(memory_space=pl.ANY))] * 2


def parts_scratch(width):
    return [pltpu.VMEM((4, width, width), bf16), pltpu.SemaphoreType.DMA((4,))]


def last_step():
    return pl.program_id(0) == pl.num_programs(0) - 1


def norm_back(stream, gain, grad):
    normal, scale = statistics(stream)
    scaled = grad * gain
    mean_plain = jnp.mean(scaled, axis=-1, keepdims=True)
    mean_normal = jnp.mean(scaled * normal, axis=-1, keepdims=True)
    inner = scale * (scaled - mean_plain - normal * mean_normal)
    return inner, grad * normal


def gelu_both(hidden):
    root = 0.7978845608028654
    cubic = 0.044715
    square = hidden * hidden
    bend = jnp.tanh(hidden * (root + root * cubic * square))
    rise = 0.5 + 0.5 * bend
    active = hidden * rise
    slope = rise + (active - active * rise) * (2.0 * root + 6.0 * root * cubic * square)
    return active.astype(bf16), slope.astype(bf16)


def allowed_of(place_ref):
    head_index = place_ref[0]
    frame_count = place_ref[1]

    def valid(axis):
        position = lax.broadcasted_iota(jnp.int32, (WINDOW, WINDOW), axis)
        frame = 4 * ((position >> 6) ^ head_index) + ((position >> 4) & 3)
        return frame < frame_count

    return jnp.logical_or(valid(0), jnp.logical_not(valid(1)))


def shuffle_of(place_ref, axis):
    arranged = lax.broadcasted_iota(jnp.int32, (WINDOW, WINDOW), axis)
    plain = lax.broadcasted_iota(jnp.int32, (WINDOW, WINDOW), 1 - axis)
    band = (arranged >> 6) ^ place_ref[0]
    source = band * BAND + ((arranged >> 2) & 3) * 16 + ((arranged >> 4) & 3) * 4 + (arranged & 3)
    return (source == plain).astype(f32).astype(bf16)


def small_rows(ref, start, count=1):
    terms = [ref[SMALLS * n + start : SMALLS * n + start + count, :].astype(f32) for n in range(3)]
    return terms[0] + terms[1] + terms[2]


def small_of(a):
    rows, width = a.shape
    return pl.BlockSpec((CELL, width), lambda i, s: (rows // CELL - 1, 0))


def assemble_qkv(packs, scratch):
    width = scratch.shape[1]
    share = width // 4
    for k in range(4):
        for j in range(3):
            start = j * width + k * share
            scratch[start : start + share, :] = packs[k][j * share : (j + 1) * share, :]


def assemble_out(packs, scratch):
    share = scratch.shape[0] // 4
    for k in range(4):
        scratch[k * share : (k + 1) * share, :] = packs[k][3 * share : 4 * share, :]


def stack_heads(pair):
    low = lax.broadcasted_iota(jnp.int32, pair.shape, 1) < HD
    zero = jnp.zeros((), bf16)
    return jnp.concatenate([jnp.where(low, pair, zero), jnp.where(low, zero, pair)], axis=0)


def attend_core(qkv, allowed, att_ref, lse_ref, part_ref):
    width = att_ref.shape[1]
    pairs = width // PAIR

    def part(j, pair):
        return qkv[:, j * width + pair * PAIR : j * width + (pair + 1) * PAIR]

    def scores_of(pair):
        query = part(0, pair) * jnp.asarray(HD ** (-0.5), bf16)
        return dot_nt(stack_heads(part(1, pair)), query)

    ahead = scores_of(0)
    for pair in range(pairs):
        scores = ahead
        if pair + 1 < pairs:
            ahead = scores_of(pair + 1)
        probs = []
        for half in range(2):
            mine = scores[half * WINDOW : (half + 1) * WINDOW]
            if allowed is not None:
                mine = jnp.where(allowed, mine, masked_score)
            top = jnp.max(mine, axis=0, keepdims=True)
            terms = jnp.exp(mine - top)
            total = jnp.sum(terms, axis=0, keepdims=True)
            probs.append((terms * (1.0 / total)).astype(bf16))
            head = 2 * pair + half
            lse_ref[head : head + 1, :] = top + jnp.log(total)
        out = dot_tn(jnp.concatenate(probs, axis=0), stack_heads(part(2, pair)))
        att_ref[:, pair * PAIR : (pair + 1) * PAIR] = out.astype(bf16)
    share = width // 4
    for k in range(4):
        part_ref[k] = att_ref[:, k * share : (k + 1) * share]


def attend_kernel(layer, place_ref, *refs):
    if layer == 0:
        tokens_ref, marks_ref, *refs = refs
        shuffle = shuffle_of(place_ref, 0)
        stream = dot(shuffle, tokens_ref[...])
    else:
        pieces, refs = refs[:4], refs[4:]
        stream = jnp.concatenate(
            [p[...].reshape(BAND, p.shape[-1]) for p in pieces], axis=0
        ).astype(f32)
    gain_ref, shift_ref, s0, s1, s2, s3, p0, p1, p2, p3, x_ref, normed_ref, qkv_ref, att_ref, lse_ref, part_ref, *refs = refs
    *mark_refs, scratch = refs
    share = scratch.shape[1] // 4

    @pl.when(pl.program_id(0) == 0)
    def _():
        assemble_qkv((p0, p1, p2, p3), scratch)

    if layer == 0:
        given = marks_ref[pl.ds(pl.program_id(0), 1), :]
        high = given >> 4
        both = jnp.concatenate([high, given - 16 * high], axis=0).astype(f32).astype(bf16)
        both = dot(both, shuffle_of(place_ref, 1))
        marks = 16.0 * both[0:1] + both[1:2]
        for k in range(4):
            mark_refs[k][pl.ds(pl.program_id(0), 1), :] = marks[:, k * BAND : (k + 1) * BAND]
    x_ref[...] = stream.astype(bf16)
    normal, _ = statistics(stream)
    normed = (normal * gain_ref[layer, 0:1] + shift_ref[layer, 0:1]).astype(bf16)
    normed_ref[...] = normed
    start = 2 * layer * share
    smalls = [small_rows(r, 2) for r in (s0, s1, s2, s3)]
    bias = jnp.concatenate(
        [r[:, start : start + share] for r in smalls]
        + [jnp.zeros((1, 4 * share), f32)]
        + [r[:, start + share : start + 2 * share] for r in smalls],
        axis=1,
    )
    qkv = (dot_nt(normed, scratch[...]) + bias).astype(bf16)
    qkv_ref[...] = qkv
    allowed = allowed_of(place_ref) if layer == 1 else None
    attend_core(qkv, allowed, att_ref, lse_ref, part_ref)


def whole(array):
    zeros = (0,) * array.ndim
    return pl.BlockSpec(array.shape, lambda i, s: zeros, pipeline_mode=pl.Buffered(1))


def rows_of(columns, rows=WINDOW):
    return pl.BlockSpec((rows, columns), lambda i, s: (i, 0))


def parts_of(columns):
    return pl.BlockSpec((4, WINDOW, columns), lambda i, s: (0, i, 0))


def tube_of(columns):
    return pl.BlockSpec((4, 1, CELL, columns), lambda i, s: (0, i, 0, 0))


def sums_of(columns):
    return pl.BlockSpec((8, columns), lambda i, s: (0, 0))


def call(kernel, name, place, steps, operands, outs, scratch=(), aliases={}):
    return pl.pallas_call(
        kernel,
        grid_spec=pltpu.PrefetchScalarGridSpec(
            num_scalar_prefetch=1,
            grid=(steps,),
            in_specs=[spec for _, spec in operands],
            out_specs=[spec for _, _, spec in outs],
            scratch_shapes=list(scratch),
        ),
        out_shape=[jax.ShapeDtypeStruct(shape, dtype) for shape, dtype, _ in outs],
        compiler_params=pltpu.CompilerParams(vmem_limit_bytes=LIMITS.get(name, VMEM_LIMIT)),
        cost_estimate=cost_of(name),
        input_output_aliases=aliases,
        name=name,
    )(place, *[array for array, _ in operands])


def attend(layer, place, inputs, gain, shift, smalls, packs):
    width = gain.shape[-1]
    rows = 4 * WINDOW
    if layer == 0:
        tokens, marks = inputs
        first = [(tokens, rows_of(width)), (marks, whole(marks))]
    else:
        first = [(p, tube_of(width)) for p in inputs]
    operands = first + [(a, whole(a)) for a in (gain, shift)]
    operands += [(a, small_of(a)) for a in smalls] + [(a, whole(a)) for a in packs]
    outs = [
        ((rows, width), bf16, rows_of(width)),
        ((rows, width), bf16, rows_of(width)),
        ((rows, 3 * width), bf16, rows_of(3 * width)),
        ((rows, width), bf16, rows_of(width)),
        ((4 * LSE_ROWS, WINDOW), f32, rows_of(WINDOW, LSE_ROWS)),
        ((4, rows, width // 4), bf16, parts_of(width // 4)),
    ]
    if layer == 0:
        outs += [((4, BAND), f32, pl.BlockSpec((4, BAND), lambda i, s: (0, 0)))] * 4
    return call(
        partial(attend_kernel, layer), "attend", place, 4, operands, outs,
        [pltpu.VMEM((3 * width, width), bf16)],
    )


def attend_back_core(qkv, grad, lse_ref, allowed):
    width = grad.shape[1]
    pairs = width // PAIR

    def part(j, pair):
        return qkv[:, j * width + pair * PAIR : j * width + (pair + 1) * PAIR]

    def first_of(pair):
        query = part(0, pair) * jnp.asarray(HD ** (-0.5), bf16)
        grad_part = grad[:, pair * PAIR : (pair + 1) * PAIR]
        keys = stack_heads(part(1, pair))
        scores = dot_nt(keys, query)
        grad_probs = dot_nt(stack_heads(part(2, pair)), grad_part)
        return query, grad_part, keys, scores, grad_probs

    low = lax.broadcasted_iota(jnp.int32, (WINDOW, PAIR), 1) < HD
    results = [[], [], []]
    ahead = first_of(0)
    for pair in range(pairs):
        query, grad_part, keys, scores, grad_probs = ahead
        if pair + 1 < pairs:
            ahead = first_of(pair + 1)
        all_probs, all_scores = [], []
        for half in range(2):
            rows = slice(half * WINDOW, (half + 1) * WINDOW)
            mine = scores[rows]
            if allowed is not None:
                mine = jnp.where(allowed, mine, masked_score)
            head = 2 * pair + half
            probs = jnp.exp(mine - lse_ref[head : head + 1, :])
            grad_mine = grad_probs[rows]
            delta = jnp.sum(probs * grad_mine, axis=0, keepdims=True)
            all_probs.append(probs.astype(bf16))
            all_scores.append((probs * (grad_mine - delta)).astype(bf16))
        probs = jnp.concatenate(all_probs, axis=0)
        grad_scores = jnp.concatenate(all_scores, axis=0)
        grad_query = dot_tn(grad_scores, keys) * HD ** (-0.5)
        grad_key = dot(grad_scores, query)
        grad_value = dot(probs, grad_part)
        results[0].append(grad_query.astype(bf16))
        results[1].append(jnp.where(low, grad_key[:WINDOW], grad_key[WINDOW:]).astype(bf16))
        results[2].append(jnp.where(low, grad_value[:WINDOW], grad_value[WINDOW:]).astype(bf16))
    return [jnp.concatenate(part, axis=1) for part in results]


def attend_back_kernel(layer, place_ref, *refs):
    (stream_ref, g1_ref, x_ref, qkv_ref, lse_ref, gain_ref, p0, p1, p2, p3, *outs) = refs
    if layer == 1:
        side_ref, *outs = outs
        pieces, outs = outs[:4], outs[4:]
        sums_ref, scratch, out_scratch, acc = outs
        rows = slice(None)
    else:
        (
            normed_ref, part_ref, final_ref, sums_ref, leaving_ref, staying_ref,
            scratch, out_scratch, acc, side_ref, all_normed, all_parts, all_g1, buf, sem,
        ) = outs
        rows = step_rows()
        all_normed[rows, :] = normed_ref[...]
        all_g1[rows, :] = g1_ref[...]
        for k in range(4):
            all_parts[k, rows, :] = part_ref[k]
    width = stream_ref.shape[1]
    share = width // 4

    @pl.when(pl.program_id(0) == 0)
    def _():
        assemble_qkv((p0, p1, p2, p3), scratch)
        assemble_out((p0, p1, p2, p3), out_scratch)

    grad_att = dot_nt(g1_ref[...], out_scratch[...]).astype(bf16)
    allowed = allowed_of(place_ref) if layer == 1 else None
    parts = attend_back_core(qkv_ref[...], grad_att, lse_ref, allowed)
    for k in range(4):
        for j in range(3):
            side_ref[k, rows, j * share : (j + 1) * share] = parts[j][:, k * share : (k + 1) * share]
    joined = jnp.concatenate(parts, axis=1)
    grad_normed = dot(joined, scratch[...])
    inner, scaled = norm_back(x_ref[...].astype(f32), gain_ref[layer, 0:1], grad_normed)
    gather_sums(acc, [parts[0].astype(f32), parts[2].astype(f32), scaled, grad_normed])
    stream = stream_ref[...] + inner
    if layer == 1:
        for k in range(4):
            pieces[k][...] = (
                stream[k * BAND : (k + 1) * BAND].astype(bf16).reshape(4, 1, CELL, width)
            )
    else:
        shuffle = shuffle_of(place_ref, 1)
        high = stream.astype(bf16)
        low = (stream - high.astype(f32)).astype(bf16)
        final_ref[...] = dot(shuffle, high) + dot(shuffle, low)

    @pl.when(last_step())
    def _():
        total = jnp.sum(acc[...], axis=0, keepdims=True)
        sums_ref[...] = jnp.zeros(sums_ref.shape, f32)
        for k in range(4):
            query = total[:, k * share : (k + 1) * share]
            value = total[:, width + k * share : width + (k + 1) * share]
            sums_ref[pl.ds(place_ref[0] ^ k, 1), : 2 * share] = jnp.concatenate([query, value], axis=1)
        sums_ref[4:5, :] = total[:, 2 * width : 3 * width]
        sums_ref[5:6, :] = total[:, 3 * width :]
        if layer == 0:

            def gradient_of(k):
                upper = dot_tn(side_ref[k], all_normed[...])
                lower = dot_tn(all_parts[k], all_g1[...])
                return jnp.concatenate([upper, lower], axis=0)

            put_parts(leaving_ref, staying_ref, buf, sem, gradient_of)


def attend_back(layer, place, stream, g1, x, qkv, lse, gain, packs, normed, attended):
    rows, width = stream.shape
    share = width // 4
    operands = [
        (stream, rows_of(width)),
        (g1, rows_of(width)),
        (x, rows_of(width)),
        (qkv, rows_of(3 * width)),
        (lse, rows_of(WINDOW, LSE_ROWS)),
    ] + [(a, whole(a)) for a in (gain, *packs)]
    sums = [((8, width), f32, sums_of(width))]
    scratch = [
        pltpu.VMEM((3 * width, width), bf16), pltpu.VMEM((width, width), bf16), pltpu.VMEM((8, 4 * width), f32)
    ]
    if layer == 1:
        outs = [((4, rows, 3 * share), bf16, parts_of(3 * share))]
        outs = outs + [((4, 4, CELL, width), bf16, tube_of(width))] * 4 + sums
    else:
        operands += [(normed, rows_of(width)), (attended, parts_of(share))]
        outs = [((rows, width), f32, rows_of(width))] + sums + parts_outs(width)
        scratch += [
            pltpu.VMEM((4, rows, 3 * share), bf16), pltpu.VMEM((rows, width), bf16),
            pltpu.VMEM((4, rows, share), bf16), pltpu.VMEM((rows, width), bf16),
        ] + parts_scratch(width)
    return call(partial(attend_back_kernel, layer), "attend_back", place, 4, operands, outs, scratch)


def feed_kernel(layer, place_ref, *refs):
    (
        x_ref, att_ref, a0, a1, a2, a3, vec_ref, gain_ref, shift_ref, s0, s1, s2, s3,
        u0, u1, u2, u3, d0, d1, d2, d3, stream_ref, normed_ref, active_ref, slope_ref, *outs
    ) = refs
    ups, downs = (u0, u1, u2, u3), (d0, d1, d2, d3)
    *pieces, scratch = outs
    width = x_ref.shape[1]

    @pl.when(pl.program_id(0) == 0)
    def _():
        share = width // 4
        for k, part in enumerate((a0, a1, a2, a3)):
            scratch[k * share : (k + 1) * share, :] = part[...]

    stream = x_ref[...].astype(f32) + dot(att_ref[...], scratch[...]) + vec_ref[layer, 0:1]
    stream_ref[...] = stream
    normal, _ = statistics(stream)
    normed = (normal * gain_ref[layer, 1:2] + shift_ref[layer, 1:2]).astype(bf16)
    normed_ref[...] = normed
    total = stream + vec_ref[layer, 1:2]
    units = u0.shape[1]
    ahead = dot(normed, ups[0][...])
    for k in range(4):
        hidden = ahead
        if k < 3:
            ahead = dot(normed, ups[k + 1][...])
        cut = slice(k * units, (k + 1) * units)
        active, slope = gelu_both(hidden + small_rows((s0, s1, s2, s3)[k], layer))
        active_ref[:, cut] = active
        slope_ref[:, cut] = slope
        total = total + dot(active, downs[k][...])
    total = total.astype(bf16)
    if layer == 0:
        for k in range(4):
            pieces[k][...] = total[k * BAND : (k + 1) * BAND].reshape(1, BAND, width)
    else:
        pieces[0][...] = total


def feed_specs(layer, packs):
    ups, downs, ups_across, downs_across = packs

    def of_layer(a):
        return (a, pl.BlockSpec(
            (None, *a.shape[1:]), lambda i, s: (layer, 0, 0), pipeline_mode=pl.Buffered(1)
        ))

    return [
        *[of_layer(a) for a in ups],
        *[(a, whole(a)) for a in ups_across],
        *[of_layer(a) for a in downs],
        *[(a, whole(a)) for a in downs_across],
    ]


def feed(layer, place, x, att, attn_packs, vecs, gain, shift, smalls, packs):
    rows, width = x.shape
    units = packs[0][0].shape[2]
    last = pl.BlockSpec((width // 4, width), lambda i, s: (3, 0))
    operands = (
        [(x, rows_of(width)), (att, rows_of(width))]
        + [(a, last) for a in attn_packs]
        + [(a, whole(a)) for a in (vecs, gain, shift)]
        + [(a, small_of(a)) for a in smalls]
        + feed_specs(layer, packs)
    )
    outs = [
        ((rows, width), f32, rows_of(width)),
        ((rows, width), bf16, rows_of(width)),
        ((rows, 4 * units), bf16, rows_of(4 * units)),
        ((rows, 4 * units), bf16, rows_of(4 * units)),
    ]
    if layer == 0:
        piece = pl.BlockSpec((1, BAND, width), lambda i, s: (i, 0, 0))
        outs = outs + [((4, BAND, width), bf16, piece)] * 4
    else:
        outs = outs + [((rows, width), bf16, rows_of(width))]
    return call(
        partial(feed_kernel, layer), "feed", place, 4, operands, outs,
        [pltpu.VMEM((width, width), bf16)],
    )


def loss_kernel(
    place_ref, final_ref, head_ref, m0, m1, m2, m3, active_ref, grad_ref, loss_ref, leaving_ref, staying_ref,
    acc, all_active, all_g2, buf, sem,
):
    logits = dot(final_ref[...], head_ref[...])
    spread = jnp.concatenate(
        [jnp.broadcast_to(m[f : f + 1, :], (CELL, BAND)) for m in (m0, m1, m2, m3) for f in range(4)],
        axis=0,
    )
    position = lax.broadcasted_iota(jnp.int32, (WINDOW, BAND), 0)
    lane = lax.broadcasted_iota(jnp.int32, (WINDOW, BAND), 1)
    mine = lane == pl.program_id(0) * CELL + (position & (CELL - 1))
    mark = jnp.sum(jnp.where(mine, spread, 0.0), axis=1, keepdims=True).astype(jnp.int32)
    place_of = lax.broadcasted_iota(jnp.int32, (WINDOW, 1), 0)
    frame = 4 * ((place_of >> 6) ^ place_ref[0]) + ((place_of >> 4) & 3)
    weight = jnp.where(frame < place_ref[1], (mark & 1).astype(f32), 0.0)
    top = jnp.max(logits, axis=1, keepdims=True)
    terms = jnp.exp(logits - top)
    total = jnp.sum(terms, axis=1, keepdims=True)
    code = lax.broadcasted_iota(jnp.int32, logits.shape, 1)
    chosen = code == (mark >> 1)
    picked = jnp.sum(jnp.where(chosen, logits, 0.0), axis=1, keepdims=True)
    entry = weight * (top + jnp.log(total) - picked)
    soft = terms * (1.0 / total)
    grad_logits = (weight * (soft - jnp.where(chosen, 1.0, 0.0))).astype(bf16)
    grad = dot_nt(grad_logits, head_ref[...])
    grad_ref[...] = grad
    all_g2[step_rows(), :] = grad.astype(bf16)
    all_active[step_rows(), :] = active_ref[...]
    gather_sums(acc, [jnp.broadcast_to(entry, (WINDOW, PAIR))])

    @pl.when(last_step())
    def _():
        total = jnp.sum(acc[...], axis=0, keepdims=True)
        loss_ref[...] = jnp.broadcast_to(total[:, :1], loss_ref.shape)
        width = grad_ref.shape[1]
        put_parts(
            leaving_ref, staying_ref, buf, sem,
            lambda k: dot_tn(all_active[:, k * width : (k + 1) * width], all_g2[...]),
        )


def code_loss(place, final, code_head, marks, active):
    rows, width = final.shape
    operands = [(final, rows_of(width))] + [(a, whole(a)) for a in (code_head, *marks)]
    operands += [(active, rows_of(active.shape[1]))]
    outs = [
        ((rows, width), f32, rows_of(width)),
        ((8, width), f32, sums_of(width)),
    ] + parts_outs(width)
    scratch = [
        pltpu.VMEM((8, PAIR), f32), pltpu.VMEM(active.shape, bf16), pltpu.VMEM((rows, width), bf16)
    ] + parts_scratch(width)
    return call(loss_kernel, "code_loss", place, 4, operands, outs, scratch)


def feed_back_kernel(layer, place_ref, *refs):
    if layer == 1:
        grad_ref, *refs = refs
        grad = grad_ref[...]
    else:
        grad_ref, *refs = refs
        grad = grad_ref[...].astype(f32)
    (
        slope_ref, stream_ref, normed_ref, gain_ref, u0, u1, u2, u3, d0, d1, d2, d3, next_ref, g1_ref,
        sums_ref, leaving_ref, staying_ref, acc, all_hidden, all_normed, buf, sem,
    ) = refs
    all_normed[step_rows(), :] = normed_ref[...]
    g2 = grad.astype(bf16)
    units = u0.shape[1]
    grad_normed = jnp.zeros(grad.shape, f32)
    sums = []
    ups, downs = (u0, u1, u2, u3), (d0, d1, d2, d3)
    ahead = dot_nt(g2, downs[0][...])
    for k in range(4):
        grad_active = ahead
        if k < 3:
            ahead = dot_nt(g2, downs[k + 1][...])
        cut = slice(k * units, (k + 1) * units)
        grad_hidden = (grad_active * slope_ref[:, cut].astype(f32)).astype(bf16)
        all_hidden[step_rows(), cut] = grad_hidden
        sums.append(grad_hidden.astype(f32))
        grad_normed = grad_normed + dot_nt(grad_hidden, ups[k][...])
    inner, scaled = norm_back(stream_ref[...], gain_ref[layer, 1:2], grad_normed)
    grad = grad + inner
    next_ref[...] = grad
    g1 = grad.astype(bf16)
    g1_ref[...] = g1
    gather_sums(acc, sums + [scaled, grad_normed, g2.astype(f32), g1.astype(f32)])

    @pl.when(last_step())
    def _():
        total = jnp.sum(acc[...], axis=0, keepdims=True)
        for k in range(4):
            sums_ref[pl.ds(place_ref[0] ^ k, 1), :] = total[:, k * units : (k + 1) * units]
            start = 4 * units + k * grad.shape[1]
            sums_ref[4 + k : 5 + k, :] = total[:, start : start + grad.shape[1]]
        put_parts(
            leaving_ref, staying_ref, buf, sem,
            lambda k: dot_tn(all_normed[...], all_hidden[:, k * units : (k + 1) * units]),
        )


def feed_back(layer, place, grad, slope, stream, normed, gain, packs):
    rows, width = stream.shape
    units = packs[0][0].shape[2]
    operands = (
        [(grad, rows_of(width)), (slope, rows_of(4 * units)), (stream, rows_of(width)), (normed, rows_of(width))]
        + [(gain, whole(gain))]
        + feed_specs(layer, packs)
    )
    outs = [
        ((rows, width), f32, rows_of(width)),
        ((rows, width), bf16, rows_of(width)),
        ((8, width), f32, sums_of(width)),
    ] + parts_outs(width)
    scratch = [
        pltpu.VMEM((8, 4 * units + 4 * width), f32),
        pltpu.VMEM((rows, 4 * units), bf16),
        pltpu.VMEM((rows, width), bf16),
    ] + parts_scratch(width)
    return call(partial(feed_back_kernel, layer), "feed_back", place, 4, operands, outs, scratch)


def grad_kernel(kind, place_ref, *refs):
    *inputs, leaving_ref, staying_ref = refs
    if kind == "attn":
        side_ref, normed_ref, part_ref, g1_ref = inputs
        upper = dot_tn(side_ref[...], normed_ref[...])
        lower = dot_tn(part_ref[...], g1_ref[...])
        value = jnp.concatenate([upper, lower], axis=0)
    else:
        left_ref, right_ref = inputs
        value = dot_tn(left_ref[...], right_ref[...])
    value = value.astype(bf16)
    step = pl.program_id(0)

    @pl.when(step < 2)
    def _():
        leaving_ref[...] = value

    @pl.when(step >= 2)
    def _():
        staying_ref[...] = value


def grads(kind, place, arrays, width):
    rows = arrays[1].shape[0]

    def part_at(i):
        return jnp.where(i < 2, 2 * i + 1, 2 * i - 4)

    part = pl.BlockSpec((rows, width), lambda i, s: (0, part_at(i)))

    def of_part(a):
        return pl.BlockSpec((None, *a.shape[1:]), lambda i, s: (part_at(i), 0, 0))

    if kind == "attn":
        side, normed, attended, g1 = arrays
        specs = [of_part(side), whole(normed), of_part(attended), whole(g1)]
    elif kind == "up":
        specs = [whole(arrays[0]), part]
    else:
        specs = [part, whole(arrays[1])]
    block = (None, width, width)
    outs = [
        ((2, width, width), bf16, pl.BlockSpec(block, lambda i, s: (jnp.minimum(i, 1), 0, 0))),
        ((2, width, width), bf16, pl.BlockSpec(block, lambda i, s: (jnp.maximum(i - 2, 0), 0, 0))),
    ]
    return call(
        partial(grad_kernel, kind), "grads_" + kind, place, 4, list(zip(arrays, specs)), outs
    )


def emit_kernel(attention, aliased, place_ref, mine_ref, other_ref, *refs):
    outs = refs[aliased:]
    half, width = mine_ref.shape
    upper = place_ref[2] == 1
    mine, other = mine_ref[...].astype(f32), other_ref[...].astype(f32)
    low, high = jnp.where(upper, other, mine), jnp.where(upper, mine, other)
    if attention:
        qkv_ref, out_ref = outs
        share = width // 4
        qkv_ref[0, 0], qkv_ref[0, 1] = low[:share], low[share:]
        qkv_ref[0, 2], out_ref[0] = high[:share], high[share:]
    else:
        outs[0][0, :half] = low
        outs[0][0, half:] = high


def emit(place, layer, attention, summed, earlier):
    width = summed[0].shape[1]
    share = width // 4
    if attention:
        outs = [
            ((2, 3, share, width), f32, pl.BlockSpec((1, 3, share, width), lambda i, s: (layer, 0, 0, 0))),
            ((2, share, width), f32, pl.BlockSpec((1, share, width), lambda i, s: (layer, 0, 0))),
        ]
    else:
        outs = [((2, width, width), f32, pl.BlockSpec((1, width, width), lambda i, s: (layer, 0, 0)))]
    operands = [(a, whole(a)) for a in summed]
    aliases = {}
    if earlier is not None:
        aliases = {3 + n: n for n in range(len(earlier))}
        operands += [(e, pl.BlockSpec(memory_space=pl.ANY)) for e in earlier]
    return call(
        partial(emit_kernel, attention, len(aliases)), "emit", place, 1, operands, outs, aliases=aliases
    )


def head_swap(values, distance):
    count = lax.axis_size("head")
    return lax.ppermute(values, "head", [(i, i ^ distance) for i in range(count)])


def clip_swap(values, distance):
    count = lax.axis_size("clip")
    return lax.ppermute(values, "clip", [(i, i ^ distance) for i in range(count)])


class Order:
    def __init__(self):
        self.last = ()
        self.pending = []

    def run(self, step, *values):
        values, _ = lax.optimization_barrier((values, self.last))
        out = step(*values)
        self.last = (jax.tree.leaves(out)[0],)
        return out

    def send(self, swap, values, distance):
        values, _ = lax.optimization_barrier((values, self.last))
        out = swap(values, distance)
        self.pending.append(out)
        return out

    def close(self):
        self.last = self.last + tuple(self.pending)
        self.pending = []


def split_halves(total, upper):
    half = total.shape[-2] // 2
    low, high = total[..., :half, :], total[..., half:, :]
    return jnp.where(upper, low, high).astype(bf16), jnp.where(upper, high, low).astype(bf16)


def join_halves(mine, other, upper):
    return jnp.concatenate(
        [jnp.where(upper, other, mine), jnp.where(upper, mine, other)], axis=0
    )


class Pack:
    def __init__(self, order, leaving, staying, halving=True, late=False):
        self.order = order
        self.late = late
        self.out, self.kept = leaving, staying
        levels = lax.axis_size("clip").bit_length() - 1
        clip = lax.axis_index("clip")
        self.uppers = [((clip >> n) & 1) == 1 for n in range(levels)]
        depth = levels - 1 if halving else 1
        down = [("halve", n) for n in range(depth)]
        level = [("all", n) for n in range(depth, levels)]
        up = [("join", n) for n in reversed(range(depth))]
        if late:
            self.stages = ["core"] + down + ["across"] + level + up
        else:
            self.stages = ["core", "across"] + down + level + up
        self.at = 0
        self.prepared = False

    def prepare(self):
        if self.prepared:
            return
        self.prepared = True
        stage = self.stages[self.at]
        run = self.order.run
        if stage == "core":
            self.leaving = self.out
        elif self.late and stage == "across":

            def parted(total, moved):
                total = total.astype(f32) + moved.astype(f32)
                return total[1].astype(bf16), total[0].astype(bf16)

            self.leaving, self.sum = run(parted, self.sum, self.moved)
        elif self.late and self.at == 1:
            upper = self.uppers[stage[1]]

            def halved(kept, near):
                return split_halves(kept.astype(f32) + near.astype(f32), upper)

            self.leaving, self.sum = run(halved, self.kept, self.near)
        elif stage == "across":
            self.leaving = run(
                lambda kept, near: (kept[1].astype(f32) + near[1].astype(f32)).astype(bf16),
                self.kept, self.near,
            )
        else:
            kind, level = stage
            upper = self.uppers[level]
            if self.at == 2 and not self.late:
                start = lambda kept, near, moved: (
                    kept[0].astype(f32) + near[0].astype(f32) + moved.astype(f32)
                )
                values = (self.kept, self.near, self.moved)
            else:
                start = lambda total, moved: total.astype(f32) + moved.astype(f32)
                values = (self.sum, self.moved)
            if kind == "halve":
                self.leaving, self.sum = run(lambda *v: split_halves(start(*v), upper), *values)
            elif kind == "all" or self.stages[self.at - 1][0] == "all":
                self.leaving = self.sum = run(lambda *v: start(*v).astype(bf16), *values)
            else:
                before = self.uppers[self.stages[self.at - 1][1]]
                self.leaving = self.sum = run(
                    lambda mine, other: join_halves(mine, other, before), self.sum, self.moved
                )

    def launch(self):
        stage = self.stages[self.at]
        send = self.order.send
        if stage == "core":
            self.near = send(head_swap, self.leaving, 1)
        elif stage == "across":
            self.moved = send(head_swap, self.leaving, 2)
        else:
            self.moved = send(clip_swap, self.leaving, 1 << stage[1])
        self.at += 1
        self.prepared = False

    def done(self):
        return self.at == len(self.stages)

    def whole(self):
        assert self.done()
        return self.sum, self.moved


def on_device(
    tokens,
    frame_counts,
    token_mask,
    targets,
    norm_gain,
    norm_bias,
    w_qkv,
    qv_bias,
    w_out,
    vec_bias,
    w_up,
    up_bias,
    w_down,
    code_head,
):
    head_index = lax.axis_index("head")
    width = tokens.shape[1]
    share = w_out.shape[1]
    upper = lax.axis_index("clip") & 1
    place = jnp.stack(
        [head_index.astype(jnp.int32), frame_counts[0], upper.astype(jnp.int32)]
    )
    order = Order()

    def tied(values, *after):
        return lax.optimization_barrier((values, after))[0]

    clip_count = lax.axis_size("clip")
    own_small = jnp.concatenate([up_bias, qv_bias.reshape(1, width)], axis=0)
    clip_index = lax.axis_index("clip")

    def chunk(matrix):
        piece = matrix.shape[0] // clip_count
        return lax.dynamic_slice_in_dim(matrix, clip_index * piece, piece, 0)

    def over_clips(chunk_across):
        return lax.all_gather(chunk_across, "clip", axis=0, tiled=True)

    y_place, z_place = clip_index & 1, (clip_index >> 1) & 1

    def quarter(matrix):
        rows = matrix.shape[0] // 4
        return lax.dynamic_slice_in_dim(matrix, (2 * y_place + z_place) * rows, rows, 0)

    def along_y(first):
        return jnp.concatenate([first, clip_swap(first, 1)], axis=0)

    def by_place(pair, others):
        rows = pair.shape[0] // 2
        pieces = []
        for y in range(2):
            for z in range(2):
                same = z_place == z
                mine = jnp.where(same, pair[:rows], others[:rows])
                next_one = jnp.where(same, pair[rows:], others[rows:])
                pieces.append(jnp.where(y_place == y, mine, next_one))
        return jnp.concatenate(pieces, axis=0)

    def attn_pack(layer):
        transposed = w_qkv[layer].swapaxes(1, 2).reshape(-1, width)
        return jnp.concatenate([transposed, w_out[layer]], axis=0)

    def spread(own, across):
        return [own, head_swap(own, 1), across, head_swap(across, 1)]

    up_quarter = head_swap(quarter(w_up[0]), 2)
    down_quarter = head_swap(quarter(w_down[0]), 2)
    terms, left = [], own_small
    for _ in range(3):
        term = lax.reduce_precision(left, 8, 7)
        terms.append(term.astype(bf16))
        left = left - term
    fill = jnp.zeros((CELL - 3 * SMALLS, width), bf16)
    own = jnp.concatenate([attn_pack(0), *terms, fill], axis=0)
    up_quarter, down_quarter, own = lax.optimization_barrier((up_quarter, down_quarter, own))
    later = jnp.concatenate([chunk(w_up[1]), chunk(w_down[1])], axis=0)
    marks = (2 * targets + token_mask).reshape(4, WINDOW)
    up_pair, down_pair = along_y(up_quarter), along_y(down_quarter)
    up_x = by_place(up_pair, clip_swap(up_pair, 2))
    across, later, marks, place, up_x, down_pair = lax.optimization_barrier(
        (head_swap(own, 2), later, marks, place, up_x, down_pair)
    )
    attn = [spread(own, across), None]
    order.last = (across,)
    down_others = order.send(clip_swap, down_pair, 2)
    chunk_1 = order.send(head_swap, later, 2)
    smalls = attn[0]
    order.last = (attn[0][1], attn[0][3])
    ups = [w_up, order.send(head_swap, w_up, 1)]
    downs = [w_down, order.send(head_swap, w_down, 1)]
    up_diagonal = order.send(head_swap, up_x, 1)
    packs = [None, None]

    def feed_packs(up_x, down_x):
        return (
            ups, downs,
            [up_x, order.send(head_swap, up_x, 1)],
            [down_x, order.send(head_swap, down_x, 1)],
        )

    kept = []
    inputs = (tokens, marks)
    for layer in range(2):
        x, normed, qkv, att, lse, att_parts, *mark_pieces = order.run(
            lambda *a: attend(layer, place, a, norm_gain, norm_bias, smalls, attn[layer]), *inputs
        )
        order.close()
        if layer == 0:
            gathered = over_clips(tied(chunk_1, x))
            marks = [mark_pieces[0]] + [head_swap(mark_pieces[k], k) for k in (1, 2, 3)]
            down_x = order.run(by_place, down_pair, down_others)
            packs[0] = (ups, downs, [up_x, up_diagonal], [down_x, order.send(head_swap, down_x, 1)])
            order.close()
            own = attn_pack(1)
            attn_across = order.send(head_swap, own, 2)
            attn[1] = [own, head_swap(own, 1), attn_across]
        stream, normed2, active, slope, *outs = order.run(
            lambda a, b: feed(
                layer, place, a, b, attn[layer], vec_bias, norm_gain, norm_bias, smalls, packs[layer]
            ),
            x, att,
        )
        kept.append((x, normed, qkv, att_parts, lse, stream, normed2, active, slope))
        if layer == 0:
            order.close()
            pieces = gathered.reshape(clip_count, 2, -1, width)
            attn[1].append(order.send(head_swap, attn_across, 1))
            inputs = [outs[0]] + [order.send(head_swap, outs[k], k) for k in (1, 2, 3)]
            inputs = [p.reshape(4, 4, CELL, width) for p in inputs]
            order.close()
            packs[1] = feed_packs(pieces[:, 0].reshape(-1, width), pieces[:, 1].reshape(-1, width))
    grad, loss_sum, *parts = order.run(
        lambda a: code_loss(place, a, code_head, marks, active), outs[0]
    )
    down_1 = Pack(order, *parts, halving=False)

    def run_feed_back(layer, grad):
        x, normed, qkv, att, lse, stream, normed2, active, slope = kept[layer]
        return order.run(
            lambda a: feed_back(layer, place, a, slope, stream, normed2, norm_gain, packs[layer]), grad
        )

    def run_attend_back(layer, grad_next, g1):
        x, normed, qkv, att, lse, *_ = kept[layer]
        return order.run(
            lambda a, b: attend_back(
                layer, place, a, b, x, qkv, lse, norm_gain, attn[layer], normed, att
            ),
            grad_next, g1,
        )

    def pack(kind, *arrays, **options):
        parts = order.run(lambda *a: grads(kind, place, a, width), *arrays)
        return Pack(order, *parts, **options)

    def move(*ones):
        for one in ones:
            one.prepare()
        for one in ones:
            one.launch()

    move(down_1)
    order.close()
    move(down_1)
    grad_next, g1, feed_sum_1, *parts = run_feed_back(1, grad)
    up_1 = Pack(order, *parts, halving=False)
    order.close()
    move(up_1)
    down_1.prepare()
    order.close()
    move(up_1, down_1)
    side, *outs, attn_sum_1 = run_attend_back(1, grad_next, g1)
    order.close()

    grad = [outs[0]] + [order.send(head_swap, outs[k], k) for k in (1, 2, 3)]
    grad = [p.reshape(4, BAND, width) for p in grad]
    move(up_1, down_1)
    attn_1 = pack("attn", side, kept[1][1], kept[1][3], g1, late=True)
    order.close()

    move(attn_1)
    g2 = jnp.stack(grad, axis=1).reshape(-1, width)
    down_0 = pack("down", kept[0][7], g2)
    order.close()
    move(down_0)
    for one in (attn_1, down_1, up_1):
        one.prepare()
    order.close()
    move(down_0, attn_1, down_1, up_1)
    grad_next, g1, feed_sum_0, *parts = run_feed_back(0, g2)
    up_0 = Pack(order, *parts)
    order.close()
    move(up_0)
    for one in (down_0, attn_1, up_1, down_1):
        one.prepare()
    order.close()
    move(up_0, down_0, attn_1, up_1, down_1)
    grad_input, attn_sum_0, *parts = run_attend_back(0, grad_next, g1)
    attn_0 = Pack(order, *parts)
    order.close()
    move(attn_0)
    move(attn_1, down_0)
    for one in (up_0, up_1):
        one.prepare()
    order.close()
    move(down_0, attn_0, attn_1, up_0, up_1)
    order.close()

    packed = jnp.concatenate([feed_sum_0, feed_sum_1, attn_sum_0, attn_sum_1, loss_sum], axis=0)
    swaps = [(head_swap, 1), (head_swap, 2)]
    swaps += [(clip_swap, 1 << n) for n in range(clip_count.bit_length() - 1)]

    def pack_step():
        swap, distance = swaps.pop(0)
        return packed + order.send(swap, packed, distance)

    ready = {}

    def write(one, layer, attention, earlier):
        ready[one] = order.run(lambda *a: emit(place, layer, attention, a, earlier), *one.whole())

    late = [down_1, up_1]
    moving = [attn_0, up_0, down_0]
    everyone = moving + late + [attn_1]
    closed = [one for one in everyone if one.done()]
    jobs = [
        (down_1, 1, False, None), (up_1, 1, False, None), (down_0, 0, False, down_1),
        (attn_1, 1, True, None), (up_0, 0, False, up_1), (attn_0, 0, True, attn_1),
    ]
    wait = 0
    while swaps or not all(one.done() for one in moving + late + [attn_1]):
        held = [down_0] if wait == 0 else []
        move(*[one for one in moving + [attn_1] + late if not one.done() and one not in held])
        wait += 1
        if swaps:
            packed = pack_step()
        for job in jobs:
            one, layer, attention, earlier = job
            if one in closed and (earlier is None or earlier in ready):
                write(one, layer, attention, ready.get(earlier))
                jobs.remove(job)
                break
        order.close()
        closed = [one for one in everyone if one.done()]

    for one, layer, attention, earlier in jobs:
        write(one, layer, attention, ready.get(earlier))

    attn_out, up_out, down_out = ready[attn_0], ready[up_0], ready[down_0]

    feed_sums = packed[:16].reshape(2, 8, width)
    attn_sums = packed[16:32].reshape(2, 8, width)
    loss_total = packed[32, 0]
    own_feed = lax.dynamic_index_in_dim(feed_sums, head_index, 1, keepdims=False)
    own_attn = lax.dynamic_index_in_dim(attn_sums, head_index, 1, keepdims=False)
    slot_total = clip_count * frame_counts.shape[0] * FRAMES * SIDE * SIDE

    return (
        loss_total / slot_total,
        grad_input,
        jnp.stack([attn_sums[:, 4], feed_sums[:, 4]], axis=1),
        jnp.stack([attn_sums[:, 5], feed_sums[:, 5]], axis=1),
        attn_out[0].swapaxes(2, 3),
        own_attn[:, : 2 * share].reshape(2, 2, share),
        attn_out[1],
        jnp.stack([feed_sums[:, 7], feed_sums[:, 6]], axis=1),
        up_out[0],
        own_feed,
        down_out[0],
    )


def solution(mesh):
    placed = (
        P(("clip", "head"), None),
        P("clip"),
        P(("clip", "head")),
        P(("clip", "head")),
        P(),
        P(),
        P(None, None, None, "head"),
        P(None, None, "head"),
        P(None, "head", None),
        P(),
        P(None, None, "head"),
        P(None, "head"),
        P(None, "head", None),
        P(),
    )
    return jax.shard_map(
        on_device,
        mesh=mesh,
        in_specs=placed,
        out_specs=(
            P(),
            P(("clip", "head"), None),
            P(),
            P(),
            P(None, None, None, "head"),
            P(None, None, "head"),
            P(None, "head", None),
            P(),
            P(None, None, "head"),
            P(None, "head"),
            P(None, "head", None),
        ),
        check_vma=False,
    )
```

```python
from functools import partial

import jax
import jax.numpy as jnp
from jax import lax
from jax.experimental import pallas as pl
from jax.experimental.pallas import tpu as pltpu
from jax.sharding import PartitionSpec as P

HD = 64
FRAMES = 16
SIDE = 16
TUBE = 4
WINDOW = 256
PAIR = 128
BAND = 64
CELL = 16
LSE_ROWS = 16
SMALLS = 3

epsilon = 1e-06
masked_score = -1e30
f32 = jnp.float32
bf16 = jnp.bfloat16
VMEM_LIMIT = 44 * 1024 * 1024
LIMITS = {"emit": 20 * 1024 * 1024, "grads_down": 24 * 1024 * 1024, "grads_attn": 24 * 1024 * 1024}
TIMES = {
    "attend": 17, "feed": 23, "code_loss": 18, "feed_back": 26, "attend_back": 25,
    "grads_down": 10, "grads_attn": 11, "emit": 3,
}
SCALE = 1.0


def cost_of(name):
    time = TIMES[name] * SCALE
    return pl.CostEstimate(flops=int(time * 1.15e9), bytes_accessed=int(time * 3.6e6), transcendentals=0)


def dot(a, b):
    return lax.dot_general(a, b, (((1,), (0,)), ((), ())), preferred_element_type=f32)


def dot_nt(a, b):
    return lax.dot_general(a, b, (((1,), (1,)), ((), ())), preferred_element_type=f32)


def dot_tn(a, b):
    return lax.dot_general(a, b, (((0,), (0,)), ((), ())), preferred_element_type=f32)


def statistics(stream):
    centre = jnp.mean(stream, axis=-1, keepdims=True)
    centred = stream - centre
    spread = jnp.mean(centred * centred, axis=-1, keepdims=True)
    scale = lax.rsqrt(spread + epsilon)
    return centred * scale, scale


def by_eight(values):
    rows, columns = values.shape
    return jnp.sum(values.reshape(rows // 8, 8, columns), axis=0)


def gather_sums(acc_ref, values):
    first = pl.program_id(0) == 0
    parts = jnp.concatenate([by_eight(v) for v in values], axis=1)

    @pl.when(first)
    def _():
        acc_ref[...] = parts

    @pl.when(jnp.logical_not(first))
    def _():
        acc_ref[...] += parts


ORDER = (1, 3, 0, 2)


def step_rows():
    return pl.ds(pl.multiple_of(pl.program_id(0) * WINDOW, WINDOW), WINDOW)


def put_parts(leaving_ref, staying_ref, buf, sem, gradient_of):
    copies = []
    for n, k in enumerate(ORDER):
        buf[n] = gradient_of(k).astype(bf16)
        target = (leaving_ref if n < 2 else staying_ref).at[n % 2]
        copy = pltpu.make_async_copy(buf.at[n], target, sem.at[n])
        copy.start()
        copies.append(copy)
    for copy in copies:
        copy.wait()


def parts_outs(width):
    return [((2, width, width), bf16, pl.BlockSpec(memory_space=pl.ANY))] * 2


def parts_scratch(width):
    return [pltpu.VMEM((4, width, width), bf16), pltpu.SemaphoreType.DMA((4,))]


def last_step():
    return pl.program_id(0) == pl.num_programs(0) - 1


def norm_back(stream, gain, grad):
    normal, scale = statistics(stream)
    scaled = grad * gain
    mean_plain = jnp.mean(scaled, axis=-1, keepdims=True)
    mean_normal = jnp.mean(scaled * normal, axis=-1, keepdims=True)
    inner = scale * (scaled - mean_plain - normal * mean_normal)
    return inner, grad * normal


def gelu_both(hidden):
    root = 0.7978845608028654
    cubic = 0.044715
    square = hidden * hidden
    bend = jnp.tanh(hidden * (root + root * cubic * square))
    rise = 0.5 + 0.5 * bend
    active = hidden * rise
    slope = rise + (active - active * rise) * (2.0 * root + 6.0 * root * cubic * square)
    return active.astype(bf16), slope.astype(bf16)


def allowed_of(place_ref):
    head_index = place_ref[0]
    frame_count = place_ref[1]

    def valid(axis):
        position = lax.broadcasted_iota(jnp.int32, (WINDOW, WINDOW), axis)
        frame = 4 * ((position >> 6) ^ head_index) + ((position >> 4) & 3)
        return frame < frame_count

    return jnp.logical_or(valid(0), jnp.logical_not(valid(1)))


def shuffle_of(place_ref, axis):
    arranged = lax.broadcasted_iota(jnp.int32, (WINDOW, WINDOW), axis)
    plain = lax.broadcasted_iota(jnp.int32, (WINDOW, WINDOW), 1 - axis)
    band = (arranged >> 6) ^ place_ref[0]
    source = band * BAND + ((arranged >> 2) & 3) * 16 + ((arranged >> 4) & 3) * 4 + (arranged & 3)
    return (source == plain).astype(f32).astype(bf16)


def small_rows(ref, start):
    rows = ref[...].astype(f32)
    terms = [rows[SMALLS * n + start : SMALLS * n + start + 1, :] for n in range(3)]
    return terms[0] + terms[1] + terms[2]


def small_of(a):
    rows, width = a.shape
    return pl.BlockSpec((CELL, width), lambda i, s: (rows // CELL - 1, 0))


def assemble_qkv(packs, scratch):
    width = scratch.shape[1]
    share = width // 4
    for k in range(4):
        for j in range(3):
            start = j * width + k * share
            scratch[start : start + share, :] = packs[k][j * share : (j + 1) * share, :]


def assemble_out(packs, scratch):
    share = scratch.shape[0] // 4
    for k in range(4):
        scratch[k * share : (k + 1) * share, :] = packs[k][3 * share : 4 * share, :]


def stack_heads(pair):
    low = lax.broadcasted_iota(jnp.int32, pair.shape, 1) < HD
    zero = jnp.zeros((), bf16)
    return jnp.concatenate([jnp.where(low, pair, zero), jnp.where(low, zero, pair)], axis=0)


def attend_core(qkv, allowed, att_ref, lse_ref, part_ref):
    width = att_ref.shape[1]
    pairs = width // PAIR

    def part(j, pair):
        return qkv[:, j * width + pair * PAIR : j * width + (pair + 1) * PAIR]

    def scores_of(pair):
        query = part(0, pair) * jnp.asarray(HD ** (-0.5), bf16)
        return dot_nt(stack_heads(part(1, pair)), query)

    ahead = scores_of(0)
    for pair in range(pairs):
        scores = ahead
        if pair + 1 < pairs:
            ahead = scores_of(pair + 1)
        probs = []
        for half in range(2):
            mine = scores[half * WINDOW : (half + 1) * WINDOW]
            if allowed is not None:
                mine = jnp.where(allowed, mine, masked_score)
            top = jnp.max(mine, axis=0, keepdims=True)
            terms = jnp.exp(mine - top)
            total = jnp.sum(terms, axis=0, keepdims=True)
            probs.append((terms * (1.0 / total)).astype(bf16))
            head = 2 * pair + half
            lse_ref[head : head + 1, :] = top + jnp.log(total)
        out = dot_tn(jnp.concatenate(probs, axis=0), stack_heads(part(2, pair)))
        att_ref[:, pair * PAIR : (pair + 1) * PAIR] = out.astype(bf16)
    share = width // 4
    for k in range(4):
        part_ref[k] = att_ref[:, k * share : (k + 1) * share]


def attend_kernel(layer, place_ref, *refs):
    if layer == 0:
        tokens_ref, marks_ref, *refs = refs
        shuffle = shuffle_of(place_ref, 0)
        stream = dot(shuffle, tokens_ref[...])
    else:
        pieces, refs = refs[:4], refs[4:]
        stream = jnp.concatenate(
            [p[...].reshape(BAND, p.shape[-1]) for p in pieces], axis=0
        ).astype(f32)
    gain_ref, shift_ref, s0, s1, s2, s3, p0, p1, p2, p3, x_ref, normed_ref, qkv_ref, att_ref, lse_ref, part_ref, *refs = refs
    *mark_refs, scratch = refs
    share = scratch.shape[1] // 4

    @pl.when(pl.program_id(0) == 0)
    def _():
        assemble_qkv((p0, p1, p2, p3), scratch)

    if layer == 0:
        given = marks_ref[pl.ds(pl.program_id(0), 1), :]
        high = given >> 4
        both = [jnp.broadcast_to(v, (8, WINDOW)) for v in (high, given - 16 * high)]
        both = jnp.concatenate(both, axis=0).astype(f32).astype(bf16)
        both = dot(both, shuffle_of(place_ref, 1))
        marks = 16.0 * both[0:1] + both[8:9]
        for k in range(4):
            mark_refs[k][pl.ds(pl.program_id(0), 1), :] = marks[:, k * BAND : (k + 1) * BAND]
    x_ref[...] = stream.astype(bf16)
    normal, _ = statistics(stream)
    normed = (normal * gain_ref[layer, 0:1] + shift_ref[layer, 0:1]).astype(bf16)
    normed_ref[...] = normed
    start = 2 * layer * share
    smalls = [small_rows(r, 2) for r in (s0, s1, s2, s3)]
    bias = jnp.concatenate(
        [r[:, start : start + share] for r in smalls]
        + [jnp.zeros((1, 4 * share), f32)]
        + [r[:, start + share : start + 2 * share] for r in smalls],
        axis=1,
    )
    qkv = (dot_nt(normed, scratch[...]) + bias).astype(bf16)
    qkv_ref[...] = qkv
    allowed = allowed_of(place_ref) if layer == 1 else None
    attend_core(qkv, allowed, att_ref, lse_ref, part_ref)


def whole(array):
    zeros = (0,) * array.ndim
    return pl.BlockSpec(array.shape, lambda i, s: zeros, pipeline_mode=pl.Buffered(1))


def rows_of(columns, rows=WINDOW):
    return pl.BlockSpec((rows, columns), lambda i, s: (i, 0))


def parts_of(columns):
    return pl.BlockSpec((4, WINDOW, columns), lambda i, s: (0, i, 0))


def tube_of(columns):
    return pl.BlockSpec((4, 1, CELL, columns), lambda i, s: (0, i, 0, 0))


def sums_of(columns):
    return pl.BlockSpec((8, columns), lambda i, s: (0, 0))


def call(kernel, name, place, steps, operands, outs, scratch=(), aliases={}):
    return pl.pallas_call(
        kernel,
        grid_spec=pltpu.PrefetchScalarGridSpec(
            num_scalar_prefetch=1,
            grid=(steps,),
            in_specs=[spec for _, spec in operands],
            out_specs=[spec for _, _, spec in outs],
            scratch_shapes=list(scratch),
        ),
        out_shape=[jax.ShapeDtypeStruct(shape, dtype) for shape, dtype, _ in outs],
        compiler_params=pltpu.CompilerParams(vmem_limit_bytes=LIMITS.get(name, VMEM_LIMIT)),
        cost_estimate=cost_of(name),
        input_output_aliases=aliases,
        name=name,
    )(place, *[array for array, _ in operands])


def attend(layer, place, inputs, gain, shift, smalls, packs):
    width = gain.shape[-1]
    rows = 4 * WINDOW
    if layer == 0:
        tokens, marks = inputs
        first = [(tokens, rows_of(width)), (marks, whole(marks))]
    else:
        first = [(p, tube_of(width)) for p in inputs]
    operands = first + [(a, whole(a)) for a in (gain, shift)]
    operands += [(a, small_of(a)) for a in smalls] + [(a, whole(a)) for a in packs]
    outs = [
        ((rows, width), bf16, rows_of(width)),
        ((rows, width), bf16, rows_of(width)),
        ((rows, 3 * width), bf16, rows_of(3 * width)),
        ((rows, width), bf16, rows_of(width)),
        ((4 * LSE_ROWS, WINDOW), f32, rows_of(WINDOW, LSE_ROWS)),
        ((4, rows, width // 4), bf16, parts_of(width // 4)),
    ]
    if layer == 0:
        outs += [((4, BAND), f32, pl.BlockSpec((4, BAND), lambda i, s: (0, 0)))] * 4
    return call(
        partial(attend_kernel, layer), "attend", place, 4, operands, outs,
        [pltpu.VMEM((3 * width, width), bf16)],
    )


def attend_back_core(qkv, grad, lse_ref, allowed):
    width = grad.shape[1]
    pairs = width // PAIR

    def part(j, pair):
        return qkv[:, j * width + pair * PAIR : j * width + (pair + 1) * PAIR]

    def first_of(pair):
        query = part(0, pair) * jnp.asarray(HD ** (-0.5), bf16)
        grad_part = grad[:, pair * PAIR : (pair + 1) * PAIR]
        keys = stack_heads(part(1, pair))
        scores = dot_nt(keys, query)
        grad_probs = dot_nt(stack_heads(part(2, pair)), grad_part)
        return query, grad_part, keys, scores, grad_probs

    low = lax.broadcasted_iota(jnp.int32, (WINDOW, PAIR), 1) < HD
    results = [[], [], []]
    ahead = first_of(0)
    for pair in range(pairs):
        query, grad_part, keys, scores, grad_probs = ahead
        if pair + 1 < pairs:
            ahead = first_of(pair + 1)
        all_probs, all_scores = [], []
        for half in range(2):
            rows = slice(half * WINDOW, (half + 1) * WINDOW)
            mine = scores[rows]
            if allowed is not None:
                mine = jnp.where(allowed, mine, masked_score)
            head = 2 * pair + half
            probs = jnp.exp(mine - lse_ref[head : head + 1, :])
            grad_mine = grad_probs[rows]
            delta = jnp.sum(probs * grad_mine, axis=0, keepdims=True)
            all_probs.append(probs.astype(bf16))
            all_scores.append((probs * (grad_mine - delta)).astype(bf16))
        probs = jnp.concatenate(all_probs, axis=0)
        grad_scores = jnp.concatenate(all_scores, axis=0)
        grad_query = dot_tn(grad_scores, keys) * HD ** (-0.5)
        grad_key = dot(grad_scores, query)
        grad_value = dot(probs, grad_part)
        results[0].append(grad_query.astype(bf16))
        results[1].append(jnp.where(low, grad_key[:WINDOW], grad_key[WINDOW:]).astype(bf16))
        results[2].append(jnp.where(low, grad_value[:WINDOW], grad_value[WINDOW:]).astype(bf16))
    return [jnp.concatenate(part, axis=1) for part in results]


def attend_back_kernel(layer, place_ref, *refs):
    (stream_ref, g1_ref, x_ref, qkv_ref, lse_ref, gain_ref, p0, p1, p2, p3, *outs) = refs
    if layer == 1:
        side_ref, *outs = outs
        pieces, outs = outs[:4], outs[4:]
        sums_ref, scratch, out_scratch, acc = outs
        rows = slice(None)
    else:
        (
            normed_ref, part_ref, final_ref, sums_ref, leaving_ref, staying_ref,
            scratch, out_scratch, acc, side_ref, all_normed, all_parts, all_g1, buf, sem,
        ) = outs
        rows = step_rows()
        all_normed[rows, :] = normed_ref[...]
        all_g1[rows, :] = g1_ref[...]
        for k in range(4):
            all_parts[k, rows, :] = part_ref[k]
    width = stream_ref.shape[1]
    share = width // 4

    @pl.when(pl.program_id(0) == 0)
    def _():
        assemble_qkv((p0, p1, p2, p3), scratch)
        assemble_out((p0, p1, p2, p3), out_scratch)

    grad_att = dot_nt(g1_ref[...], out_scratch[...]).astype(bf16)
    allowed = allowed_of(place_ref) if layer == 1 else None
    parts = attend_back_core(qkv_ref[...], grad_att, lse_ref, allowed)
    for k in range(4):
        for j in range(3):
            side_ref[k, rows, j * share : (j + 1) * share] = parts[j][:, k * share : (k + 1) * share]
    joined = jnp.concatenate(parts, axis=1)
    grad_normed = dot(joined, scratch[...])
    inner, scaled = norm_back(x_ref[...].astype(f32), gain_ref[layer, 0:1], grad_normed)
    gather_sums(acc, [parts[0].astype(f32), parts[2].astype(f32), scaled, grad_normed])
    stream = stream_ref[...] + inner
    if layer == 1:
        for k in range(4):
            pieces[k][...] = (
                stream[k * BAND : (k + 1) * BAND].astype(bf16).reshape(4, 1, CELL, width)
            )
    else:
        shuffle = shuffle_of(place_ref, 1)
        high = stream.astype(bf16)
        low = (stream - high.astype(f32)).astype(bf16)
        final_ref[...] = dot(shuffle, high) + dot(shuffle, low)

    @pl.when(last_step())
    def _():
        total = jnp.sum(acc[...], axis=0, keepdims=True)
        sums_ref[...] = jnp.zeros(sums_ref.shape, f32)
        for k in range(4):
            query = total[:, k * share : (k + 1) * share]
            value = total[:, width + k * share : width + (k + 1) * share]
            sums_ref[pl.ds(place_ref[0] ^ k, 1), : 2 * share] = jnp.concatenate([query, value], axis=1)
        sums_ref[4:5, :] = total[:, 2 * width : 3 * width]
        sums_ref[5:6, :] = total[:, 3 * width :]
        if layer == 0:

            def gradient_of(k):
                upper = dot_tn(side_ref[k], all_normed[...])
                lower = dot_tn(all_parts[k], all_g1[...])
                return jnp.concatenate([upper, lower], axis=0)

            put_parts(leaving_ref, staying_ref, buf, sem, gradient_of)


def attend_back(layer, place, stream, g1, x, qkv, lse, gain, packs, normed, attended):
    rows, width = stream.shape
    share = width // 4
    operands = [
        (stream, rows_of(width)),
        (g1, rows_of(width)),
        (x, rows_of(width)),
        (qkv, rows_of(3 * width)),
        (lse, rows_of(WINDOW, LSE_ROWS)),
    ] + [(a, whole(a)) for a in (gain, *packs)]
    sums = [((8, width), f32, sums_of(width))]
    scratch = [
        pltpu.VMEM((3 * width, width), bf16), pltpu.VMEM((width, width), bf16), pltpu.VMEM((8, 4 * width), f32)
    ]
    if layer == 1:
        outs = [((4, rows, 3 * share), bf16, parts_of(3 * share))]
        outs = outs + [((4, 4, CELL, width), bf16, tube_of(width))] * 4 + sums
    else:
        operands += [(normed, rows_of(width)), (attended, parts_of(share))]
        outs = [((rows, width), f32, rows_of(width))] + sums + parts_outs(width)
        scratch += [
            pltpu.VMEM((4, rows, 3 * share), bf16), pltpu.VMEM((rows, width), bf16),
            pltpu.VMEM((4, rows, share), bf16), pltpu.VMEM((rows, width), bf16),
        ] + parts_scratch(width)
    return call(partial(attend_back_kernel, layer), "attend_back", place, 4, operands, outs, scratch)


def feed_kernel(layer, place_ref, *refs):
    (
        x_ref, att_ref, a0, a1, a2, a3, vec_ref, gain_ref, shift_ref, s0, s1, s2, s3,
        u0, u1, u2, u3, d0, d1, d2, d3, stream_ref, normed_ref, active_ref, slope_ref, *outs
    ) = refs
    ups, downs = (u0, u1, u2, u3), (d0, d1, d2, d3)
    *pieces, scratch = outs
    width = x_ref.shape[1]

    @pl.when(pl.program_id(0) == 0)
    def _():
        share = width // 4
        for k, part in enumerate((a0, a1, a2, a3)):
            scratch[k * share : (k + 1) * share, :] = part[...]

    stream = x_ref[...].astype(f32) + dot(att_ref[...], scratch[...]) + vec_ref[layer, 0:1]
    stream_ref[...] = stream
    normal, _ = statistics(stream)
    normed = (normal * gain_ref[layer, 1:2] + shift_ref[layer, 1:2]).astype(bf16)
    normed_ref[...] = normed
    total = stream + vec_ref[layer, 1:2]
    units = u0.shape[1]
    ahead = dot(normed, ups[0][...])
    for k in range(4):
        hidden = ahead
        if k < 3:
            ahead = dot(normed, ups[k + 1][...])
        cut = slice(k * units, (k + 1) * units)
        active, slope = gelu_both(hidden + small_rows((s0, s1, s2, s3)[k], layer))
        active_ref[:, cut] = active
        slope_ref[:, cut] = slope
        total = total + dot(active, downs[k][...])
    total = total.astype(bf16)
    if layer == 0:
        for k in range(4):
            pieces[k][...] = total[k * BAND : (k + 1) * BAND].reshape(1, BAND, width)
    else:
        pieces[0][...] = total


def feed_specs(layer, packs):
    ups, downs, ups_across, downs_across = packs

    def of_layer(a):
        return (a, pl.BlockSpec(
            (None, *a.shape[1:]), lambda i, s: (layer, 0, 0), pipeline_mode=pl.Buffered(1)
        ))

    return [
        *[of_layer(a) for a in ups],
        *[(a, whole(a)) for a in ups_across],
        *[of_layer(a) for a in downs],
        *[(a, whole(a)) for a in downs_across],
    ]


def feed(layer, place, x, att, attn_packs, vecs, gain, shift, smalls, packs):
    rows, width = x.shape
    units = packs[0][0].shape[2]
    last = pl.BlockSpec((width // 4, width), lambda i, s: (3, 0))
    operands = (
        [(x, rows_of(width)), (att, rows_of(width))]
        + [(a, last) for a in attn_packs]
        + [(a, whole(a)) for a in (vecs, gain, shift)]
        + [(a, small_of(a)) for a in smalls]
        + feed_specs(layer, packs)
    )
    outs = [
        ((rows, width), f32, rows_of(width)),
        ((rows, width), bf16, rows_of(width)),
        ((rows, 4 * units), bf16, rows_of(4 * units)),
        ((rows, 4 * units), bf16, rows_of(4 * units)),
    ]
    if layer == 0:
        piece = pl.BlockSpec((1, BAND, width), lambda i, s: (i, 0, 0))
        outs = outs + [((4, BAND, width), bf16, piece)] * 4
    else:
        outs = outs + [((rows, width), bf16, rows_of(width))]
    return call(
        partial(feed_kernel, layer), "feed", place, 4, operands, outs,
        [pltpu.VMEM((width, width), bf16)],
    )


def loss_kernel(
    place_ref, final_ref, head_ref, m0, m1, m2, m3, active_ref, grad_ref, loss_ref, leaving_ref, staying_ref,
    acc, all_active, all_g2, buf, sem,
):
    logits = dot(final_ref[...], head_ref[...])
    spread = jnp.concatenate(
        [jnp.broadcast_to(m[f : f + 1, :], (CELL, BAND)) for m in (m0, m1, m2, m3) for f in range(4)],
        axis=0,
    )
    position = lax.broadcasted_iota(jnp.int32, (WINDOW, BAND), 0)
    lane = lax.broadcasted_iota(jnp.int32, (WINDOW, BAND), 1)
    mine = lane == pl.program_id(0) * CELL + (position & (CELL - 1))
    mark = jnp.sum(jnp.where(mine, spread, 0.0), axis=1, keepdims=True).astype(jnp.int32)
    place_of = lax.broadcasted_iota(jnp.int32, (WINDOW, 1), 0)
    frame = 4 * ((place_of >> 6) ^ place_ref[0]) + ((place_of >> 4) & 3)
    weight = jnp.where(frame < place_ref[1], (mark & 1).astype(f32), 0.0)
    top = jnp.max(logits, axis=1, keepdims=True)
    terms = jnp.exp(logits - top)
    total = jnp.sum(terms, axis=1, keepdims=True)
    code = lax.broadcasted_iota(jnp.int32, logits.shape, 1)
    chosen = code == (mark >> 1)
    picked = jnp.sum(jnp.where(chosen, logits, 0.0), axis=1, keepdims=True)
    entry = weight * (top + jnp.log(total) - picked)
    soft = terms * (1.0 / total)
    grad_logits = (weight * (soft - jnp.where(chosen, 1.0, 0.0))).astype(bf16)
    grad = dot_nt(grad_logits, head_ref[...])
    grad_ref[...] = grad
    all_g2[step_rows(), :] = grad.astype(bf16)
    all_active[step_rows(), :] = active_ref[...]
    gather_sums(acc, [jnp.broadcast_to(entry, (WINDOW, PAIR))])

    @pl.when(last_step())
    def _():
        total = jnp.sum(acc[...], axis=0, keepdims=True)
        loss_ref[...] = jnp.broadcast_to(total[:, :1], loss_ref.shape)
        width = grad_ref.shape[1]
        put_parts(
            leaving_ref, staying_ref, buf, sem,
            lambda k: dot_tn(all_active[:, k * width : (k + 1) * width], all_g2[...]),
        )


def code_loss(place, final, code_head, marks, active):
    rows, width = final.shape
    operands = [(final, rows_of(width))] + [(a, whole(a)) for a in (code_head, *marks)]
    operands += [(active, rows_of(active.shape[1]))]
    outs = [
        ((rows, width), f32, rows_of(width)),
        ((8, width), f32, sums_of(width)),
    ] + parts_outs(width)
    scratch = [
        pltpu.VMEM((8, PAIR), f32), pltpu.VMEM(active.shape, bf16), pltpu.VMEM((rows, width), bf16)
    ] + parts_scratch(width)
    return call(loss_kernel, "code_loss", place, 4, operands, outs, scratch)


def feed_back_kernel(layer, place_ref, *refs):
    if layer == 1:
        grad_ref, *refs = refs
        grad = grad_ref[...]
    else:
        grad_ref, *refs = refs
        grad = grad_ref[...].astype(f32)
    (
        slope_ref, stream_ref, normed_ref, gain_ref, u0, u1, u2, u3, d0, d1, d2, d3, next_ref, g1_ref,
        sums_ref, leaving_ref, staying_ref, acc, all_hidden, all_normed, buf, sem,
    ) = refs
    all_normed[step_rows(), :] = normed_ref[...]
    g2 = grad.astype(bf16)
    units = u0.shape[1]
    grad_normed = jnp.zeros(grad.shape, f32)
    sums = []
    ups, downs = (u0, u1, u2, u3), (d0, d1, d2, d3)
    ahead = dot_nt(g2, downs[0][...])
    for k in range(4):
        grad_active = ahead
        if k < 3:
            ahead = dot_nt(g2, downs[k + 1][...])
        cut = slice(k * units, (k + 1) * units)
        grad_hidden = (grad_active * slope_ref[:, cut].astype(f32)).astype(bf16)
        all_hidden[step_rows(), cut] = grad_hidden
        sums.append(grad_hidden.astype(f32))
        grad_normed = grad_normed + dot_nt(grad_hidden, ups[k][...])
    inner, scaled = norm_back(stream_ref[...], gain_ref[layer, 1:2], grad_normed)
    grad = grad + inner
    next_ref[...] = grad
    g1 = grad.astype(bf16)
    g1_ref[...] = g1
    gather_sums(acc, sums + [scaled, grad_normed, g2.astype(f32), g1.astype(f32)])

    @pl.when(last_step())
    def _():
        total = jnp.sum(acc[...], axis=0, keepdims=True)
        for k in range(4):
            sums_ref[pl.ds(place_ref[0] ^ k, 1), :] = total[:, k * units : (k + 1) * units]
            start = 4 * units + k * grad.shape[1]
            sums_ref[4 + k : 5 + k, :] = total[:, start : start + grad.shape[1]]
        put_parts(
            leaving_ref, staying_ref, buf, sem,
            lambda k: dot_tn(all_normed[...], all_hidden[:, k * units : (k + 1) * units]),
        )


def feed_back(layer, place, grad, slope, stream, normed, gain, packs):
    rows, width = stream.shape
    units = packs[0][0].shape[2]
    operands = (
        [(grad, rows_of(width)), (slope, rows_of(4 * units)), (stream, rows_of(width)), (normed, rows_of(width))]
        + [(gain, whole(gain))]
        + feed_specs(layer, packs)
    )
    outs = [
        ((rows, width), f32, rows_of(width)),
        ((rows, width), bf16, rows_of(width)),
        ((8, width), f32, sums_of(width)),
    ] + parts_outs(width)
    scratch = [
        pltpu.VMEM((8, 4 * units + 4 * width), f32),
        pltpu.VMEM((rows, 4 * units), bf16),
        pltpu.VMEM((rows, width), bf16),
    ] + parts_scratch(width)
    return call(partial(feed_back_kernel, layer), "feed_back", place, 4, operands, outs, scratch)


def grad_kernel(kind, place_ref, *refs):
    *inputs, leaving_ref, staying_ref = refs
    if kind == "attn":
        side_ref, normed_ref, part_ref, g1_ref = inputs
        upper = dot_tn(side_ref[...], normed_ref[...])
        lower = dot_tn(part_ref[...], g1_ref[...])
        value = jnp.concatenate([upper, lower], axis=0)
    else:
        left_ref, right_ref = inputs
        value = dot_tn(left_ref[...], right_ref[...])
    value = value.astype(bf16)
    step = pl.program_id(0)

    @pl.when(step < 2)
    def _():
        leaving_ref[...] = value

    @pl.when(step >= 2)
    def _():
        staying_ref[...] = value


def grads(kind, place, arrays, width):
    rows = arrays[1].shape[0]

    def part_at(i):
        return jnp.where(i < 2, 2 * i + 1, 2 * i - 4)

    part = pl.BlockSpec((rows, width), lambda i, s: (0, part_at(i)))

    def of_part(a):
        return pl.BlockSpec((None, *a.shape[1:]), lambda i, s: (part_at(i), 0, 0))

    if kind == "attn":
        side, normed, attended, g1 = arrays
        specs = [of_part(side), whole(normed), of_part(attended), whole(g1)]
    elif kind == "up":
        specs = [whole(arrays[0]), part]
    else:
        specs = [part, whole(arrays[1])]
    block = (None, width, width)
    outs = [
        ((2, width, width), bf16, pl.BlockSpec(block, lambda i, s: (jnp.minimum(i, 1), 0, 0))),
        ((2, width, width), bf16, pl.BlockSpec(block, lambda i, s: (jnp.maximum(i - 2, 0), 0, 0))),
    ]
    return call(
        partial(grad_kernel, kind), "grads_" + kind, place, 4, list(zip(arrays, specs)), outs
    )


def emit_kernel(attention, aliased, place_ref, mine_ref, other_ref, *refs):
    outs = refs[aliased:]
    half, width = mine_ref.shape
    upper = place_ref[2] == 1
    mine, other = mine_ref[...].astype(f32), other_ref[...].astype(f32)
    low, high = jnp.where(upper, other, mine), jnp.where(upper, mine, other)
    if attention:
        qkv_ref, out_ref = outs
        share = width // 4
        qkv_ref[0, 0], qkv_ref[0, 1] = low[:share], low[share:]
        qkv_ref[0, 2], out_ref[0] = high[:share], high[share:]
    else:
        outs[0][0, :half] = low
        outs[0][0, half:] = high


def emit(place, layer, attention, summed, earlier):
    width = summed[0].shape[1]
    share = width // 4
    if attention:
        outs = [
            ((2, 3, share, width), f32, pl.BlockSpec((1, 3, share, width), lambda i, s: (layer, 0, 0, 0))),
            ((2, share, width), f32, pl.BlockSpec((1, share, width), lambda i, s: (layer, 0, 0))),
        ]
    else:
        outs = [((2, width, width), f32, pl.BlockSpec((1, width, width), lambda i, s: (layer, 0, 0)))]
    operands = [(a, whole(a)) for a in summed]
    aliases = {}
    if earlier is not None:
        aliases = {3 + n: n for n in range(len(earlier))}
        operands += [(e, pl.BlockSpec(memory_space=pl.ANY)) for e in earlier]
    return call(
        partial(emit_kernel, attention, len(aliases)), "emit", place, 1, operands, outs, aliases=aliases
    )


def head_swap(values, distance):
    count = lax.axis_size("head")
    return lax.ppermute(values, "head", [(i, i ^ distance) for i in range(count)])


def clip_swap(values, distance):
    count = lax.axis_size("clip")
    return lax.ppermute(values, "clip", [(i, i ^ distance) for i in range(count)])


class Order:
    def __init__(self):
        self.last = ()
        self.pending = []

    def run(self, step, *values):
        values, _ = lax.optimization_barrier((values, self.last))
        out = step(*values)
        self.last = (jax.tree.leaves(out)[0],)
        return out

    def send(self, swap, values, distance):
        values, _ = lax.optimization_barrier((values, self.last))
        out = swap(values, distance)
        self.pending.append(out)
        return out

    def close(self):
        self.last = self.last + tuple(self.pending)
        self.pending = []


def split_halves(total, upper):
    half = total.shape[-2] // 2
    low, high = total[..., :half, :], total[..., half:, :]
    return jnp.where(upper, low, high).astype(bf16), jnp.where(upper, high, low).astype(bf16)


def join_halves(mine, other, upper):
    return jnp.concatenate(
        [jnp.where(upper, other, mine), jnp.where(upper, mine, other)], axis=0
    )


class Pack:
    def __init__(self, order, leaving, staying, halving=True, late=False):
        self.order = order
        self.late = late
        self.out, self.kept = leaving, staying
        levels = lax.axis_size("clip").bit_length() - 1
        clip = lax.axis_index("clip")
        self.uppers = [((clip >> n) & 1) == 1 for n in range(levels)]
        depth = levels - 1 if halving else 1
        down = [("halve", n) for n in range(depth)]
        level = [("all", n) for n in range(depth, levels)]
        up = [("join", n) for n in reversed(range(depth))]
        if late:
            self.stages = ["core"] + down + ["across"] + level + up
        else:
            self.stages = ["core", "across"] + down + level + up
        self.at = 0
        self.prepared = False

    def prepare(self):
        if self.prepared:
            return
        self.prepared = True
        stage = self.stages[self.at]
        run = self.order.run
        if stage == "core":
            self.leaving = self.out
        elif self.late and stage == "across":

            def parted(total, moved):
                total = total.astype(f32) + moved.astype(f32)
                return total[1].astype(bf16), total[0].astype(bf16)

            self.leaving, self.sum = run(parted, self.sum, self.moved)
        elif self.late and self.at == 1:
            upper = self.uppers[stage[1]]

            def halved(kept, near):
                return split_halves(kept.astype(f32) + near.astype(f32), upper)

            self.leaving, self.sum = run(halved, self.kept, self.near)
        elif stage == "across":
            self.leaving = run(
                lambda kept, near: (kept[1].astype(f32) + near[1].astype(f32)).astype(bf16),
                self.kept, self.near,
            )
        else:
            kind, level = stage
            upper = self.uppers[level]
            if self.at == 2 and not self.late:
                start = lambda kept, near, moved: (
                    kept[0].astype(f32) + near[0].astype(f32) + moved.astype(f32)
                )
                values = (self.kept, self.near, self.moved)
            else:
                start = lambda total, moved: total.astype(f32) + moved.astype(f32)
                values = (self.sum, self.moved)
            if kind == "halve":
                self.leaving, self.sum = run(lambda *v: split_halves(start(*v), upper), *values)
            elif kind == "all" or self.stages[self.at - 1][0] == "all":
                self.leaving = self.sum = run(lambda *v: start(*v).astype(bf16), *values)
            else:
                before = self.uppers[self.stages[self.at - 1][1]]
                self.leaving = self.sum = run(
                    lambda mine, other: join_halves(mine, other, before), self.sum, self.moved
                )

    def launch(self):
        stage = self.stages[self.at]
        send = self.order.send
        if stage == "core":
            self.near = send(head_swap, self.leaving, 1)
        elif stage == "across":
            self.moved = send(head_swap, self.leaving, 2)
        else:
            self.moved = send(clip_swap, self.leaving, 1 << stage[1])
        self.at += 1
        self.prepared = False

    def done(self):
        return self.at == len(self.stages)

    def whole(self):
        assert self.done()
        return self.sum, self.moved


def on_device(
    tokens,
    frame_counts,
    token_mask,
    targets,
    norm_gain,
    norm_bias,
    w_qkv,
    qv_bias,
    w_out,
    vec_bias,
    w_up,
    up_bias,
    w_down,
    code_head,
):
    head_index = lax.axis_index("head")
    width = tokens.shape[1]
    share = w_out.shape[1]
    upper = lax.axis_index("clip") & 1
    place = jnp.stack(
        [head_index.astype(jnp.int32), frame_counts[0], upper.astype(jnp.int32)]
    )
    order = Order()

    def tied(values, *after):
        return lax.optimization_barrier((values, after))[0]

    clip_count = lax.axis_size("clip")
    own_small = jnp.concatenate([up_bias, qv_bias.reshape(1, width)], axis=0)
    clip_index = lax.axis_index("clip")

    def chunk(matrix):
        piece = matrix.shape[0] // clip_count
        return lax.dynamic_slice_in_dim(matrix, clip_index * piece, piece, 0)

    def over_clips(chunk_across):
        return lax.all_gather(chunk_across, "clip", axis=0, tiled=True)

    y_place, z_place = clip_index & 1, (clip_index >> 1) & 1

    def quarter(matrix):
        rows = matrix.shape[0] // 4
        return lax.dynamic_slice_in_dim(matrix, (2 * y_place + z_place) * rows, rows, 0)

    def along_y(first):
        return jnp.concatenate([first, clip_swap(first, 1)], axis=0)

    def by_place(pair, others):
        rows = pair.shape[0] // 2
        pieces = []
        for y in range(2):
            for z in range(2):
                same = z_place == z
                mine = jnp.where(same, pair[:rows], others[:rows])
                next_one = jnp.where(same, pair[rows:], others[rows:])
                pieces.append(jnp.where(y_place == y, mine, next_one))
        return jnp.concatenate(pieces, axis=0)

    def attn_pack(layer):
        transposed = w_qkv[layer].swapaxes(1, 2).reshape(-1, width)
        return jnp.concatenate([transposed, w_out[layer]], axis=0)

    def spread(own, across):
        return [own, head_swap(own, 1), across, head_swap(across, 1)]

    up_quarter = head_swap(quarter(w_up[0]), 2)
    down_quarter = head_swap(quarter(w_down[0]), 2)
    terms, left = [], own_small
    for _ in range(3):
        term = lax.reduce_precision(left, 8, 7)
        terms.append(term.astype(bf16))
        left = left - term
    fill = jnp.zeros((CELL - 3 * SMALLS, width), bf16)
    own = jnp.concatenate([attn_pack(0), *terms, fill], axis=0)
    up_quarter, down_quarter, own = lax.optimization_barrier((up_quarter, down_quarter, own))
    later = jnp.concatenate([chunk(w_up[1]), chunk(w_down[1])], axis=0)
    marks = (2 * targets + token_mask).reshape(4, WINDOW)
    up_pair, down_pair = along_y(up_quarter), along_y(down_quarter)
    up_x = by_place(up_pair, clip_swap(up_pair, 2))
    across, later, marks, place, up_x, down_pair = lax.optimization_barrier(
        (head_swap(own, 2), later, marks, place, up_x, down_pair)
    )
    attn = [spread(own, across), None]
    order.last = (across,)
    down_others = order.send(clip_swap, down_pair, 2)
    chunk_1 = order.send(head_swap, later, 2)
    smalls = attn[0]
    order.last = (attn[0][1], attn[0][3])
    ups = [w_up, order.send(head_swap, w_up, 1)]
    downs = [w_down, order.send(head_swap, w_down, 1)]
    up_diagonal = order.send(head_swap, up_x, 1)
    packs = [None, None]

    def feed_packs(up_x, down_x):
        return (
            ups, downs,
            [up_x, order.send(head_swap, up_x, 1)],
            [down_x, order.send(head_swap, down_x, 1)],
        )

    kept = []
    inputs = (tokens, marks)
    for layer in range(2):
        x, normed, qkv, att, lse, att_parts, *mark_pieces = order.run(
            lambda *a: attend(layer, place, a, norm_gain, norm_bias, smalls, attn[layer]), *inputs
        )
        order.close()
        if layer == 0:
            gathered = over_clips(tied(chunk_1, x))
            marks = [mark_pieces[0]] + [head_swap(mark_pieces[k], k) for k in (1, 2, 3)]
            down_x = order.run(by_place, down_pair, down_others)
            packs[0] = (ups, downs, [up_x, up_diagonal], [down_x, order.send(head_swap, down_x, 1)])
            order.close()
            own = attn_pack(1)
            attn_across = order.send(head_swap, own, 2)
            attn[1] = [own, head_swap(own, 1), attn_across]
        stream, normed2, active, slope, *outs = order.run(
            lambda a, b: feed(
                layer, place, a, b, attn[layer], vec_bias, norm_gain, norm_bias, smalls, packs[layer]
            ),
            x, att,
        )
        kept.append((x, normed, qkv, att_parts, lse, stream, normed2, active, slope))
        if layer == 0:
            order.close()
            pieces = gathered.reshape(clip_count, 2, -1, width)
            attn[1].append(order.send(head_swap, attn_across, 1))
            inputs = [outs[0]] + [order.send(head_swap, outs[k], k) for k in (1, 2, 3)]
            inputs = [p.reshape(4, 4, CELL, width) for p in inputs]
            order.close()
            packs[1] = feed_packs(pieces[:, 0].reshape(-1, width), pieces[:, 1].reshape(-1, width))
    grad, loss_sum, *parts = order.run(
        lambda a: code_loss(place, a, code_head, marks, active), outs[0]
    )
    down_1 = Pack(order, *parts, halving=False)

    def run_feed_back(layer, grad):
        x, normed, qkv, att, lse, stream, normed2, active, slope = kept[layer]
        return order.run(
            lambda a: feed_back(layer, place, a, slope, stream, normed2, norm_gain, packs[layer]), grad
        )

    def run_attend_back(layer, grad_next, g1):
        x, normed, qkv, att, lse, *_ = kept[layer]
        return order.run(
            lambda a, b: attend_back(
                layer, place, a, b, x, qkv, lse, norm_gain, attn[layer], normed, att
            ),
            grad_next, g1,
        )

    def pack(kind, *arrays, **options):
        parts = order.run(lambda *a: grads(kind, place, a, width), *arrays)
        return Pack(order, *parts, **options)

    def move(*ones):
        for one in ones:
            one.prepare()
        for one in ones:
            one.launch()

    move(down_1)
    order.close()
    move(down_1)
    grad_next, g1, feed_sum_1, *parts = run_feed_back(1, grad)
    up_1 = Pack(order, *parts, halving=False)
    order.close()
    move(up_1)
    down_1.prepare()
    order.close()
    move(up_1, down_1)
    side, *outs, attn_sum_1 = run_attend_back(1, grad_next, g1)
    order.close()

    grad = [outs[0]] + [order.send(head_swap, outs[k], k) for k in (1, 2, 3)]
    grad = [p.reshape(4, BAND, width) for p in grad]
    move(up_1, down_1)
    attn_1 = pack("attn", side, kept[1][1], kept[1][3], g1, late=True)
    order.close()

    move(attn_1)
    g2 = jnp.stack(grad, axis=1).reshape(-1, width)
    down_0 = pack("down", kept[0][7], g2)
    order.close()
    move(down_0)
    for one in (attn_1, down_1, up_1):
        one.prepare()
    order.close()
    move(down_0, attn_1, down_1, up_1)
    grad_next, g1, feed_sum_0, *parts = run_feed_back(0, g2)
    up_0 = Pack(order, *parts)
    order.close()
    move(up_0)
    for one in (attn_1, up_1, down_1, down_0):
        one.prepare()
    order.close()
    move(up_0, down_0, attn_1, up_1, down_1)
    grad_input, attn_sum_0, *parts = run_attend_back(0, grad_next, g1)
    attn_0 = Pack(order, *parts)
    order.close()
    move(attn_0)
    move(attn_1, down_0)
    for one in (up_0, up_1):
        one.prepare()
    order.close()
    move(down_0, attn_0, attn_1, up_0, up_1)
    order.close()

    packed = jnp.concatenate([feed_sum_0, feed_sum_1, attn_sum_0, attn_sum_1, loss_sum], axis=0)
    swaps = [(head_swap, 1), (head_swap, 2)]
    swaps += [(clip_swap, 1 << n) for n in range(clip_count.bit_length() - 1)]

    def pack_step():
        swap, distance = swaps.pop(0)
        return packed + order.send(swap, packed, distance)

    ready = {}

    def write(one, layer, attention, earlier):
        ready[one] = order.run(lambda *a: emit(place, layer, attention, a, earlier), *one.whole())

    late = [down_1, up_1]
    moving = [attn_0, up_0, down_0]
    everyone = moving + late + [attn_1]
    closed = [one for one in everyone if one.done()]
    jobs = [
        (down_1, 1, False, None), (up_1, 1, False, None), (down_0, 0, False, down_1),
        (attn_1, 1, True, None), (up_0, 0, False, up_1), (attn_0, 0, True, attn_1),
    ]
    wait = 0
    while swaps or not all(one.done() for one in moving + late + [attn_1]):
        held = [down_0] if wait == 0 else []
        move(*[one for one in moving + [attn_1] + late if not one.done() and one not in held])
        wait += 1
        if swaps:
            packed = pack_step()
        for job in jobs:
            one, layer, attention, earlier = job
            if one in closed and (earlier is None or earlier in ready):
                write(one, layer, attention, ready.get(earlier))
                jobs.remove(job)
                break
        order.close()
        closed = [one for one in everyone if one.done()]

    for one, layer, attention, earlier in jobs:
        write(one, layer, attention, ready.get(earlier))

    attn_out, up_out, down_out = ready[attn_0], ready[up_0], ready[down_0]

    feed_sums = packed[:16].reshape(2, 8, width)
    attn_sums = packed[16:32].reshape(2, 8, width)
    loss_total = packed[32, 0]
    own_feed = lax.dynamic_index_in_dim(feed_sums, head_index, 1, keepdims=False)
    own_attn = lax.dynamic_index_in_dim(attn_sums, head_index, 1, keepdims=False)
    slot_total = clip_count * frame_counts.shape[0] * FRAMES * SIDE * SIDE

    return (
        loss_total / slot_total,
        grad_input,
        jnp.stack([attn_sums[:, 4], feed_sums[:, 4]], axis=1),
        jnp.stack([attn_sums[:, 5], feed_sums[:, 5]], axis=1),
        attn_out[0].swapaxes(2, 3),
        own_attn[:, : 2 * share].reshape(2, 2, share),
        attn_out[1],
        jnp.stack([feed_sums[:, 7], feed_sums[:, 6]], axis=1),
        up_out[0],
        own_feed,
        down_out[0],
    )


def solution(mesh):
    placed = (
        P(("clip", "head"), None),
        P("clip"),
        P(("clip", "head")),
        P(("clip", "head")),
        P(),
        P(),
        P(None, None, None, "head"),
        P(None, None, "head"),
        P(None, "head", None),
        P(),
        P(None, None, "head"),
        P(None, "head"),
        P(None, "head", None),
        P(),
    )
    return jax.shard_map(
        on_device,
        mesh=mesh,
        in_specs=placed,
        out_specs=(
            P(),
            P(("clip", "head"), None),
            P(),
            P(),
            P(None, None, None, "head"),
            P(None, None, "head"),
            P(None, "head", None),
            P(),
            P(None, None, "head"),
            P(None, "head"),
            P(None, "head", None),
        ),
        check_vma=False,
    )
```

```python
from functools import partial

import jax
import jax.numpy as jnp
from jax import lax
from jax.experimental import pallas as pl
from jax.experimental.pallas import tpu as pltpu
from jax.sharding import PartitionSpec as P

HD = 64
FRAMES = 16
SIDE = 16
TUBE = 4
WINDOW = 256
PAIR = 128
BAND = 64
CELL = 16
LSE_ROWS = 16
SMALLS = 3

epsilon = 1e-06
masked_score = -1e30
f32 = jnp.float32
bf16 = jnp.bfloat16
VMEM_LIMIT = 44 * 1024 * 1024
LIMITS = {"emit": 20 * 1024 * 1024, "grads_down": 24 * 1024 * 1024, "grads_attn": 24 * 1024 * 1024}
TIMES = {
    "attend": 17, "feed": 23, "code_loss": 18, "feed_back": 26, "attend_back": 25,
    "grads_down": 10, "grads_attn": 11, "emit": 3,
}
SCALE = 1.0


def cost_of(name):
    time = TIMES[name] * SCALE
    return pl.CostEstimate(flops=int(time * 1.15e9), bytes_accessed=int(time * 3.6e6), transcendentals=0)


def dot(a, b):
    return lax.dot_general(a, b, (((1,), (0,)), ((), ())), preferred_element_type=f32)


def dot_nt(a, b):
    return lax.dot_general(a, b, (((1,), (1,)), ((), ())), preferred_element_type=f32)


def dot_tn(a, b):
    return lax.dot_general(a, b, (((0,), (0,)), ((), ())), preferred_element_type=f32)


def statistics(stream):
    centre = jnp.mean(stream, axis=-1, keepdims=True)
    centred = stream - centre
    spread = jnp.mean(centred * centred, axis=-1, keepdims=True)
    scale = lax.rsqrt(spread + epsilon)
    return centred * scale, scale


def by_eight(values):
    rows, columns = values.shape
    return jnp.sum(values.reshape(rows // 8, 8, columns), axis=0)


def gather_sums(acc_ref, values):
    first = pl.program_id(0) == 0
    parts = jnp.concatenate([by_eight(v) for v in values], axis=1)

    @pl.when(first)
    def _():
        acc_ref[...] = parts

    @pl.when(jnp.logical_not(first))
    def _():
        acc_ref[...] += parts


ORDER = (1, 3, 0, 2)


def step_rows():
    return pl.ds(pl.multiple_of(pl.program_id(0) * WINDOW, WINDOW), WINDOW)


def put_parts(leaving_ref, staying_ref, buf, sem, gradient_of):
    copies = []
    for n, k in enumerate(ORDER):
        buf[n] = gradient_of(k).astype(bf16)
        target = (leaving_ref if n < 2 else staying_ref).at[n % 2]
        copy = pltpu.make_async_copy(buf.at[n], target, sem.at[n])
        copy.start()
        copies.append(copy)
    for copy in copies:
        copy.wait()


def parts_outs(width):
    return [((2, width, width), bf16, pl.BlockSpec(memory_space=pl.ANY))] * 2


def parts_scratch(width):
    return [pltpu.VMEM((4, width, width), bf16), pltpu.SemaphoreType.DMA((4,))]


def last_step():
    return pl.program_id(0) == pl.num_programs(0) - 1


def norm_back(stream, gain, grad):
    normal, scale = statistics(stream)
    scaled = grad * gain
    mean_plain = jnp.mean(scaled, axis=-1, keepdims=True)
    mean_normal = jnp.mean(scaled * normal, axis=-1, keepdims=True)
    inner = scale * (scaled - mean_plain - normal * mean_normal)
    return inner, grad * normal


def gelu_both(hidden):
    root = 0.7978845608028654
    cubic = 0.044715
    square = hidden * hidden
    bend = jnp.tanh(hidden * (root + root * cubic * square))
    rise = 0.5 + 0.5 * bend
    active = hidden * rise
    slope = rise + (active - active * rise) * (2.0 * root + 6.0 * root * cubic * square)
    return active.astype(bf16), slope.astype(bf16)


def allowed_of(place_ref):
    head_index = place_ref[0]
    frame_count = place_ref[1]

    def valid(axis):
        position = lax.broadcasted_iota(jnp.int32, (WINDOW, WINDOW), axis)
        frame = 4 * ((position >> 6) ^ head_index) + ((position >> 4) & 3)
        return frame < frame_count

    return jnp.logical_or(valid(0), jnp.logical_not(valid(1)))


def shuffle_of(place_ref, axis):
    arranged = lax.broadcasted_iota(jnp.int32, (WINDOW, WINDOW), axis)
    plain = lax.broadcasted_iota(jnp.int32, (WINDOW, WINDOW), 1 - axis)
    band = (arranged >> 6) ^ place_ref[0]
    source = band * BAND + ((arranged >> 2) & 3) * 16 + ((arranged >> 4) & 3) * 4 + (arranged & 3)
    return (source == plain).astype(f32).astype(bf16)


def small_rows(ref, start):
    rows = ref[...].astype(f32)
    terms = [rows[SMALLS * n + start : SMALLS * n + start + 1, :] for n in range(3)]
    return terms[0] + terms[1] + terms[2]


def small_of(a):
    rows, width = a.shape
    return pl.BlockSpec((CELL, width), lambda i, s: (rows // CELL - 1, 0))


def assemble_qkv(packs, scratch):
    width = scratch.shape[1]
    share = width // 4
    for k in range(4):
        for j in range(3):
            start = j * width + k * share
            scratch[start : start + share, :] = packs[k][j * share : (j + 1) * share, :]


def assemble_out(packs, scratch):
    share = scratch.shape[0] // 4
    for k in range(4):
        scratch[k * share : (k + 1) * share, :] = packs[k][3 * share : 4 * share, :]


def stack_heads(pair):
    low = lax.broadcasted_iota(jnp.int32, pair.shape, 1) < HD
    zero = jnp.zeros((), bf16)
    return jnp.concatenate([jnp.where(low, pair, zero), jnp.where(low, zero, pair)], axis=0)


def attend_core(qkv, allowed, att_ref, lse_ref, part_ref):
    width = att_ref.shape[1]
    pairs = width // PAIR

    def part(j, pair):
        return qkv[:, j * width + pair * PAIR : j * width + (pair + 1) * PAIR]

    def scores_of(pair):
        query = part(0, pair) * jnp.asarray(HD ** (-0.5), bf16)
        return dot_nt(stack_heads(part(1, pair)), query)

    ahead = scores_of(0)
    for pair in range(pairs):
        scores = ahead
        if pair + 1 < pairs:
            ahead = scores_of(pair + 1)
        probs = []
        for half in range(2):
            mine = scores[half * WINDOW : (half + 1) * WINDOW]
            if allowed is not None:
                mine = jnp.where(allowed, mine, masked_score)
            top = jnp.max(mine, axis=0, keepdims=True)
            terms = jnp.exp(mine - top)
            total = jnp.sum(terms, axis=0, keepdims=True)
            probs.append((terms * (1.0 / total)).astype(bf16))
            head = 2 * pair + half
            lse_ref[head : head + 1, :] = top + jnp.log(total)
        out = dot_tn(jnp.concatenate(probs, axis=0), stack_heads(part(2, pair)))
        att_ref[:, pair * PAIR : (pair + 1) * PAIR] = out.astype(bf16)
    share = width // 4
    for k in range(4):
        part_ref[k] = att_ref[:, k * share : (k + 1) * share]


def attend_kernel(layer, place_ref, *refs):
    if layer == 0:
        tokens_ref, marks_ref, *refs = refs
        shuffle = shuffle_of(place_ref, 0)
        stream = dot(shuffle, tokens_ref[...])
    else:
        pieces, refs = refs[:4], refs[4:]
        stream = jnp.concatenate(
            [p[...].reshape(BAND, p.shape[-1]) for p in pieces], axis=0
        ).astype(f32)
    gain_ref, shift_ref, s0, s1, s2, s3, p0, p1, p2, p3, x_ref, normed_ref, qkv_ref, att_ref, lse_ref, part_ref, *refs = refs
    *mark_refs, scratch = refs
    share = scratch.shape[1] // 4

    @pl.when(pl.program_id(0) == 0)
    def _():
        assemble_qkv((p0, p1, p2, p3), scratch)

    if layer == 0:
        given = marks_ref[pl.ds(pl.program_id(0), 1), :]
        high = given >> 4
        both = [jnp.broadcast_to(v, (8, WINDOW)) for v in (high, given - 16 * high)]
        both = jnp.concatenate(both, axis=0).astype(f32).astype(bf16)
        both = dot(both, shuffle_of(place_ref, 1))
        marks = 16.0 * both[0:1] + both[8:9]
        for k in range(4):
            mark_refs[k][pl.ds(pl.program_id(0), 1), :] = marks[:, k * BAND : (k + 1) * BAND]
    x_ref[...] = stream.astype(bf16)
    normal, _ = statistics(stream)
    normed = (normal * gain_ref[layer, 0:1] + shift_ref[layer, 0:1]).astype(bf16)
    normed_ref[...] = normed
    start = 2 * layer * share
    smalls = [small_rows(r, 2) for r in (s0, s1, s2, s3)]
    bias = jnp.concatenate(
        [r[:, start : start + share] for r in smalls]
        + [jnp.zeros((1, 4 * share), f32)]
        + [r[:, start + share : start + 2 * share] for r in smalls],
        axis=1,
    )
    qkv = (dot_nt(normed, scratch[...]) + bias).astype(bf16)
    qkv_ref[...] = qkv
    allowed = allowed_of(place_ref) if layer == 1 else None
    attend_core(qkv, allowed, att_ref, lse_ref, part_ref)


def whole(array):
    zeros = (0,) * array.ndim
    return pl.BlockSpec(array.shape, lambda i, s: zeros, pipeline_mode=pl.Buffered(1))


def rows_of(columns, rows=WINDOW):
    return pl.BlockSpec((rows, columns), lambda i, s: (i, 0))


def parts_of(columns):
    return pl.BlockSpec((4, WINDOW, columns), lambda i, s: (0, i, 0))


def tube_of(columns):
    return pl.BlockSpec((4, 1, CELL, columns), lambda i, s: (0, i, 0, 0))


def sums_of(columns):
    return pl.BlockSpec((8, columns), lambda i, s: (0, 0))


def call(kernel, name, place, steps, operands, outs, scratch=(), aliases={}):
    return pl.pallas_call(
        kernel,
        grid_spec=pltpu.PrefetchScalarGridSpec(
            num_scalar_prefetch=1,
            grid=(steps,),
            in_specs=[spec for _, spec in operands],
            out_specs=[spec for _, _, spec in outs],
            scratch_shapes=list(scratch),
        ),
        out_shape=[jax.ShapeDtypeStruct(shape, dtype) for shape, dtype, _ in outs],
        compiler_params=pltpu.CompilerParams(vmem_limit_bytes=LIMITS.get(name, VMEM_LIMIT)),
        cost_estimate=cost_of(name),
        input_output_aliases=aliases,
        name=name,
    )(place, *[array for array, _ in operands])


def attend(layer, place, inputs, gain, shift, smalls, packs):
    width = gain.shape[-1]
    rows = 4 * WINDOW
    if layer == 0:
        tokens, marks = inputs
        first = [(tokens, rows_of(width)), (marks, whole(marks))]
    else:
        first = [(p, tube_of(width)) for p in inputs]
    operands = first + [(a, whole(a)) for a in (gain, shift)]
    operands += [(a, small_of(a)) for a in smalls] + [(a, whole(a)) for a in packs]
    outs = [
        ((rows, width), bf16, rows_of(width)),
        ((rows, width), bf16, rows_of(width)),
        ((rows, 3 * width), bf16, rows_of(3 * width)),
        ((rows, width), bf16, rows_of(width)),
        ((4 * LSE_ROWS, WINDOW), f32, rows_of(WINDOW, LSE_ROWS)),
        ((4, rows, width // 4), bf16, parts_of(width // 4)),
    ]
    if layer == 0:
        outs += [((4, BAND), f32, pl.BlockSpec((4, BAND), lambda i, s: (0, 0)))] * 4
    return call(
        partial(attend_kernel, layer), "attend", place, 4, operands, outs,
        [pltpu.VMEM((3 * width, width), bf16)],
    )


def attend_back_core(qkv, grad, lse_ref, allowed):
    width = grad.shape[1]
    pairs = width // PAIR

    def part(j, pair):
        return qkv[:, j * width + pair * PAIR : j * width + (pair + 1) * PAIR]

    def first_of(pair):
        query = part(0, pair) * jnp.asarray(HD ** (-0.5), bf16)
        grad_part = grad[:, pair * PAIR : (pair + 1) * PAIR]
        keys = stack_heads(part(1, pair))
        scores = dot_nt(keys, query)
        grad_probs = dot_nt(stack_heads(part(2, pair)), grad_part)
        return query, grad_part, keys, scores, grad_probs

    low = lax.broadcasted_iota(jnp.int32, (WINDOW, PAIR), 1) < HD
    results = [[], [], []]
    ahead = first_of(0)
    for pair in range(pairs):
        query, grad_part, keys, scores, grad_probs = ahead
        if pair + 1 < pairs:
            ahead = first_of(pair + 1)
        all_probs, all_scores = [], []
        for half in range(2):
            rows = slice(half * WINDOW, (half + 1) * WINDOW)
            mine = scores[rows]
            if allowed is not None:
                mine = jnp.where(allowed, mine, masked_score)
            head = 2 * pair + half
            probs = jnp.exp(mine - lse_ref[head : head + 1, :])
            grad_mine = grad_probs[rows]
            delta = jnp.sum(probs * grad_mine, axis=0, keepdims=True)
            all_probs.append(probs.astype(bf16))
            all_scores.append((probs * (grad_mine - delta)).astype(bf16))
        probs = jnp.concatenate(all_probs, axis=0)
        grad_scores = jnp.concatenate(all_scores, axis=0)
        grad_query = dot_tn(grad_scores, keys) * HD ** (-0.5)
        grad_key = dot(grad_scores, query)
        grad_value = dot(probs, grad_part)
        results[0].append(grad_query.astype(bf16))
        results[1].append(jnp.where(low, grad_key[:WINDOW], grad_key[WINDOW:]).astype(bf16))
        results[2].append(jnp.where(low, grad_value[:WINDOW], grad_value[WINDOW:]).astype(bf16))
    return [jnp.concatenate(part, axis=1) for part in results]


def attend_back_kernel(layer, place_ref, *refs):
    (stream_ref, g1_ref, x_ref, qkv_ref, lse_ref, gain_ref, p0, p1, p2, p3, *outs) = refs
    if layer == 1:
        side_ref, *outs = outs
        pieces, outs = outs[:4], outs[4:]
        sums_ref, scratch, out_scratch, acc = outs
        rows = slice(None)
    else:
        (
            normed_ref, part_ref, final_ref, sums_ref, leaving_ref, staying_ref,
            scratch, out_scratch, acc, side_ref, all_normed, all_parts, all_g1, buf, sem,
        ) = outs
        rows = step_rows()
        all_normed[rows, :] = normed_ref[...]
        all_g1[rows, :] = g1_ref[...]
        for k in range(4):
            all_parts[k, rows, :] = part_ref[k]
    width = stream_ref.shape[1]
    share = width // 4

    @pl.when(pl.program_id(0) == 0)
    def _():
        assemble_qkv((p0, p1, p2, p3), scratch)
        assemble_out((p0, p1, p2, p3), out_scratch)

    grad_att = dot_nt(g1_ref[...], out_scratch[...]).astype(bf16)
    allowed = allowed_of(place_ref) if layer == 1 else None
    parts = attend_back_core(qkv_ref[...], grad_att, lse_ref, allowed)
    for k in range(4):
        for j in range(3):
            side_ref[k, rows, j * share : (j + 1) * share] = parts[j][:, k * share : (k + 1) * share]
    joined = jnp.concatenate(parts, axis=1)
    grad_normed = dot(joined, scratch[...])
    inner, scaled = norm_back(x_ref[...].astype(f32), gain_ref[layer, 0:1], grad_normed)
    gather_sums(acc, [parts[0].astype(f32), parts[2].astype(f32), scaled, grad_normed])
    stream = stream_ref[...] + inner
    if layer == 1:
        for k in range(4):
            pieces[k][...] = (
                stream[k * BAND : (k + 1) * BAND].astype(bf16).reshape(4, 1, CELL, width)
            )
    else:
        shuffle = shuffle_of(place_ref, 1)
        high = stream.astype(bf16)
        low = (stream - high.astype(f32)).astype(bf16)
        final_ref[...] = dot(shuffle, high) + dot(shuffle, low)

    @pl.when(last_step())
    def _():
        total = jnp.sum(acc[...], axis=0, keepdims=True)
        sums_ref[...] = jnp.zeros(sums_ref.shape, f32)
        for k in range(4):
            query = total[:, k * share : (k + 1) * share]
            value = total[:, width + k * share : width + (k + 1) * share]
            sums_ref[pl.ds(place_ref[0] ^ k, 1), : 2 * share] = jnp.concatenate([query, value], axis=1)
        sums_ref[4:5, :] = total[:, 2 * width : 3 * width]
        sums_ref[5:6, :] = total[:, 3 * width :]
        if layer == 0:

            def gradient_of(k):
                upper = dot_tn(side_ref[k], all_normed[...])
                lower = dot_tn(all_parts[k], all_g1[...])
                return jnp.concatenate([upper, lower], axis=0)

            put_parts(leaving_ref, staying_ref, buf, sem, gradient_of)


def attend_back(layer, place, stream, g1, x, qkv, lse, gain, packs, normed, attended):
    rows, width = stream.shape
    share = width // 4
    operands = [
        (stream, rows_of(width)),
        (g1, rows_of(width)),
        (x, rows_of(width)),
        (qkv, rows_of(3 * width)),
        (lse, rows_of(WINDOW, LSE_ROWS)),
    ] + [(a, whole(a)) for a in (gain, *packs)]
    sums = [((8, width), f32, sums_of(width))]
    scratch = [
        pltpu.VMEM((3 * width, width), bf16), pltpu.VMEM((width, width), bf16), pltpu.VMEM((8, 4 * width), f32)
    ]
    if layer == 1:
        outs = [((4, rows, 3 * share), bf16, parts_of(3 * share))]
        outs = outs + [((4, 4, CELL, width), bf16, tube_of(width))] * 4 + sums
    else:
        operands += [(normed, rows_of(width)), (attended, parts_of(share))]
        outs = [((rows, width), f32, rows_of(width))] + sums + parts_outs(width)
        scratch += [
            pltpu.VMEM((4, rows, 3 * share), bf16), pltpu.VMEM((rows, width), bf16),
            pltpu.VMEM((4, rows, share), bf16), pltpu.VMEM((rows, width), bf16),
        ] + parts_scratch(width)
    return call(partial(attend_back_kernel, layer), "attend_back", place, 4, operands, outs, scratch)


def feed_kernel(layer, place_ref, *refs):
    (
        x_ref, att_ref, a0, a1, a2, a3, vec_ref, gain_ref, shift_ref, s0, s1, s2, s3,
        u0, u1, u2, u3, d0, d1, d2, d3, stream_ref, normed_ref, active_ref, slope_ref, *outs
    ) = refs
    ups, downs = (u0, u1, u2, u3), (d0, d1, d2, d3)
    *pieces, scratch = outs
    width = x_ref.shape[1]

    @pl.when(pl.program_id(0) == 0)
    def _():
        share = width // 4
        for k, part in enumerate((a0, a1, a2, a3)):
            scratch[k * share : (k + 1) * share, :] = part[...]

    stream = x_ref[...].astype(f32) + dot(att_ref[...], scratch[...]) + vec_ref[layer, 0:1]
    stream_ref[...] = stream
    normal, _ = statistics(stream)
    normed = (normal * gain_ref[layer, 1:2] + shift_ref[layer, 1:2]).astype(bf16)
    normed_ref[...] = normed
    total = stream + vec_ref[layer, 1:2]
    units = u0.shape[1]
    ahead = dot(normed, ups[0][...])
    for k in range(4):
        hidden = ahead
        if k < 3:
            ahead = dot(normed, ups[k + 1][...])
        cut = slice(k * units, (k + 1) * units)
        active, slope = gelu_both(hidden + small_rows((s0, s1, s2, s3)[k], layer))
        active_ref[:, cut] = active
        slope_ref[:, cut] = slope
        total = total + dot(active, downs[k][...])
    total = total.astype(bf16)
    if layer == 0:
        for k in range(4):
            pieces[k][...] = total[k * BAND : (k + 1) * BAND].reshape(1, BAND, width)
    else:
        pieces[0][...] = total


def feed_specs(layer, packs):
    ups, downs, ups_across, downs_across = packs

    def of_layer(a):
        return (a, pl.BlockSpec(
            (None, *a.shape[1:]), lambda i, s: (layer, 0, 0), pipeline_mode=pl.Buffered(1)
        ))

    return [
        *[of_layer(a) for a in ups],
        *[(a, whole(a)) for a in ups_across],
        *[of_layer(a) for a in downs],
        *[(a, whole(a)) for a in downs_across],
    ]


def feed(layer, place, x, att, attn_packs, vecs, gain, shift, smalls, packs):
    rows, width = x.shape
    units = packs[0][0].shape[2]
    last = pl.BlockSpec((width // 4, width), lambda i, s: (3, 0))
    operands = (
        [(x, rows_of(width)), (att, rows_of(width))]
        + [(a, last) for a in attn_packs]
        + [(a, whole(a)) for a in (vecs, gain, shift)]
        + [(a, small_of(a)) for a in smalls]
        + feed_specs(layer, packs)
    )
    outs = [
        ((rows, width), f32, rows_of(width)),
        ((rows, width), bf16, rows_of(width)),
        ((rows, 4 * units), bf16, rows_of(4 * units)),
        ((rows, 4 * units), bf16, rows_of(4 * units)),
    ]
    if layer == 0:
        piece = pl.BlockSpec((1, BAND, width), lambda i, s: (i, 0, 0))
        outs = outs + [((4, BAND, width), bf16, piece)] * 4
    else:
        outs = outs + [((rows, width), bf16, rows_of(width))]
    return call(
        partial(feed_kernel, layer), "feed", place, 4, operands, outs,
        [pltpu.VMEM((width, width), bf16)],
    )


def loss_kernel(
    place_ref, final_ref, head_ref, m0, m1, m2, m3, active_ref, grad_ref, loss_ref, leaving_ref, staying_ref,
    acc, all_active, all_g2, buf, sem,
):
    logits = dot(final_ref[...], head_ref[...])
    spread = jnp.concatenate(
        [jnp.broadcast_to(m[f : f + 1, :], (CELL, BAND)) for m in (m0, m1, m2, m3) for f in range(4)],
        axis=0,
    )
    position = lax.broadcasted_iota(jnp.int32, (WINDOW, BAND), 0)
    lane = lax.broadcasted_iota(jnp.int32, (WINDOW, BAND), 1)
    mine = lane == pl.program_id(0) * CELL + (position & (CELL - 1))
    mark = jnp.sum(jnp.where(mine, spread, 0.0), axis=1, keepdims=True).astype(jnp.int32)
    place_of = lax.broadcasted_iota(jnp.int32, (WINDOW, 1), 0)
    frame = 4 * ((place_of >> 6) ^ place_ref[0]) + ((place_of >> 4) & 3)
    weight = jnp.where(frame < place_ref[1], (mark & 1).astype(f32), 0.0)
    top = jnp.max(logits, axis=1, keepdims=True)
    terms = jnp.exp(logits - top)
    total = jnp.sum(terms, axis=1, keepdims=True)
    code = lax.broadcasted_iota(jnp.int32, logits.shape, 1)
    chosen = code == (mark >> 1)
    picked = jnp.sum(jnp.where(chosen, logits, 0.0), axis=1, keepdims=True)
    entry = weight * (top + jnp.log(total) - picked)
    soft = terms * (1.0 / total)
    grad_logits = (weight * (soft - jnp.where(chosen, 1.0, 0.0))).astype(bf16)
    grad = dot_nt(grad_logits, head_ref[...])
    grad_ref[...] = grad
    all_g2[step_rows(), :] = grad.astype(bf16)
    all_active[step_rows(), :] = active_ref[...]
    gather_sums(acc, [jnp.broadcast_to(entry, (WINDOW, PAIR))])

    @pl.when(last_step())
    def _():
        total = jnp.sum(acc[...], axis=0, keepdims=True)
        loss_ref[...] = jnp.broadcast_to(total[:, :1], loss_ref.shape)
        width = grad_ref.shape[1]
        put_parts(
            leaving_ref, staying_ref, buf, sem,
            lambda k: dot_tn(all_active[:, k * width : (k + 1) * width], all_g2[...]),
        )


def code_loss(place, final, code_head, marks, active):
    rows, width = final.shape
    operands = [(final, rows_of(width))] + [(a, whole(a)) for a in (code_head, *marks)]
    operands += [(active, rows_of(active.shape[1]))]
    outs = [
        ((rows, width), f32, rows_of(width)),
        ((8, width), f32, sums_of(width)),
    ] + parts_outs(width)
    scratch = [
        pltpu.VMEM((8, PAIR), f32), pltpu.VMEM(active.shape, bf16), pltpu.VMEM((rows, width), bf16)
    ] + parts_scratch(width)
    return call(loss_kernel, "code_loss", place, 4, operands, outs, scratch)


def feed_back_kernel(layer, place_ref, *refs):
    if layer == 1:
        grad_ref, *refs = refs
        grad = grad_ref[...]
    else:
        grad_ref, *refs = refs
        grad = grad_ref[...].astype(f32)
    (
        slope_ref, stream_ref, normed_ref, gain_ref, u0, u1, u2, u3, d0, d1, d2, d3, next_ref, g1_ref,
        sums_ref, leaving_ref, staying_ref, acc, all_hidden, all_normed, buf, sem,
    ) = refs
    all_normed[step_rows(), :] = normed_ref[...]
    g2 = grad.astype(bf16)
    units = u0.shape[1]
    grad_normed = jnp.zeros(grad.shape, f32)
    sums = []
    ups, downs = (u0, u1, u2, u3), (d0, d1, d2, d3)
    ahead = dot_nt(g2, downs[0][...])
    for k in range(4):
        grad_active = ahead
        if k < 3:
            ahead = dot_nt(g2, downs[k + 1][...])
        cut = slice(k * units, (k + 1) * units)
        grad_hidden = (grad_active * slope_ref[:, cut].astype(f32)).astype(bf16)
        all_hidden[step_rows(), cut] = grad_hidden
        sums.append(grad_hidden.astype(f32))
        grad_normed = grad_normed + dot_nt(grad_hidden, ups[k][...])
    inner, scaled = norm_back(stream_ref[...], gain_ref[layer, 1:2], grad_normed)
    grad = grad + inner
    next_ref[...] = grad
    g1 = grad.astype(bf16)
    g1_ref[...] = g1
    gather_sums(acc, sums + [scaled, grad_normed, g2.astype(f32), g1.astype(f32)])

    @pl.when(last_step())
    def _():
        total = jnp.sum(acc[...], axis=0, keepdims=True)
        for k in range(4):
            sums_ref[pl.ds(place_ref[0] ^ k, 1), :] = total[:, k * units : (k + 1) * units]
            start = 4 * units + k * grad.shape[1]
            sums_ref[4 + k : 5 + k, :] = total[:, start : start + grad.shape[1]]
        put_parts(
            leaving_ref, staying_ref, buf, sem,
            lambda k: dot_tn(all_normed[...], all_hidden[:, k * units : (k + 1) * units]),
        )


def feed_back(layer, place, grad, slope, stream, normed, gain, packs):
    rows, width = stream.shape
    units = packs[0][0].shape[2]
    operands = (
        [(grad, rows_of(width)), (slope, rows_of(4 * units)), (stream, rows_of(width)), (normed, rows_of(width))]
        + [(gain, whole(gain))]
        + feed_specs(layer, packs)
    )
    outs = [
        ((rows, width), f32, rows_of(width)),
        ((rows, width), bf16, rows_of(width)),
        ((8, width), f32, sums_of(width)),
    ] + parts_outs(width)
    scratch = [
        pltpu.VMEM((8, 4 * units + 4 * width), f32),
        pltpu.VMEM((rows, 4 * units), bf16),
        pltpu.VMEM((rows, width), bf16),
    ] + parts_scratch(width)
    return call(partial(feed_back_kernel, layer), "feed_back", place, 4, operands, outs, scratch)


def grad_kernel(kind, place_ref, *refs):
    *inputs, leaving_ref, staying_ref = refs
    if kind == "attn":
        side_ref, normed_ref, part_ref, g1_ref = inputs
        upper = dot_tn(side_ref[...], normed_ref[...])
        lower = dot_tn(part_ref[...], g1_ref[...])
        value = jnp.concatenate([upper, lower], axis=0)
    else:
        left_ref, right_ref = inputs
        value = dot_tn(left_ref[...], right_ref[...])
    value = value.astype(bf16)
    step = pl.program_id(0)

    @pl.when(step < 2)
    def _():
        leaving_ref[...] = value

    @pl.when(step >= 2)
    def _():
        staying_ref[...] = value


def grads(kind, place, arrays, width):
    rows = arrays[1].shape[0]

    def part_at(i):
        return jnp.where(i < 2, 2 * i + 1, 2 * i - 4)

    part = pl.BlockSpec((rows, width), lambda i, s: (0, part_at(i)))

    def of_part(a):
        return pl.BlockSpec((None, *a.shape[1:]), lambda i, s: (part_at(i), 0, 0))

    if kind == "attn":
        side, normed, attended, g1 = arrays
        specs = [of_part(side), whole(normed), of_part(attended), whole(g1)]
    elif kind == "up":
        specs = [whole(arrays[0]), part]
    else:
        specs = [part, whole(arrays[1])]
    block = (None, width, width)
    outs = [
        ((2, width, width), bf16, pl.BlockSpec(block, lambda i, s: (jnp.minimum(i, 1), 0, 0))),
        ((2, width, width), bf16, pl.BlockSpec(block, lambda i, s: (jnp.maximum(i - 2, 0), 0, 0))),
    ]
    return call(
        partial(grad_kernel, kind), "grads_" + kind, place, 4, list(zip(arrays, specs)), outs
    )


def emit_kernel(attention, aliased, place_ref, mine_ref, other_ref, *refs):
    outs = refs[aliased:]
    half, width = mine_ref.shape
    upper = place_ref[2] == 1
    mine, other = mine_ref[...].astype(f32), other_ref[...].astype(f32)
    low, high = jnp.where(upper, other, mine), jnp.where(upper, mine, other)
    if attention:
        qkv_ref, out_ref = outs
        share = width // 4
        qkv_ref[0, 0], qkv_ref[0, 1] = low[:share], low[share:]
        qkv_ref[0, 2], out_ref[0] = high[:share], high[share:]
    else:
        outs[0][0, :half] = low
        outs[0][0, half:] = high


def emit(place, layer, attention, summed, earlier):
    width = summed[0].shape[1]
    share = width // 4
    if attention:
        outs = [
            ((2, 3, share, width), f32, pl.BlockSpec((1, 3, share, width), lambda i, s: (layer, 0, 0, 0))),
            ((2, share, width), f32, pl.BlockSpec((1, share, width), lambda i, s: (layer, 0, 0))),
        ]
    else:
        outs = [((2, width, width), f32, pl.BlockSpec((1, width, width), lambda i, s: (layer, 0, 0)))]
    operands = [(a, whole(a)) for a in summed]
    aliases = {}
    if earlier is not None:
        aliases = {3 + n: n for n in range(len(earlier))}
        operands += [(e, pl.BlockSpec(memory_space=pl.ANY)) for e in earlier]
    return call(
        partial(emit_kernel, attention, len(aliases)), "emit", place, 1, operands, outs, aliases=aliases
    )


def head_swap(values, distance):
    count = lax.axis_size("head")
    return lax.ppermute(values, "head", [(i, i ^ distance) for i in range(count)])


def clip_swap(values, distance):
    count = lax.axis_size("clip")
    return lax.ppermute(values, "clip", [(i, i ^ distance) for i in range(count)])


class Order:
    def __init__(self):
        self.last = ()
        self.pending = []

    def run(self, step, *values):
        values, _ = lax.optimization_barrier((values, self.last))
        out = step(*values)
        self.last = (jax.tree.leaves(out)[0],)
        return out

    def send(self, swap, values, distance):
        values, _ = lax.optimization_barrier((values, self.last))
        out = swap(values, distance)
        self.pending.append(out)
        return out

    def close(self):
        self.last = self.last + tuple(self.pending)
        self.pending = []


def split_halves(total, upper):
    half = total.shape[-2] // 2
    low, high = total[..., :half, :], total[..., half:, :]
    return jnp.where(upper, low, high).astype(bf16), jnp.where(upper, high, low).astype(bf16)


def join_halves(mine, other, upper):
    return jnp.concatenate(
        [jnp.where(upper, other, mine), jnp.where(upper, mine, other)], axis=0
    )


class Pack:
    def __init__(self, order, leaving, staying, halving=True, late=False):
        self.order = order
        self.late = late
        self.out, self.kept = leaving, staying
        levels = lax.axis_size("clip").bit_length() - 1
        clip = lax.axis_index("clip")
        self.uppers = [((clip >> n) & 1) == 1 for n in range(levels)]
        depth = levels - 1 if halving else 1
        down = [("halve", n) for n in range(depth)]
        level = [("all", n) for n in range(depth, levels)]
        up = [("join", n) for n in reversed(range(depth))]
        if late:
            self.stages = ["core"] + down + ["across"] + level + up
        else:
            self.stages = ["core", "across"] + down + level + up
        self.at = 0
        self.prepared = False

    def prepare(self):
        if self.prepared:
            return
        self.prepared = True
        stage = self.stages[self.at]
        run = self.order.run
        if stage == "core":
            self.leaving = self.out
        elif self.late and stage == "across":

            def parted(total, moved):
                total = total.astype(f32) + moved.astype(f32)
                return total[1].astype(bf16), total[0].astype(bf16)

            self.leaving, self.sum = run(parted, self.sum, self.moved)
        elif self.late and self.at == 1:
            upper = self.uppers[stage[1]]

            def halved(kept, near):
                return split_halves(kept.astype(f32) + near.astype(f32), upper)

            self.leaving, self.sum = run(halved, self.kept, self.near)
        elif stage == "across":
            self.leaving = run(
                lambda kept, near: (kept[1].astype(f32) + near[1].astype(f32)).astype(bf16),
                self.kept, self.near,
            )
        else:
            kind, level = stage
            upper = self.uppers[level]
            if self.at == 2 and not self.late:
                start = lambda kept, near, moved: (
                    kept[0].astype(f32) + near[0].astype(f32) + moved.astype(f32)
                )
                values = (self.kept, self.near, self.moved)
            else:
                start = lambda total, moved: total.astype(f32) + moved.astype(f32)
                values = (self.sum, self.moved)
            if kind == "halve":
                self.leaving, self.sum = run(lambda *v: split_halves(start(*v), upper), *values)
            elif kind == "all" or self.stages[self.at - 1][0] == "all":
                self.leaving = self.sum = run(lambda *v: start(*v).astype(bf16), *values)
            else:
                before = self.uppers[self.stages[self.at - 1][1]]
                self.leaving = self.sum = run(
                    lambda mine, other: join_halves(mine, other, before), self.sum, self.moved
                )

    def launch(self):
        stage = self.stages[self.at]
        send = self.order.send
        if stage == "core":
            self.near = send(head_swap, self.leaving, 1)
        elif stage == "across":
            self.moved = send(head_swap, self.leaving, 2)
        else:
            self.moved = send(clip_swap, self.leaving, 1 << stage[1])
        self.at += 1
        self.prepared = False

    def done(self):
        return self.at == len(self.stages)

    def whole(self):
        assert self.done()
        return self.sum, self.moved


def on_device(
    tokens,
    frame_counts,
    token_mask,
    targets,
    norm_gain,
    norm_bias,
    w_qkv,
    qv_bias,
    w_out,
    vec_bias,
    w_up,
    up_bias,
    w_down,
    code_head,
):
    head_index = lax.axis_index("head")
    width = tokens.shape[1]
    share = w_out.shape[1]
    upper = lax.axis_index("clip") & 1
    place = jnp.stack(
        [head_index.astype(jnp.int32), frame_counts[0], upper.astype(jnp.int32)]
    )
    order = Order()

    def tied(values, *after):
        return lax.optimization_barrier((values, after))[0]

    clip_count = lax.axis_size("clip")
    own_small = jnp.concatenate([up_bias, qv_bias.reshape(1, width)], axis=0)
    clip_index = lax.axis_index("clip")

    def chunk(matrix):
        piece = matrix.shape[0] // clip_count
        return lax.dynamic_slice_in_dim(matrix, clip_index * piece, piece, 0)

    def over_clips(chunk_across):
        return lax.all_gather(chunk_across, "clip", axis=0, tiled=True)

    y_place, z_place = clip_index & 1, (clip_index >> 1) & 1

    def quarter(matrix):
        rows = matrix.shape[0] // 4
        return lax.dynamic_slice_in_dim(matrix, (2 * y_place + z_place) * rows, rows, 0)

    def along_y(first):
        return jnp.concatenate([first, clip_swap(first, 1)], axis=0)

    def by_place(pair, others):
        rows = pair.shape[0] // 2
        pieces = []
        for y in range(2):
            for z in range(2):
                same = z_place == z
                mine = jnp.where(same, pair[:rows], others[:rows])
                next_one = jnp.where(same, pair[rows:], others[rows:])
                pieces.append(jnp.where(y_place == y, mine, next_one))
        return jnp.concatenate(pieces, axis=0)

    def attn_pack(layer):
        transposed = w_qkv[layer].swapaxes(1, 2).reshape(-1, width)
        return jnp.concatenate([transposed, w_out[layer]], axis=0)

    def spread(own, across):
        return [own, head_swap(own, 1), across, head_swap(across, 1)]

    up_quarter = head_swap(quarter(w_up[0]), 2)
    down_quarter = head_swap(quarter(w_down[0]), 2)
    terms, left = [], own_small
    for _ in range(3):
        term = lax.reduce_precision(left, 8, 7)
        terms.append(term.astype(bf16))
        left = left - term
    fill = jnp.zeros((CELL - 3 * SMALLS, width), bf16)
    own = jnp.concatenate([attn_pack(0), *terms, fill], axis=0)
    up_quarter, down_quarter, own = lax.optimization_barrier((up_quarter, down_quarter, own))
    later = jnp.concatenate([chunk(w_up[1]), chunk(w_down[1])], axis=0)
    marks = (2 * targets + token_mask).reshape(4, WINDOW)
    up_pair, down_pair = along_y(up_quarter), along_y(down_quarter)
    up_x = by_place(up_pair, clip_swap(up_pair, 2))
    across, later, marks, place, up_x, down_pair = lax.optimization_barrier(
        (head_swap(own, 2), later, marks, place, up_x, down_pair)
    )
    attn = [spread(own, across), None]
    order.last = (across,)
    down_others = order.send(clip_swap, down_pair, 2)
    chunk_1 = order.send(head_swap, later, 2)
    smalls = attn[0]
    order.last = (attn[0][1], attn[0][3])
    ups = [w_up, order.send(head_swap, w_up, 1)]
    downs = [w_down, order.send(head_swap, w_down, 1)]
    up_diagonal = order.send(head_swap, up_x, 1)
    packs = [None, None]

    def feed_packs(up_x, down_x):
        return (
            ups, downs,
            [up_x, order.send(head_swap, up_x, 1)],
            [down_x, order.send(head_swap, down_x, 1)],
        )

    kept = []
    inputs = (tokens, marks)
    for layer in range(2):
        x, normed, qkv, att, lse, att_parts, *mark_pieces = order.run(
            lambda *a: attend(layer, place, a, norm_gain, norm_bias, smalls, attn[layer]), *inputs
        )
        order.close()
        if layer == 0:
            gathered = over_clips(tied(chunk_1, x))
            marks = [mark_pieces[0]] + [head_swap(mark_pieces[k], k) for k in (1, 2, 3)]
            down_x = order.run(by_place, down_pair, down_others)
            packs[0] = (ups, downs, [up_x, up_diagonal], [down_x, order.send(head_swap, down_x, 1)])
            order.close()
            own = attn_pack(1)
            attn_across = order.send(head_swap, own, 2)
            attn[1] = [own, head_swap(own, 1), attn_across]
        stream, normed2, active, slope, *outs = order.run(
            lambda a, b: feed(
                layer, place, a, b, attn[layer], vec_bias, norm_gain, norm_bias, smalls, packs[layer]
            ),
            x, att,
        )
        kept.append((x, normed, qkv, att_parts, lse, stream, normed2, active, slope))
        if layer == 0:
            order.close()
            pieces = gathered.reshape(clip_count, 2, -1, width)
            attn[1].append(order.send(head_swap, attn_across, 1))
            inputs = [outs[0]] + [order.send(head_swap, outs[k], k) for k in (1, 2, 3)]
            inputs = [p.reshape(4, 4, CELL, width) for p in inputs]
            order.close()
            packs[1] = feed_packs(pieces[:, 0].reshape(-1, width), pieces[:, 1].reshape(-1, width))
    grad, loss_sum, *parts = order.run(
        lambda a: code_loss(place, a, code_head, marks, active), outs[0]
    )
    down_1 = Pack(order, *parts, halving=False)

    def run_feed_back(layer, grad):
        x, normed, qkv, att, lse, stream, normed2, active, slope = kept[layer]
        return order.run(
            lambda a: feed_back(layer, place, a, slope, stream, normed2, norm_gain, packs[layer]), grad
        )

    def run_attend_back(layer, grad_next, g1):
        x, normed, qkv, att, lse, *_ = kept[layer]
        return order.run(
            lambda a, b: attend_back(
                layer, place, a, b, x, qkv, lse, norm_gain, attn[layer], normed, att
            ),
            grad_next, g1,
        )

    def pack(kind, *arrays, **options):
        parts = order.run(lambda *a: grads(kind, place, a, width), *arrays)
        return Pack(order, *parts, **options)

    def move(*ones):
        for one in ones:
            one.prepare()
        for one in ones:
            one.launch()

    move(down_1)
    order.close()
    move(down_1)
    grad_next, g1, feed_sum_1, *parts = run_feed_back(1, grad)
    up_1 = Pack(order, *parts, halving=False)
    order.close()
    move(up_1)
    down_1.prepare()
    order.close()
    move(up_1, down_1)
    side, *outs, attn_sum_1 = run_attend_back(1, grad_next, g1)
    order.close()

    grad = [outs[0]] + [order.send(head_swap, outs[k], k) for k in (1, 2, 3)]
    grad = [p.reshape(4, BAND, width) for p in grad]
    move(up_1, down_1)
    attn_1 = pack("attn", side, kept[1][1], kept[1][3], g1, late=True)
    order.close()

    move(attn_1)
    g2 = jnp.stack(grad, axis=1).reshape(-1, width)
    down_0 = pack("down", kept[0][7], g2)
    order.close()
    move(down_0)
    for one in (attn_1, down_1, up_1):
        one.prepare()
    order.close()
    move(down_0, attn_1, down_1, up_1)
    grad_next, g1, feed_sum_0, *parts = run_feed_back(0, g2)
    up_0 = Pack(order, *parts)
    order.close()
    move(up_0)
    for one in (attn_1, up_1, down_1, down_0):
        one.prepare()
    order.close()
    move(up_0, down_0, attn_1, up_1, down_1)
    grad_input, attn_sum_0, *parts = run_attend_back(0, grad_next, g1)
    attn_0 = Pack(order, *parts)
    order.close()
    move(attn_0)
    move(attn_1)
    move(down_0)
    for one in (up_0, up_1):
        one.prepare()
    order.close()
    move(down_0, attn_0, attn_1, up_0, up_1)
    order.close()

    packed = jnp.concatenate([feed_sum_0, feed_sum_1, attn_sum_0, attn_sum_1, loss_sum], axis=0)
    swaps = [(head_swap, 1), (head_swap, 2)]
    swaps += [(clip_swap, 1 << n) for n in range(clip_count.bit_length() - 1)]

    def pack_step():
        swap, distance = swaps.pop(0)
        return packed + order.send(swap, packed, distance)

    ready = {}

    def write(one, layer, attention, earlier):
        ready[one] = order.run(lambda *a: emit(place, layer, attention, a, earlier), *one.whole())

    late = [down_1, up_1]
    moving = [attn_0, up_0, down_0]
    everyone = moving + late + [attn_1]
    closed = [one for one in everyone if one.done()]
    jobs = [
        (down_1, 1, False, None), (up_1, 1, False, None), (down_0, 0, False, down_1),
        (attn_1, 1, True, None), (up_0, 0, False, up_1), (attn_0, 0, True, attn_1),
    ]
    wait = 0
    while swaps or not all(one.done() for one in moving + late + [attn_1]):
        held = [down_0] if wait == 0 else []
        move(*[one for one in moving + [attn_1] + late if not one.done() and one not in held])
        wait += 1
        if swaps:
            packed = pack_step()
        for job in jobs:
            one, layer, attention, earlier = job
            if one in closed and (earlier is None or earlier in ready):
                write(one, layer, attention, ready.get(earlier))
                jobs.remove(job)
                break
        order.close()
        closed = [one for one in everyone if one.done()]

    for one, layer, attention, earlier in jobs:
        write(one, layer, attention, ready.get(earlier))

    attn_out, up_out, down_out = ready[attn_0], ready[up_0], ready[down_0]

    feed_sums = packed[:16].reshape(2, 8, width)
    attn_sums = packed[16:32].reshape(2, 8, width)
    loss_total = packed[32, 0]
    own_feed = lax.dynamic_index_in_dim(feed_sums, head_index, 1, keepdims=False)
    own_attn = lax.dynamic_index_in_dim(attn_sums, head_index, 1, keepdims=False)
    slot_total = clip_count * frame_counts.shape[0] * FRAMES * SIDE * SIDE

    return (
        loss_total / slot_total,
        grad_input,
        jnp.stack([attn_sums[:, 4], feed_sums[:, 4]], axis=1),
        jnp.stack([attn_sums[:, 5], feed_sums[:, 5]], axis=1),
        attn_out[0].swapaxes(2, 3),
        own_attn[:, : 2 * share].reshape(2, 2, share),
        attn_out[1],
        jnp.stack([feed_sums[:, 7], feed_sums[:, 6]], axis=1),
        up_out[0],
        own_feed,
        down_out[0],
    )


def solution(mesh):
    placed = (
        P(("clip", "head"), None),
        P("clip"),
        P(("clip", "head")),
        P(("clip", "head")),
        P(),
        P(),
        P(None, None, None, "head"),
        P(None, None, "head"),
        P(None, "head", None),
        P(),
        P(None, None, "head"),
        P(None, "head"),
        P(None, "head", None),
        P(),
    )
    return jax.shard_map(
        on_device,
        mesh=mesh,
        in_specs=placed,
        out_specs=(
            P(),
            P(("clip", "head"), None),
            P(),
            P(),
            P(None, None, None, "head"),
            P(None, None, "head"),
            P(None, "head", None),
            P(),
            P(None, None, "head"),
            P(None, "head"),
            P(None, "head", None),
        ),
        check_vma=False,
    )
```
